32 devices in a mesh: rep: 4 (over z), sec: 2 (over x), mdl: 4 (over y, core).
Axes of the slice: x: 2, y: 2, z: 4, core: 2. Of those that a mesh axis runs over, the one named last changes fastest.
Arguments:
- obs: bfloat16 [2, 2048, 1536], P('sec', 'rep'), may hold values from -6 to 6
- a_query: bfloat16 [1536, 1536], P(None, 'mdl'), may hold values from -0.15309311 to 0.15309311
- a_keyval: bfloat16 [2, 1536, 512], P(None, None, 'mdl'), may hold values from -0.15309311 to 0.15309311
- a_out: bfloat16 [1536, 1536], P('mdl'), may hold values from -0.15625 to 0.15625
- w_policy: bfloat16 [1536, 128], replicated, may hold values from -0.15625 to 0.15625
- c_in: bfloat16 [1536, 2048], P(None, 'mdl'), may hold values from -0.15309311 to 0.15309311
- c_query: bfloat16 [2048, 2048], P(None, 'mdl'), may hold values from -0.13258252 to 0.13258252
- c_keyval: bfloat16 [2, 2048, 512], P(None, None, 'mdl'), may hold values from -0.13258252 to 0.13258252
- c_out: bfloat16 [2048, 2048], P('mdl'), may hold values from -0.125 to 0.125
- w_value: bfloat16 [2048], replicated, may hold values from -0.110485435 to 0.110485435
- actions: int32 [2, 2048], P('sec', 'rep'), may hold values from 0 to 127
- advantages: float32 [2, 2048], P('sec', 'rep'), may hold values from -6 to 6
- old_logp: float32 [2, 2048], P('sec', 'rep'), may hold values from -7 to -4
- returns: float32 [2, 2048], P('sec', 'rep'), may hold values from -6 to 6
- robot_count: int32 [2], replicated, may hold values from 512 to 2048, as said below
Outputs:
- values: float32 [2, 2048], P('sec', ('rep', 'mdl'))
- grad_a_out: float32 [1536, 1536], P('mdl')
- grad_c_out: float32 [2048, 2048], P('mdl')
The draws below stay inside these ranges and needn't reach their ends.
Inputs may be any that keep to these rules, and one draw needn't show every extreme that they name: `robot_count`: one of the two micro-batches holds all 2048 robots, the other at least 512; live robots are the first ones.
All inputs are finite; a program needn't handle non-finite values.
Results may differ from the reference program's by a relative error of at most 0.023.
Values may be sent and summed in bfloat16 or wider, within the bound.
No kernel may reach another device: no remote copies, remote signals or barrier semaphores. Data moves between devices by JAX's collectives and lax.ppermute only.
A program may use at most 128 MiB of HBM per device.

```python
import math
import jax
import jax.numpy as jnp
from jax import lax

DA = 1536
HA = 12
KVA = 4
DC = 2048
HC = 16
KVC = 4
HEAD = 128
ACTIONS = 128
ROBOTS = 2048


def draw_robot_count(key, part):
    partial_value = jax.random.randint(jax.random.fold_in(key, 11), (), ROBOTS // 4, ROBOTS + 1)
    leading = jax.random.randint(jax.random.fold_in(key, 12), (), 0, 2)
    return jnp.where(jnp.arange(2) == leading, ROBOTS, partial_value).astype(jnp.int32)


def drawn_weight(key, tag, shape, fan_in):
    return jnp.clip(jax.random.normal(jax.random.fold_in(key, tag), shape, jnp.float32), -5.0, 5.0) * fan_in ** (-0.5)


def draw_obs(key, part):
    values_out = jnp.clip(jax.random.normal(jax.random.fold_in(key, 21), (2, ROBOTS, DA), jnp.float32), -6.0, 6.0)
    return values_out.astype(jnp.bfloat16)


def draw_a_query(key, part):
    shape = (DA, HA * HEAD)
    values_out = drawn_weight(key, 41, shape, DA)
    return values_out.astype(jnp.bfloat16)


def draw_a_keyval(key, part):
    shape = (2, DA, KVA * HEAD)
    values_out = drawn_weight(key, 42, shape, DA)
    return values_out.astype(jnp.bfloat16)


def draw_c_in(key, part):
    shape = (DA, DC)
    values_out = drawn_weight(key, 43, shape, DA)
    return values_out.astype(jnp.bfloat16)


def draw_c_query(key, part):
    shape = (DC, HC * HEAD)
    values_out = drawn_weight(key, 44, shape, DC)
    return values_out.astype(jnp.bfloat16)


def draw_c_keyval(key, part):
    shape = (2, DC, KVC * HEAD)
    values_out = drawn_weight(key, 45, shape, DC)
    return values_out.astype(jnp.bfloat16)


def draw_w_value(key, part):
    values_out = drawn_weight(key, 46, (DC,), DC)
    return values_out.astype(jnp.bfloat16)


def with_ends(drawn, own_key, low, largest):
    spot = [jax.random.randint(jax.random.fold_in(own_key, axis), (), 0, length) for axis, length in enumerate(drawn.shape)]
    main_axis = drawn.shape.index(max(drawn.shape))
    next_to = spot[:main_axis] + [(spot[main_axis] + 1) % drawn.shape[main_axis]] + spot[main_axis + 1:]
    return drawn.at[tuple(spot)].set(low).at[tuple(next_to)].set(largest)


def levels(stream_key, extent, pieces, low, top_value):
    gain = 1.0
    for dim, shards_of in pieces:
        heights = jax.random.uniform(jax.random.fold_in(jax.random.fold_in(stream_key, 6), dim), (shards_of,), jnp.float32, low / len(pieces), top_value / len(pieces))
        gain = gain * jnp.repeat(jnp.exp(heights), extent[dim] // shards_of).reshape((-1,) + (1,) * (len(extent) - 1 - dim))
    return gain


def centred(own_key, extent, deviation, most, split=(), kind=jnp.bfloat16):
    entries = jax.random.normal(own_key, extent, jnp.float32) * deviation
    if len(split) > 0:
        entries = levels(own_key, extent, split, -0.22, 0.18) * entries
    return jnp.clip(entries, min=-most, max=most).astype(kind)


def setup_inputs(seed: int = 0) -> dict:
    key_list = jax.random.split(jax.random.key(seed), 16)
    return {
        "obs": draw_obs(jax.random.fold_in(key_list[15], 71), 0),
        "a_query": draw_a_query(jax.random.fold_in(key_list[15], 71), 0),
        "a_keyval": draw_a_keyval(jax.random.fold_in(key_list[15], 71), 0),
        "a_out": centred(key_list[3], (HA * HEAD, DA), (HA * HEAD) ** -0.5, 0.15625, ((0, 4),)),
        "w_policy": centred(key_list[4], (DA, ACTIONS), DA ** -0.5, 0.15625),
        "c_in": draw_c_in(jax.random.fold_in(key_list[15], 71), 0),
        "c_query": draw_c_query(jax.random.fold_in(key_list[15], 71), 0),
        "c_keyval": draw_c_keyval(jax.random.fold_in(key_list[15], 71), 0),
        "c_out": centred(key_list[8], (HC * HEAD, DC), (HC * HEAD) ** -0.5, 0.125, ((0, 4),)),
        "w_value": draw_w_value(jax.random.fold_in(key_list[15], 71), 0),
        "actions": with_ends(jax.random.randint(key_list[10], (2, ROBOTS), 0, ACTIONS), jax.random.fold_in(key_list[10], 1), 0, ACTIONS - 1).astype(jnp.int32),
        "advantages": centred(key_list[11], (2, ROBOTS), 1.0, 6.0, ((0, 2), (1, 4)), jnp.float32),
        "old_logp": jnp.clip(-7.0 + 3.0 * jax.random.uniform(key_list[12], (2, ROBOTS), jnp.float32) ** levels(key_list[12], (2, ROBOTS), ((0, 2), (1, 4)), -0.2, 0.2), -7.0, -4.0),
        "returns": centred(key_list[13], (2, ROBOTS), 1.0, 6.0, ((0, 2), (1, 4)), jnp.float32),
        "robot_count": draw_robot_count(jax.random.fold_in(key_list[15], 71), 0),
    }


epsilon = 1e-05
clip_range = 0.2
masked_score = -1e+30

def rms_normed(values_in):
    return values_in * lax.rsqrt(lax.optimization_barrier(jnp.mean(values_in * values_in, axis=-1, keepdims=True)) + epsilon)

def norm_backward(source, normed, grad_in):
    factor = lax.rsqrt(lax.optimization_barrier(jnp.mean(source * source, axis=-1, keepdims=True)) + epsilon)
    return factor * (grad_in - normed * lax.optimization_barrier(jnp.mean(grad_in * normed, axis=-1, keepdims=True)))

def project(source, w_query, w_keyval):
    normed = rms_normed(source).astype(jnp.bfloat16)
    queries = (jnp.dot(normed, w_query, preferred_element_type=jnp.float32) * HEAD ** (-0.5)).astype(jnp.bfloat16)
    keyval = jnp.stack([jnp.dot(normed, w_keyval[0], preferred_element_type=jnp.float32), jnp.dot(normed, w_keyval[1], preferred_element_type=jnp.float32)]).astype(jnp.bfloat16)
    return (queries, keyval)

def policy_backward(hidden, action_ids, advantage, old_values, live_mask, live_total, w_policy):
    source = hidden.astype(jnp.float32)
    normed = rms_normed(source)
    logits = jnp.dot(normed.astype(jnp.bfloat16), w_policy, preferred_element_type=jnp.float32)
    log_probs = jax.nn.log_softmax(logits, axis=-1)
    onehot = (action_ids[:, None] == lax.broadcasted_iota(jnp.int32, logits.shape, 1)).astype(jnp.float32)
    chosen = lax.optimization_barrier(jnp.sum(onehot * log_probs, axis=-1))
    prob_ratio = jnp.exp(chosen - old_values)
    plain_term = prob_ratio * advantage
    bounded = jnp.clip(prob_ratio, 1.0 - clip_range, 1.0 + clip_range) * advantage
    slope_term = jnp.where(live_mask & (plain_term <= bounded), -plain_term / live_total, jnp.float32(0.0))
    dlogits = slope_term[:, None] * (onehot - jnp.exp(log_probs))
    dnormed = jnp.dot(dlogits, w_policy.astype(jnp.float32).T, precision=lax.Precision.HIGHEST)
    return norm_backward(source, normed, dnormed)

def value_backward(mixed_out, target, live_mask, live_total, w_value):
    normed = rms_normed(mixed_out)
    value_pred = jnp.dot(normed.astype(jnp.bfloat16), w_value, preferred_element_type=jnp.float32)
    slope_term = jnp.where(live_mask, value_pred - target, jnp.float32(0.0)) / live_total
    dnormed = slope_term[:, None] * w_value.astype(jnp.float32)[None, :]
    return (value_pred, norm_backward(mixed_out, normed, dnormed))

def attend(queries, keyval, live_mask):
    row_count = queries.shape[0]
    kv_heads = keyval.shape[2] // HEAD
    groups = queries.shape[1] // HEAD // kv_heads
    key_rows = keyval[0].reshape(row_count, kv_heads, HEAD).astype(jnp.float32)
    value_rows = keyval[1].reshape(row_count, kv_heads, HEAD).astype(jnp.float32)
    block_rows = math.gcd(row_count, 512)

    def absorb_block(query_block):
        query_f = query_block.reshape(block_rows, kv_heads, groups, HEAD).astype(jnp.float32)
        scores = jnp.einsum('bkgd,jkd->kgbj', query_f, key_rows)
        scores = jnp.where(live_mask, scores, masked_score)
        row_top = lax.optimization_barrier(jnp.max(scores, axis=-1, keepdims=True))
        weights = jnp.exp(scores - row_top)
        row_sum = lax.optimization_barrier(jnp.sum(weights, axis=-1))
        combined = jnp.einsum('kgbj,jkd->bkgd', weights, value_rows, precision=lax.Precision.HIGHEST)
        combined = combined / jnp.transpose(row_sum, (2, 0, 1))[..., None]
        return combined.reshape(block_rows, kv_heads * groups * HEAD)
    attended = lax.map(absorb_block, queries.reshape(row_count // block_rows, block_rows, -1))
    return attended.reshape(row_count, -1).astype(jnp.bfloat16)

def reference(obs, a_query, a_keyval, a_out, w_policy, c_in, c_query, c_keyval, c_out, w_value, actions, advantages, old_logp, returns, robot_count):
    live_total = jnp.sum(robot_count).astype(jnp.float32)
    actor_grad = jnp.zeros((HA * HEAD, DA), jnp.float32)
    critic_grad = jnp.zeros((HC * HEAD, DC), jnp.float32)
    value_list = []
    for batch_index in range(2):
        live_mask = lax.iota(jnp.int32, ROBOTS) < robot_count[batch_index]
        obs_float = obs[batch_index].astype(jnp.float32)
        queries, keyval = project(obs_float, a_query, a_keyval)
        attended = attend(queries, keyval, live_mask)
        hidden = (obs_float + jnp.dot(attended, a_out, preferred_element_type=jnp.float32)).astype(jnp.bfloat16)
        dhidden = policy_backward(hidden, actions[batch_index], advantages[batch_index], old_logp[batch_index], live_mask, live_total, w_policy).astype(jnp.bfloat16)
        actor_grad = actor_grad + jnp.dot(attended.T, dhidden, preferred_element_type=jnp.float32)
        embedded = jnp.dot(hidden, c_in, preferred_element_type=jnp.float32).astype(jnp.bfloat16)
        embed_float = embedded.astype(jnp.float32)
        critic_queries, critic_keyval = project(embed_float, c_query, c_keyval)
        critic_attended = attend(critic_queries, critic_keyval, live_mask)
        mixed_out = embed_float + jnp.dot(critic_attended, c_out, preferred_element_type=jnp.float32)
        value_pred, dmixed = value_backward(mixed_out, returns[batch_index], live_mask, live_total, w_value)
        critic_grad = critic_grad + jnp.dot(critic_attended.T, dmixed.astype(jnp.bfloat16), preferred_element_type=jnp.float32)
        value_list.append(value_pred)
    return (jnp.stack(value_list), actor_grad, critic_grad)
```

```python
import functools
import math

import jax
import jax.numpy as jnp
from jax import lax
from jax.experimental import pallas as pl
from jax.experimental.pallas import tpu as pltpu
from jax.sharding import PartitionSpec as P

HEAD = 128
epsilon = 1e-05
clip_range = 0.2
masked_score = -1e30
LOG2E = 1.4426950408889634
F32 = jnp.float32
BF16 = jnp.bfloat16


def dot(a, b):
    return jnp.dot(a, b, preferred_element_type=F32)


def row_factor(source):
    return lax.rsqrt(jnp.mean(source * source, axis=-1, keepdims=True) + epsilon)


def attend_kernel(total_ref, q_ref, k_ref, v_ref, o_ref):
    keys = k_ref[0]
    vals = v_ref[0]
    count = keys.shape[0]
    scores = lax.dot_general(
        q_ref[...], keys, (((1,), (1,)), ((), ())), preferred_element_type=F32
    )
    live = lax.broadcasted_iota(jnp.int32, (1, count), 1) < total_ref[0]
    scores = jnp.where(live, scores, masked_score)
    top = jnp.max(scores, axis=-1, keepdims=True)
    weights = jnp.exp2(scores - top).astype(BF16)
    wide = jnp.concatenate([vals, jnp.ones_like(vals)], axis=1)
    both = dot(weights, wide)
    o_ref[...] = (both[:, :HEAD] / both[:, HEAD:]).astype(BF16)


def attend(queries, keyval, robot_total):
    rows, width = queries.shape
    count = keyval.shape[1]
    heads = width // HEAD
    groups = heads // (keyval.shape[2] // HEAD)
    block = math.gcd(rows, max(16, 256 * 2048 // max(count, 2048)))
    flops = 4 * rows * count * width
    return pl.pallas_call(
        attend_kernel,
        grid=(heads, rows // block),
        in_specs=[
            pl.BlockSpec(memory_space=pltpu.SMEM),
            pl.BlockSpec((block, HEAD), lambda h, i: (i, h)),
            pl.BlockSpec((1, count, HEAD), lambda h, i: (0, 0, h // groups)),
            pl.BlockSpec((1, count, HEAD), lambda h, i: (1, 0, h // groups)),
        ],
        out_specs=pl.BlockSpec((block, HEAD), lambda h, i: (i, h)),
        out_shape=jax.ShapeDtypeStruct((rows, width), BF16),
        compiler_params=pltpu.CompilerParams(vmem_limit_bytes=40 * 2**20),
        cost_estimate=pl.CostEstimate(
            flops=flops, bytes_accessed=4 * rows * width, transcendentals=rows * count * heads
        ),
        name="attend",
    )(robot_total.reshape(1), queries, keyval, keyval)


def gather_codes(size):
    codes = [0]
    bit = size // 2
    while bit >= 1:
        codes = codes + [c ^ bit for c in codes]
        bit //= 2
    return codes


def gather_blocks(block, axis):
    size = lax.axis_size(axis)
    blocks = [block]
    bit = size // 2
    while bit >= 1:
        perm = [(i, i ^ bit) for i in range(size)]
        blocks = blocks + [lax.ppermute(b, axis, perm) for b in blocks]
        bit //= 2
    return blocks


def on_device(
    obs,
    a_query,
    a_keyval,
    a_out,
    w_policy,
    c_in,
    c_query,
    c_keyval,
    c_out,
    w_value,
    actions,
    advantages,
    old_logp,
    returns,
    robot_count,
):
    row_count = obs.shape[1]
    batch_index = lax.axis_index("sec")
    robot_total = robot_count[batch_index]
    live_total = jnp.sum(robot_count).astype(F32)
    first_row = lax.axis_index("rep") * row_count
    live_mask = first_row + lax.iota(jnp.int32, row_count) < robot_total
    mdl_count = lax.axis_size("mdl")
    mdl_index = lax.axis_index("mdl")
    part_rows = row_count // mdl_count
    row_start = mdl_index * part_rows
    codes = gather_codes(mdl_count)
    score_scale = HEAD ** (-0.5) * LOG2E

    obs_in = obs[0]
    obs_float = obs_in.astype(F32)
    factor_a = row_factor(obs_float)
    keyval = jnp.stack([dot(obs_in, a_keyval[c]) * factor_a for c in range(2)]).astype(BF16)
    keyval_all = lax.all_gather(keyval, "rep", axis=1, tiled=True)

    a_out_blocks = gather_blocks(a_out, "mdl")
    c_in_blocks = gather_blocks(c_in, "mdl")
    c_out_blocks = gather_blocks(c_out, "mdl")

    queries = (dot(obs_in, a_query) * (factor_a * score_scale)).astype(BF16)
    attended = attend(queries, keyval_all, robot_total)
    attended_blocks = gather_blocks(attended, "mdl")
    hidden = obs_float
    for att, weight in zip(attended_blocks, a_out_blocks):
        hidden = hidden + dot(att, weight)
    hidden = hidden.astype(BF16)

    width_c = c_in.shape[1]
    c_in_all = jnp.zeros((c_in.shape[0], width_c * mdl_count), BF16)
    for code, weight in zip(codes, c_in_blocks):
        c_in_all = lax.dynamic_update_slice(c_in_all, weight, (0, (mdl_index ^ code) * width_c))
    embedded = dot(hidden, c_in_all).astype(BF16)
    embed_float = embedded.astype(F32)
    factor_c = row_factor(embed_float)
    critic_keyval = jnp.stack(
        [dot(embedded, c_keyval[c]) * factor_c for c in range(2)]
    ).astype(BF16)
    critic_keyval_all = lax.all_gather(critic_keyval, "rep", axis=1, tiled=True)
    critic_queries = (dot(embedded, c_query) * (factor_c * score_scale)).astype(BF16)

    source = hidden.astype(F32)
    factor_h = row_factor(source)
    logits = dot(hidden, w_policy) * factor_h
    log_probs = jax.nn.log_softmax(logits, axis=-1)
    onehot = (
        actions[0][:, None] == lax.broadcasted_iota(jnp.int32, logits.shape, 1)
    ).astype(F32)
    chosen = jnp.sum(onehot * log_probs, axis=-1)
    prob_ratio = jnp.exp(chosen - old_logp[0])
    plain_term = prob_ratio * advantages[0]
    bounded = jnp.clip(prob_ratio, 1.0 - clip_range, 1.0 + clip_range) * advantages[0]
    slope = jnp.where(live_mask & (plain_term <= bounded), -plain_term / live_total, F32(0.0))
    dlogits = slope[:, None] * (onehot - jnp.exp(log_probs))
    along = jnp.sum(dlogits * logits, axis=-1, keepdims=True) / source.shape[1]
    dnormed = dot(dlogits.astype(BF16), w_policy.T)
    dhidden = (factor_h * (dnormed - source * (factor_h * along))).astype(BF16)
    actor_grad = jnp.einsum("rh,rd->hd", attended, dhidden, preferred_element_type=F32)
    actor_summed = lax.psum(actor_grad.astype(BF16), ("rep", "sec"))

    critic_attended = attend(critic_queries, critic_keyval_all, robot_total)
    critic_blocks = gather_blocks(critic_attended, "mdl")
    mixed = embed_float
    for att, weight in zip(critic_blocks, c_out_blocks):
        mixed = mixed + dot(att, weight)

    w_value_float = w_value.astype(F32)
    factor_v = row_factor(mixed)
    value_pred = factor_v[:, 0] * jnp.sum(mixed * w_value_float[None, :], axis=-1)
    dvalues = jnp.where(live_mask, value_pred - returns[0], F32(0.0)) / live_total
    pull = factor_v[:, 0] * value_pred / mixed.shape[1]
    dmixed = (
        (factor_v * dvalues[:, None]) * (w_value_float[None, :] - mixed * pull[:, None])
    ).astype(BF16)
    critic_grad = jnp.einsum(
        "rh,rd->hd", critic_attended, dmixed, preferred_element_type=F32
    ).astype(BF16)
    critic_grad, actor_summed = lax.optimization_barrier((critic_grad, actor_summed))
    critic_summed = lax.psum(critic_grad, ("rep", "sec"))
    value_part = lax.dynamic_slice_in_dim(value_pred, row_start, part_rows, 0)
    return (value_part[None, :], actor_summed.astype(F32), critic_summed.astype(F32))


def solution(mesh):
    return jax.shard_map(
        on_device,
        mesh=mesh,
        in_specs=(
            P("sec", "rep", None),
            P(None, "mdl"),
            P(None, None, "mdl"),
            P("mdl", None),
            P(),
            P(None, "mdl"),
            P(None, "mdl"),
            P(None, None, "mdl"),
            P("mdl", None),
            P(),
            P("sec", "rep"),
            P("sec", "rep"),
            P("sec", "rep"),
            P("sec", "rep"),
            P(),
        ),
        out_specs=(P("sec", ("rep", "mdl")), P("mdl", None), P("mdl", None)),
        check_vma=False,
    )
```

```python
import functools
import math

import jax
import jax.numpy as jnp
from jax import lax
from jax.experimental import pallas as pl
from jax.experimental.pallas import tpu as pltpu
from jax.sharding import PartitionSpec as P

HEAD = 128
epsilon = 1e-05
clip_range = 0.2
masked_score = -1e30
LOG2E = 1.4426950408889634
F32 = jnp.float32
BF16 = jnp.bfloat16
CHUNKS = 2
LIMIT = 48 * 2**20
VMEM = pl.BlockSpec(memory_space=pltpu.VMEM)


def dot(a, b):
    return jnp.dot(a, b, preferred_element_type=F32)


def tied(*items):
    return lax.optimization_barrier(items)


def row_factor(source):
    return lax.rsqrt(jnp.mean(source * source, axis=-1, keepdims=True) + epsilon)


def whole(shape):
    return pl.BlockSpec(shape, lambda *_: (0,) * len(shape))


def first_kernel(obs_ref, w_ref, kv_ref, factor_ref):
    rows = obs_ref[...]
    factor = row_factor(rows.astype(F32))
    both = dot(rows, jnp.concatenate([w_ref[0], w_ref[1]], axis=1)) * factor
    width = w_ref.shape[2]
    kv_ref[0] = both[:, :width].astype(BF16)
    kv_ref[1] = both[:, width:].astype(BF16)
    factor_ref[...] = jnp.broadcast_to(factor, factor_ref.shape)


def first_projection(obs, w_keyval):
    rows, depth = obs.shape
    width = w_keyval.shape[2]
    block = rows // 2
    return pl.pallas_call(
        first_kernel,
        grid=(rows // block,),
        in_specs=[pl.BlockSpec((block, depth), lambda i: (i, 0)), whole(w_keyval.shape)],
        out_specs=[
            pl.BlockSpec((2, block, width), lambda i: (0, i, 0)),
            pl.BlockSpec((block, HEAD), lambda i: (i, 0)),
        ],
        out_shape=[
            jax.ShapeDtypeStruct((2, rows, width), BF16),
            jax.ShapeDtypeStruct((rows, HEAD), F32),
        ],
        compiler_params=pltpu.CompilerParams(vmem_limit_bytes=LIMIT),
        cost_estimate=pl.CostEstimate(
            flops=4 * rows * depth * width, bytes_accessed=2 * rows * depth, transcendentals=0
        ),
        name="first_projection",
    )(obs, w_keyval)


def attend_kernel(total_ref, q_ref, k_ref, v_ref, o_ref):
    keys = k_ref[0]
    vals = v_ref[0]
    count = keys.shape[0]
    scores = lax.dot_general(
        q_ref[...], keys, (((1,), (1,)), ((), ())), preferred_element_type=F32
    )
    live = lax.broadcasted_iota(jnp.int32, (1, count), 1) < total_ref[0]
    scores = jnp.where(live, scores, masked_score)
    top = jnp.max(scores, axis=-1, keepdims=True)
    weights = jnp.exp2(scores - top).astype(BF16)
    wide = jnp.concatenate([vals, jnp.ones_like(vals)], axis=1)
    both = dot(weights, wide)
    o_ref[...] = (both[:, :HEAD] / both[:, HEAD:]).astype(BF16)


def attend(queries, keyval, robot_total):
    rows, width = queries.shape
    count = keyval.shape[1]
    heads = width // HEAD
    groups = heads // (keyval.shape[2] // HEAD)
    block = math.gcd(rows, max(16, 256 * 2048 // max(count, 2048)))
    flops = 4 * rows * count * width
    return pl.pallas_call(
        attend_kernel,
        grid=(heads, rows // block),
        in_specs=[
            pl.BlockSpec(memory_space=pltpu.SMEM),
            pl.BlockSpec((block, HEAD), lambda h, i: (i, h)),
            pl.BlockSpec((1, count, HEAD), lambda h, i: (0, 0, h // groups)),
            pl.BlockSpec((1, count, HEAD), lambda h, i: (1, 0, h // groups)),
        ],
        out_specs=pl.BlockSpec((block, HEAD), lambda h, i: (i, h)),
        out_shape=jax.ShapeDtypeStruct((rows, width), BF16),
        compiler_params=pltpu.CompilerParams(vmem_limit_bytes=LIMIT),
        cost_estimate=pl.CostEstimate(
            flops=flops, bytes_accessed=4 * rows * width, transcendentals=rows * count * heads
        ),
        name="attend",
    )(robot_total.reshape(1), queries, keyval, keyval)


def hidden_kernel(place_ref, obs_ref, t0, t1, t2, t3, w0, w1, w20, w21, w30, w31, o_ref):
    step = pl.program_id(0)

    def fill(w2, w3):
        total = obs_ref[...].astype(F32)
        for part, weight in ((t0, w0), (t1, w1), (t2, w2), (t3, w3)):
            total = total + dot(part[...], weight[...])
        o_ref[...] = total.astype(BF16)

    @pl.when(step == 0)
    def _():
        fill(w20, w30)

    @pl.when(step == 1)
    def _():
        fill(w21, w31)


def hidden_rows(place, obs, parts, full, halves):
    rows, depth = obs.shape
    inner, half = halves[0].shape
    moving = pl.BlockSpec((inner, half), lambda j, place: (0, place[0] ^ j))
    strip = pl.BlockSpec((rows, half), lambda j, place: (0, place[0] ^ j))
    return pl.pallas_call(
        hidden_kernel,
        grid_spec=pltpu.PrefetchScalarGridSpec(
            num_scalar_prefetch=1,
            grid=(2,),
            in_specs=[strip]
            + [whole(parts[0].shape)] * 4
            + [moving] * 2
            + [whole(halves[0].shape)] * 4,
            out_specs=strip,
        ),
        out_shape=jax.ShapeDtypeStruct((rows, depth), BF16),
        compiler_params=pltpu.CompilerParams(vmem_limit_bytes=LIMIT),
        cost_estimate=pl.CostEstimate(
            flops=8 * rows * depth * inner, bytes_accessed=8 * depth * inner, transcendentals=0
        ),
        name="hidden_rows",
    )(place, obs, *parts, *full, *halves)


def embed_kernel(
    place_ref, h_ref, w0, w1, w20, w21, w30, w31, wkv_ref, emb_ref, kv_ref, factor_ref
):
    step = pl.program_id(0)
    half = w0.shape[1]
    rows = h_ref.shape[0]

    def fill(w2, w3):
        for code, weight in enumerate((w0, w1, w2, w3)):
            column = ((place_ref[1] ^ code) * 2 + (place_ref[0] ^ step)) * half
            emb_ref[:, pl.ds(pl.multiple_of(column, half), half)] = dot(
                h_ref[...], weight[...]
            ).astype(BF16)

    @pl.when(step == 0)
    def _():
        fill(w20, w30)

    @pl.when(step == 1)
    def _():
        fill(w21, w31)
        width = wkv_ref.shape[2]
        both_w = jnp.concatenate([wkv_ref[0], wkv_ref[1]], axis=1)
        block = rows // 2
        for i in range(2):
            span = slice(i * block, (i + 1) * block)
            emb = emb_ref[span, :]
            factor = row_factor(emb.astype(F32))
            both = dot(emb, both_w) * factor
            kv_ref[0, span, :] = both[:, :width].astype(BF16)
            kv_ref[1, span, :] = both[:, width:].astype(BF16)
            factor_ref[span, :] = jnp.broadcast_to(factor, (block, HEAD))


def embed_rows(place, hidden, full, halves, w_keyval):
    rows, depth = hidden.shape
    half = halves[0].shape[1]
    wide = 8 * half
    width = w_keyval.shape[2]
    moving = pl.BlockSpec((depth, half), lambda j, place: (0, place[0] ^ j))
    return pl.pallas_call(
        embed_kernel,
        grid_spec=pltpu.PrefetchScalarGridSpec(
            num_scalar_prefetch=1,
            grid=(2,),
            in_specs=[whole(hidden.shape)]
            + [moving] * 2
            + [whole(halves[0].shape)] * 4
            + [whole(w_keyval.shape)],
            out_specs=[whole((rows, wide)), whole((2, rows, width)), whole((rows, HEAD))],
        ),
        out_shape=[
            jax.ShapeDtypeStruct((rows, wide), BF16),
            jax.ShapeDtypeStruct((2, rows, width), BF16),
            jax.ShapeDtypeStruct((rows, HEAD), F32),
        ],
        compiler_params=pltpu.CompilerParams(vmem_limit_bytes=LIMIT),
        cost_estimate=pl.CostEstimate(
            flops=2 * rows * depth * wide, bytes_accessed=2 * depth * wide, transcendentals=0
        ),
        name="embed_rows",
    )(place, hidden, *full, *halves, w_keyval)


def mixed_kernel(
    place_ref, emb_ref, t0, t1, t2, t3, w0, w1, w2, w3, wv_ref, ret_ref,
    value_ref, other_ref, own_ref, mixed_ref,
):
    step = pl.program_id(0)
    rows, wide = mixed_ref.shape
    strip = emb_ref.shape[1]
    total = emb_ref[...].astype(F32)
    for part, weight in ((t0, w0), (t1, w1), (t2, w2), (t3, w3)):
        total = total + dot(part[...], weight[...])
    mixed_ref[:, pl.ds(pl.multiple_of(step * strip, strip), strip)] = total

    @pl.when(step == pl.num_programs(0) - 1)
    def _():
        half = wide // 2
        block = rows // 4
        live_total = place_ref[4].astype(F32)

        @pl.loop(0, 4)
        def _(i):
            start = pl.multiple_of(i * block, block)
            span = pl.ds(start, block)
            weight = wv_ref[...].astype(F32)
            mixed = mixed_ref[span, :]
            factor = row_factor(mixed)
            value = factor * jnp.sum(mixed * weight, axis=-1, keepdims=True)
            row = place_ref[2] + start + lax.broadcasted_iota(jnp.int32, (block, 1), 0)
            gap = jnp.where(row < place_ref[3], value - ret_ref[span, :], F32(0.0)) / live_total
            lead = factor * gap
            pull = factor * value / wide
            value_ref[span, :] = jnp.broadcast_to(value, (block, HEAD))
            for out, side in ((own_ref, place_ref[0]), (other_ref, 1 - place_ref[0])):
                columns = pl.ds(pl.multiple_of(side * half, half), half)
                part = mixed_ref[span, columns]
                out[span, :] = (
                    lead * (wv_ref[:, columns].astype(F32) - part * pull)
                ).astype(BF16)


def mixed_rows(place, embedded, parts, weights, w_value, returns):
    rows, wide = embedded.shape
    inner = weights[0].shape[0]
    strip = wide // 4
    moving = pl.BlockSpec((inner, strip), lambda j, place: (0, j))
    return pl.pallas_call(
        mixed_kernel,
        grid_spec=pltpu.PrefetchScalarGridSpec(
            num_scalar_prefetch=1,
            grid=(4,),
            in_specs=[pl.BlockSpec((rows, strip), lambda j, place: (0, j))]
            + [whole(parts[0].shape)] * 4
            + [moving] * 4
            + [whole((1, wide)), whole((rows, 1))],
            out_specs=[
                whole((rows, HEAD)),
                whole((rows, wide // 2)),
                whole((rows, wide // 2)),
            ],
            scratch_shapes=[pltpu.VMEM((rows, wide), F32)],
        ),
        out_shape=[
            jax.ShapeDtypeStruct((rows, HEAD), F32),
            jax.ShapeDtypeStruct((rows, wide // 2), BF16),
            jax.ShapeDtypeStruct((rows, wide // 2), BF16),
        ],
        compiler_params=pltpu.CompilerParams(vmem_limit_bytes=LIMIT),
        cost_estimate=pl.CostEstimate(
            flops=8 * rows * wide * inner, bytes_accessed=8 * wide * inner, transcendentals=0
        ),
        name="mixed_rows",
    )(place, embedded, *parts, *weights, w_value.reshape(1, wide), returns.reshape(rows, 1))


def split_kernel(index_ref, own_ref, got_ref, *out_refs):
    count = len(out_refs)
    block = out_refs[0].shape[0]
    for k, out in enumerate(out_refs):
        owner = lax.rem(index_ref[0] + k, count)
        span = pl.ds(pl.multiple_of(owner * block, block), block)
        out[...] = (own_ref[span, :] + got_ref[span, :].astype(F32)).astype(BF16)


def split_sum(index, own, got, count):
    rows, wide = own.shape
    if (rows // count) % 16:
        got = got.astype(F32)
    shape = jax.ShapeDtypeStruct((rows // count, wide), BF16)
    return pl.pallas_call(
        split_kernel,
        in_specs=[pl.BlockSpec(memory_space=pltpu.SMEM), VMEM, VMEM],
        out_specs=[VMEM] * count,
        out_shape=[shape] * count,
        compiler_params=pltpu.CompilerParams(vmem_limit_bytes=LIMIT),
        cost_estimate=pl.CostEstimate(
            flops=rows * wide, bytes_accessed=8 * rows * wide, transcendentals=0
        ),
        name="split_sum",
    )(index, own, got)


def assemble_kernel(count, chunks, place_ref, *refs):
    out = refs[-1]
    block, strip = refs[0].shape
    for c in range(chunks):
        for side in range(2):
            for k in range(count):
                part = refs[(c * 2 + side) * count + k]
                owner = lax.rem(place_ref[1] + count - k, count)
                column = ((place_ref[0] ^ side) * chunks + c) * strip
                out[
                    pl.ds(pl.multiple_of(owner * block, block), block),
                    pl.ds(pl.multiple_of(column, strip), strip),
                ] = part[...].astype(F32)


def assemble(place, parts, count, chunks):
    block, strip = parts[0].shape
    rows, wide = block * count, strip * 2 * chunks
    return pl.pallas_call(
        functools.partial(assemble_kernel, count, chunks),
        in_specs=[pl.BlockSpec(memory_space=pltpu.SMEM)] + [VMEM] * len(parts),
        out_specs=VMEM,
        out_shape=jax.ShapeDtypeStruct((rows, wide), F32),
        compiler_params=pltpu.CompilerParams(vmem_limit_bytes=LIMIT),
        cost_estimate=pl.CostEstimate(
            flops=rows * wide, bytes_accessed=6 * rows * wide, transcendentals=0
        ),
        name="assemble",
    )(place, *parts)


def swap(block, axis, bit):
    size = lax.axis_size(axis)
    return lax.ppermute(block, axis, [(i, i ^ bit) for i in range(size)])


def shift(block, axis, step):
    size = lax.axis_size(axis)
    return lax.ppermute(block, axis, [(i, (i + step) % size) for i in range(size)])


def gather_parts(part):
    far = swap(part, "mdl", 2)
    return [part, swap(part, "mdl", 1), far, swap(far, "mdl", 1)], far


def product(left, right):
    return jnp.einsum("rh,rd->hd", left, right, preferred_element_type=F32)


def scatter_shifts(blocks):
    return [shift(block, "rep", k) for k, block in enumerate(blocks) if k > 0]


def shift_total(blocks, moved):
    total = blocks[0].astype(F32)
    for block in moved:
        total = total + block.astype(F32)
    return total.astype(BF16)


def gather_shifts(total):
    return [total] + [shift(total, "rep", k) for k in range(1, lax.axis_size("rep"))]


def half_of(weight, side):
    half = weight.shape[1] // 2
    return lax.dynamic_slice_in_dim(weight, side * half, half, 1)


def on_device(
    obs,
    a_query,
    a_keyval,
    a_out,
    w_policy,
    c_in,
    c_query,
    c_keyval,
    c_out,
    w_value,
    actions,
    advantages,
    old_logp,
    returns,
    robot_count,
):
    row_count = obs.shape[1]
    batch_index = lax.axis_index("sec")
    rep_index = lax.axis_index("rep")
    rep_count = lax.axis_size("rep")
    robot_total = robot_count[batch_index]
    live_sum = jnp.sum(robot_count)
    live_total = live_sum.astype(F32)
    first_row = rep_index * row_count
    live_mask = first_row + lax.iota(jnp.int32, row_count) < robot_total
    mdl_count = lax.axis_size("mdl")
    assert mdl_count == 4 and lax.axis_size("sec") == 2
    mdl_index = lax.axis_index("mdl")
    part_rows = row_count // mdl_count
    row_start = mdl_index * part_rows
    score_scale = HEAD ** (-0.5) * LOG2E
    rep_place = rep_index.reshape(1).astype(jnp.int32)
    place = jnp.stack([batch_index, mdl_index, first_row, robot_total, live_sum]).astype(jnp.int32)

    obs_in = obs[0]
    keyval, factor_a = first_projection(obs_in, a_keyval)
    keyval_all = lax.all_gather(keyval, "rep", axis=1, tiled=True)

    a_near = swap(a_out, "mdl", 1)
    c_near = swap(c_in, "mdl", 1)
    a_far0 = swap(half_of(a_out, batch_index), "mdl", 2)
    a_far0, c_src = tied(a_far0, half_of(c_in, batch_index))
    a_far1 = swap(a_far0, "sec", 1)
    c_far0 = swap(c_src, "mdl", 2)

    queries = (dot(obs_in, a_query) * (factor_a[:, :1] * score_scale)).astype(BF16)
    queries, a_far0 = tied(queries, a_far0)
    attended = attend(queries, keyval_all, robot_total)
    attended, a_far1, c_far0 = tied(attended, a_far1, c_far0)
    attended_parts, attended_far = gather_parts(attended)
    c_far1 = swap(c_far0, "sec", 1)
    a_halves = [a_far0, a_far1, swap(a_far0, "mdl", 1), swap(a_far1, "mdl", 1)]
    c_halves = [c_far0, c_far1, swap(c_far0, "mdl", 1), swap(c_far1, "mdl", 1)]
    hidden = hidden_rows(place, obs_in, attended_parts, [a_out, a_near], a_halves)

    attended_far, c_out_src = tied(attended_far, c_out)
    c_out_far = swap(c_out_src, "mdl", 2)

    embedded, critic_keyval, factor_c = embed_rows(
        place, hidden, [c_in, c_near], c_halves, c_keyval
    )
    critic_keyval_all = lax.all_gather(critic_keyval, "rep", axis=1, tiled=True)
    critic_queries = (dot(embedded, c_query) * (factor_c[:, :1] * score_scale)).astype(BF16)

    late_hidden, critic_keyval = tied(hidden, critic_keyval)
    source = late_hidden.astype(F32)
    factor_h = row_factor(source)
    logits = dot(late_hidden, w_policy) * factor_h
    log_probs = jax.nn.log_softmax(logits, axis=-1)
    onehot = (
        actions[0][:, None] == lax.broadcasted_iota(jnp.int32, logits.shape, 1)
    ).astype(F32)
    chosen = jnp.sum(onehot * log_probs, axis=-1)
    prob_ratio = jnp.exp(chosen - old_logp[0])
    plain_term = prob_ratio * advantages[0]
    bounded = jnp.clip(prob_ratio, 1.0 - clip_range, 1.0 + clip_range) * advantages[0]
    slope = jnp.where(live_mask & (plain_term <= bounded), -plain_term / live_total, F32(0.0))
    dlogits = slope[:, None] * (onehot - jnp.exp(log_probs))
    along = jnp.sum(dlogits * logits, axis=-1, keepdims=True) / source.shape[1]
    dnormed = dot(dlogits.astype(BF16), w_policy.T)
    dhidden = (factor_h * (dnormed - source * (factor_h * along))).astype(BF16)
    half_a = dhidden.shape[1] // 2
    got_a = swap(
        product(attended, lax.dynamic_slice_in_dim(dhidden, (1 - batch_index) * half_a, half_a, 1))
        .astype(BF16),
        "sec",
        1,
    )
    own_a = product(attended, lax.dynamic_slice_in_dim(dhidden, batch_index * half_a, half_a, 1))
    blocks_a = split_sum(rep_place, own_a, got_a, rep_count)
    critic_queries, *blocks_a = tied(critic_queries, *blocks_a)

    moved_a = scatter_shifts(blocks_a)
    critic_attended = attend(critic_queries, critic_keyval_all, robot_total)
    critic_attended, *moved_a = tied(critic_attended, *moved_a)
    critic_attended, c_out_far = tied(critic_attended, c_out_far)
    mine_a = gather_shifts(shift_total(blocks_a, moved_a))
    critic_parts, critic_far = gather_parts(critic_attended)
    critic_near, *mine_a = tied(critic_parts[3], *mine_a)
    critic_parts[3] = critic_near
    c_out_all = [c_out, swap(c_out, "mdl", 1), c_out_far, swap(c_out_far, "mdl", 1)]
    pieces_a = mine_a + [swap(block, "sec", 1) for block in mine_a]
    value_wide, d_other, d_own = mixed_rows(
        place, embedded, critic_parts, c_out_all, w_value, returns[0]
    )

    strip = d_own.shape[1] // CHUNKS
    spans = [slice(c * strip, (c + 1) * strip) for c in range(CHUNKS)]
    got = [
        swap(product(critic_attended, d_other[:, span]).astype(BF16), "sec", 1) for span in spans
    ]
    own = [product(critic_attended, d_own[:, span]) for span in spans]
    pieces = []
    for c in range(CHUNKS):
        blocks = split_sum(rep_place, own[c], got[c], rep_count)
        mine = gather_shifts(shift_total(blocks, scatter_shifts(blocks)))
        pieces += mine + [swap(block, "sec", 1) for block in mine]
    corner = jnp.stack([batch_index, rep_index]).astype(jnp.int32)
    actor_summed = assemble(corner, pieces_a, rep_count, 1)
    critic_summed = assemble(corner, pieces, rep_count, CHUNKS)

    value_part = lax.dynamic_slice_in_dim(value_wide, row_start, part_rows, 0)[:, 0]
    return (value_part[None, :], actor_summed, critic_summed)


def solution(mesh):
    return jax.shard_map(
        on_device,
        mesh=mesh,
        in_specs=(
            P("sec", "rep", None),
            P(None, "mdl"),
            P(None, None, "mdl"),
            P("mdl", None),
            P(),
            P(None, "mdl"),
            P(None, "mdl"),
            P(None, None, "mdl"),
            P("mdl", None),
            P(),
            P("sec", "rep"),
            P("sec", "rep"),
            P("sec", "rep"),
            P("sec", "rep"),
            P(),
        ),
        out_specs=(P("sec", ("rep", "mdl")), P("mdl", None), P("mdl", None)),
        check_vma=False,
    )
```

```python
import functools
import math

import jax
import jax.numpy as jnp
from jax import lax
from jax.experimental import pallas as pl
from jax.experimental.pallas import tpu as pltpu
from jax.sharding import PartitionSpec as P

HEAD = 128
epsilon = 1e-05
clip_range = 0.2
masked_score = -1e30
LOG2E = 1.4426950408889634
F32 = jnp.float32
BF16 = jnp.bfloat16
CHUNKS = 2
LIMIT = 40 * 2**20
SMALL = 20 * 2**20
VMEM = pl.BlockSpec(memory_space=pltpu.VMEM)


def dot(a, b):
    return jnp.dot(a, b, preferred_element_type=F32)


def tied(*items):
    return lax.optimization_barrier(items)


def row_factor(source):
    return lax.rsqrt(jnp.mean(source * source, axis=-1, keepdims=True) + epsilon)


def whole(shape):
    return pl.BlockSpec(shape, lambda *_: (0,) * len(shape))


def first_kernel(obs_ref, w_ref, kv_ref, factor_ref):
    rows = obs_ref[...]
    factor = row_factor(rows.astype(F32))
    both = dot(rows, jnp.concatenate([w_ref[0], w_ref[1]], axis=1)) * factor
    width = w_ref.shape[2]
    kv_ref[0] = both[:, :width].astype(BF16)
    kv_ref[1] = both[:, width:].astype(BF16)
    factor_ref[...] = jnp.broadcast_to(factor, factor_ref.shape)


def first_projection(obs, w_keyval):
    rows, depth = obs.shape
    width = w_keyval.shape[2]
    block = rows // 2
    return pl.pallas_call(
        first_kernel,
        grid=(rows // block,),
        in_specs=[pl.BlockSpec((block, depth), lambda i: (i, 0)), whole(w_keyval.shape)],
        out_specs=[
            pl.BlockSpec((2, block, width), lambda i: (0, i, 0)),
            pl.BlockSpec((block, HEAD), lambda i: (i, 0)),
        ],
        out_shape=[
            jax.ShapeDtypeStruct((2, rows, width), BF16),
            jax.ShapeDtypeStruct((rows, HEAD), F32),
        ],
        compiler_params=pltpu.CompilerParams(vmem_limit_bytes=LIMIT),
        cost_estimate=pl.CostEstimate(
            flops=4 * rows * depth * width, bytes_accessed=2 * rows * depth, transcendentals=0
        ),
        name="first_projection",
    )(obs, w_keyval)


def attend_blocks(groups, units, left_ref, q_ref, kv_refs):
    def fetch(head, span):
        kv_head = head // groups
        columns = slice(kv_head * HEAD, (kv_head + 1) * HEAD)
        query = q_ref[span, head * HEAD : (head + 1) * HEAD]
        lane = lax.broadcasted_iota(jnp.int32, query.shape, 1)
        query = jnp.concatenate([query, (lane == 0).astype(BF16)], axis=1)
        scores = []
        for p, ref in enumerate(kv_refs):
            keys = ref[0, :, columns]
            key = lax.broadcasted_iota(jnp.int32, keys.shape, 0)
            lane = lax.broadcasted_iota(jnp.int32, keys.shape, 1)
            dead = (key >= left_ref[p]) & (lane == 0)
            bias = jnp.where(dead, F32(masked_score), F32(0.0)).astype(BF16)
            keys = jnp.concatenate([keys, bias], axis=1)
            scores.append(
                lax.dot_general(
                    query, keys, (((1,), (1,)), ((), ())), preferred_element_type=F32
                )
            )
        return scores

    def values(head, p):
        kv_head = head // groups
        vals = kv_refs[p][1, :, kv_head * HEAD : (kv_head + 1) * HEAD]
        return jnp.concatenate([vals, jnp.ones_like(vals)], axis=1)

    ahead = fetch(*units[0])
    for i, (head, span) in enumerate(units):
        scores = ahead
        if i + 1 < len(units):
            ahead = fetch(*units[i + 1])
        yield head, span, scores, functools.partial(values, head)


def weigh(scores, top, values):
    total = None
    for p, part in enumerate(scores):
        both = dot(jnp.exp2(part - top).astype(BF16), values(p))
        total = both if total is None else total + both
    return total


def highest(scores):
    return functools.reduce(
        jnp.maximum, [jnp.max(part, axis=-1, keepdims=True) for part in scores]
    )


def open_kernel(groups, units, left_ref, q_ref, *refs):
    *kv_refs, wide_ref, top_ref = refs
    for head, span, scores, values in attend_blocks(groups, units, left_ref, q_ref, kv_refs):
        top = highest(scores)
        wide_ref[span, head * 2 * HEAD : (head + 1) * 2 * HEAD] = weigh(scores, top, values)
        top_ref[span, head * HEAD : (head + 1) * HEAD] = jnp.broadcast_to(
            top, (top.shape[0], HEAD)
        )


def close_kernel(groups, units, left_ref, q_ref, wide_ref, top_ref, *refs):
    *kv_refs, o_ref = refs
    for head, span, scores, values in attend_blocks(groups, units, left_ref, q_ref, kv_refs):
        before = top_ref[span, head * HEAD : head * HEAD + 1]
        top = jnp.maximum(before, highest(scores))
        wide = wide_ref[span, head * 2 * HEAD : (head + 1) * 2 * HEAD]
        wide = wide * jnp.exp2(before - top) + weigh(scores, top, values)
        o_ref[span, head * HEAD : (head + 1) * HEAD] = (
            wide[:, :HEAD] / wide[:, HEAD:]
        ).astype(BF16)


def attend_call(queries, pieces, left, state):
    rows, width = queries.shape
    heads = width // HEAD
    groups = heads // (pieces[0].shape[2] // HEAD)
    block = min(rows, 256)
    units = [
        (head, slice(i, i + block)) for head in range(heads) for i in range(0, rows, block)
    ]
    count = len(pieces) * pieces[0].shape[1]
    if state:
        body, name = close_kernel, "attend_close"
        out = jax.ShapeDtypeStruct((rows, width), BF16)
    else:
        body, name = open_kernel, "attend_open"
        out = [
            jax.ShapeDtypeStruct((rows, 2 * width), F32),
            jax.ShapeDtypeStruct((rows, width), F32),
        ]
    return pl.pallas_call(
        functools.partial(body, groups, units),
        in_specs=[pl.BlockSpec(memory_space=pltpu.SMEM)] + [VMEM] * (1 + len(state) + len(pieces)),
        out_specs=VMEM if state else [VMEM] * 2,
        out_shape=out,
        compiler_params=pltpu.CompilerParams(vmem_limit_bytes=LIMIT),
        cost_estimate=pl.CostEstimate(
            flops=24 * rows * count * width,
            bytes_accessed=4 * rows * width,
            transcendentals=rows * count * heads,
        ),
        name=name,
    )(left, queries, *state, *pieces)


def joined(refs, columns=slice(None)):
    return jnp.concatenate([ref[:, columns] for ref in refs], axis=0)


def hidden_kernel(place_ref, obs_ref, t0, t1, t2, t3, w0, w1, w20, w21, w30, w31, o_ref):
    half = w20.shape[1]
    tile = half // 3
    for side, (w2, w3) in enumerate(((w20, w30), (w21, w31))):
        start = (place_ref[0] ^ side) * half
        for i in range(3):
            near = pl.ds(pl.multiple_of(start + i * tile, HEAD), tile)
            far = slice(i * tile, (i + 1) * tile)
            weight = jnp.concatenate([w0[:, near], w1[:, near], w2[:, far], w3[:, far]], axis=0)
            parts = jnp.concatenate([t0[...], t1[...], t2[...], t3[...]], axis=1)
            o_ref[:, near] = (obs_ref[:, near].astype(F32) + dot(parts, weight)).astype(BF16)


def hidden_rows(place, obs, parts, full, halves):
    rows, depth = obs.shape
    inner = halves[0].shape[0]
    return pl.pallas_call(
        hidden_kernel,
        in_specs=[pl.BlockSpec(memory_space=pltpu.SMEM)] + [VMEM] * 11,
        out_specs=VMEM,
        out_shape=jax.ShapeDtypeStruct((rows, depth), BF16),
        compiler_params=pltpu.CompilerParams(vmem_limit_bytes=SMALL),
        cost_estimate=pl.CostEstimate(
            flops=8 * rows * depth * inner, bytes_accessed=8 * depth * inner, transcendentals=0
        ),
        name="hidden_rows",
    )(place, obs, *parts, *full, *halves)


def embed_kernel(place_ref, h_ref, w0, w1, *refs):
    far, (wkv_ref, emb_ref, kv_ref, factor_ref) = refs[:-4], refs[-4:]
    chunks = len(far) // 4
    half = far[0].shape[1]
    rows = h_ref.shape[0]
    for side in range(2):
        start = (place_ref[0] ^ side) * half
        near = pl.ds(pl.multiple_of(start, half), half)
        for code in range(4):
            if code < 2:
                weight = (w0, w1)[code][:, near]
            else:
                first = ((code - 2) * 2 + side) * chunks
                weight = joined(far[first : first + chunks])
            column = (place_ref[1] ^ code) * 2 * half + start
            emb_ref[:, pl.ds(pl.multiple_of(column, half), half)] = dot(
                h_ref[...], weight
            ).astype(BF16)
    width = wkv_ref.shape[2]
    both_w = jnp.concatenate([wkv_ref[0], wkv_ref[1]], axis=1)
    block = rows // 2
    for i in range(2):
        span = slice(i * block, (i + 1) * block)
        emb = emb_ref[span, :]
        factor = row_factor(emb.astype(F32))
        both = dot(emb, both_w) * factor
        kv_ref[0, span, :] = both[:, :width].astype(BF16)
        kv_ref[1, span, :] = both[:, width:].astype(BF16)
        factor_ref[span, :] = jnp.broadcast_to(factor, (block, HEAD))


def embed_rows(place, hidden, full, far, w_keyval):
    rows, depth = hidden.shape
    wide = full[0].shape[1] * 4
    width = w_keyval.shape[2]
    return pl.pallas_call(
        embed_kernel,
        in_specs=[pl.BlockSpec(memory_space=pltpu.SMEM)] + [VMEM] * (4 + len(far)),
        out_specs=[VMEM] * 3,
        out_shape=[
            jax.ShapeDtypeStruct((rows, wide), BF16),
            jax.ShapeDtypeStruct((2, rows, width), BF16),
            jax.ShapeDtypeStruct((rows, HEAD), F32),
        ],
        compiler_params=pltpu.CompilerParams(vmem_limit_bytes=SMALL),
        cost_estimate=pl.CostEstimate(
            flops=2 * rows * depth * wide, bytes_accessed=2 * depth * wide, transcendentals=0
        ),
        name="embed_rows",
    )(place, hidden, *full, *far, w_keyval)


def mixed_kernel(
    place_ref, emb_ref, t0, t1, t2, t3, w0, w1, w2, w3, wv_ref, ret_ref,
    value_ref, other_ref, own_ref, mixed_ref,
):
    rows, wide = mixed_ref.shape
    tile = 256

    @pl.loop(0, wide // tile)
    def _(j):
        columns = pl.ds(pl.multiple_of(j * tile, tile), tile)
        parts = jnp.concatenate([t0[...], t1[...], t2[...], t3[...]], axis=1)
        mixed_ref[:, columns] = emb_ref[:, columns].astype(F32) + dot(
            parts, joined((w0, w1, w2, w3), columns)
        )

    half = wide // 2
    block = rows // 8
    live_total = place_ref[4].astype(F32)

    @pl.loop(0, 8)
    def _(i):
        start = pl.multiple_of(i * block, block)
        span = pl.ds(start, block)
        weight = wv_ref[...].astype(F32)
        mixed = mixed_ref[span, :]
        factor = row_factor(mixed)
        value = factor * jnp.sum(mixed * weight, axis=-1, keepdims=True)
        row = place_ref[2] + start + lax.broadcasted_iota(jnp.int32, (block, 1), 0)
        gap = jnp.where(row < place_ref[3], value - ret_ref[span, :], F32(0.0)) / live_total
        lead = factor * gap
        pull = factor * value / wide
        value_ref[span, :] = jnp.broadcast_to(value, (block, HEAD))
        for out, side in ((own_ref, place_ref[0]), (other_ref, 1 - place_ref[0])):
            columns = pl.ds(pl.multiple_of(side * half, half), half)
            part = mixed_ref[span, columns]
            out[span, :] = (lead * (wv_ref[:, columns].astype(F32) - part * pull)).astype(BF16)


def mixed_rows(place, embedded, parts, weights, w_value, returns):
    rows, wide = embedded.shape
    inner = weights[0].shape[0]
    return pl.pallas_call(
        mixed_kernel,
        in_specs=[pl.BlockSpec(memory_space=pltpu.SMEM)] + [VMEM] * 11,
        out_specs=[VMEM] * 3,
        out_shape=[
            jax.ShapeDtypeStruct((rows, HEAD), F32),
            jax.ShapeDtypeStruct((rows, wide // 2), BF16),
            jax.ShapeDtypeStruct((rows, wide // 2), BF16),
        ],
        scratch_shapes=[pltpu.VMEM((rows, wide), F32)],
        compiler_params=pltpu.CompilerParams(vmem_limit_bytes=SMALL),
        cost_estimate=pl.CostEstimate(
            flops=8 * rows * wide * inner, bytes_accessed=8 * wide * inner, transcendentals=0
        ),
        name="mixed_rows",
    )(place, embedded, *parts, *weights, w_value.reshape(1, wide), returns.reshape(rows, 1))


def gather_codes(size):
    codes, bit = [0], size // 2
    while bit >= 1:
        codes = codes + [code ^ bit for code in codes]
        bit //= 2
    return codes


def split_kernel(codes, index_ref, own_ref, got_ref, keep_ref, send_ref):
    block = own_ref.shape[0] // len(codes)
    side = len(codes) // 2
    for k, code in enumerate(codes):
        span = pl.ds(pl.multiple_of((index_ref[0] ^ code) * block, block), block)
        out = (keep_ref, send_ref)[k // side]
        at = k % side * block
        out[at : at + block, :] = own_ref[span, :] + got_ref[span, :].astype(F32)


def split_sum(index, own, got, count):
    rows, wide = own.shape
    if (rows // count) % 16:
        got = got.astype(F32)
    shape = jax.ShapeDtypeStruct((rows // 2, wide), F32)
    return pl.pallas_call(
        functools.partial(split_kernel, gather_codes(count)),
        in_specs=[pl.BlockSpec(memory_space=pltpu.SMEM), VMEM, VMEM],
        out_specs=[VMEM] * 2,
        out_shape=[shape] * 2,
        compiler_params=pltpu.CompilerParams(vmem_limit_bytes=SMALL),
        cost_estimate=pl.CostEstimate(
            flops=rows * wide, bytes_accessed=8 * rows * wide, transcendentals=0
        ),
        name="split_sum",
    )(index, own, got)


def assemble_kernel(codes, chunks, place_ref, *refs):
    parts = refs[: len(codes) * 2 * chunks]
    out, wide_ref, sems = refs[len(parts) :]
    block, strip = parts[0].shape
    copies = []
    for c in range(chunks):
        for side in range(2):
            for k, code in enumerate(codes):
                at = (c * 2 + side) * len(codes) + k
                row = pl.multiple_of((place_ref[1] ^ code) * block, block)
                column = pl.multiple_of(((place_ref[0] ^ side) * chunks + c) * strip, strip)
                wide_ref[at] = parts[at][...].astype(F32)
                copy = pltpu.make_async_copy(
                    wide_ref.at[at],
                    out.at[pl.ds(row, block), pl.ds(column, strip)],
                    sems.at[at],
                )
                copy.start()
                copies.append(copy)
    for copy in copies:
        copy.wait()


def assemble(place, parts, count, chunks):
    block, strip = parts[0].shape
    rows, wide = block * count, strip * 2 * chunks
    return pl.pallas_call(
        functools.partial(assemble_kernel, gather_codes(count), chunks),
        in_specs=[pl.BlockSpec(memory_space=pltpu.SMEM)] + [VMEM] * len(parts),
        out_specs=pl.BlockSpec(memory_space=pl.ANY),
        out_shape=jax.ShapeDtypeStruct((rows, wide), F32),
        scratch_shapes=[
            pltpu.VMEM((len(parts), block, strip), F32),
            pltpu.SemaphoreType.DMA((len(parts),)),
        ],
        compiler_params=pltpu.CompilerParams(vmem_limit_bytes=SMALL),
        cost_estimate=pl.CostEstimate(
            flops=rows * wide, bytes_accessed=6 * rows * wide, transcendentals=0
        ),
        name="assemble",
    )(place, *parts)


def swap(block, axis, bit):
    size = lax.axis_size(axis)
    return lax.ppermute(block, axis, [(i, i ^ bit) for i in range(size)])


def gather_blocks(block, axis):
    blocks, bit = [block], lax.axis_size(axis) // 2
    while bit >= 1:
        blocks = blocks + [swap(item, axis, bit) for item in blocks]
        bit //= 2
    return blocks


def gather_parts(part):
    far = swap(part, "mdl", 2)
    return [part, swap(part, "mdl", 1), far, swap(far, "mdl", 1)], far


def product(left, right):
    return jnp.einsum("rh,rd->hd", left, right, preferred_element_type=F32)


def halve(keep, got):
    total = keep + got.astype(F32)
    side = total.shape[0] // 2
    return total[:side], total[side:].astype(BF16)


def scatter_rest(keep, got):
    bit = 2
    while bit < lax.axis_size("rep"):
        keep, send = halve(keep, got)
        got = swap(send, "rep", bit)
        bit *= 2
    return (keep + got.astype(F32)).astype(BF16)


def half_of(weight, side):
    half = weight.shape[1] // 2
    return lax.dynamic_slice_in_dim(weight, side * half, half, 1)


def on_device(
    obs,
    a_query,
    a_keyval,
    a_out,
    w_policy,
    c_in,
    c_query,
    c_keyval,
    c_out,
    w_value,
    actions,
    advantages,
    old_logp,
    returns,
    robot_count,
):
    row_count = obs.shape[1]
    batch_index = lax.axis_index("sec")
    rep_index = lax.axis_index("rep")
    rep_count = lax.axis_size("rep")
    robot_total = robot_count[batch_index]
    live_sum = jnp.sum(robot_count)
    live_total = live_sum.astype(F32)
    first_row = rep_index * row_count
    live_mask = first_row + lax.iota(jnp.int32, row_count) < robot_total
    mdl_count = lax.axis_size("mdl")
    assert mdl_count == 4 and lax.axis_size("sec") == 2
    mdl_index = lax.axis_index("mdl")
    part_rows = row_count // mdl_count
    row_start = mdl_index * part_rows
    score_scale = HEAD ** (-0.5) * LOG2E
    rep_place = rep_index.reshape(1).astype(jnp.int32)
    place = jnp.stack([batch_index, mdl_index, first_row, robot_total, live_sum]).astype(jnp.int32)

    codes = gather_codes(rep_count)
    left = jnp.stack(
        [jnp.clip(robot_total - (rep_index ^ code) * row_count, 0, row_count) for code in codes]
    ).astype(jnp.int32)

    obs_in = obs[0]
    keyval, factor_a = first_projection(obs_in, a_keyval)
    pieces_k = gather_blocks(keyval, "rep")

    a_near = swap(a_out, "mdl", 1)
    c_near = swap(c_in, "mdl", 1)
    a_far0 = swap(half_of(a_out, batch_index), "mdl", 2)
    c_half = half_of(c_in, batch_index)
    c_cut = c_half.shape[0] // 2
    c_a0 = swap(c_half[:c_cut], "mdl", 2)
    c_b0 = swap(c_half[c_cut:], "mdl", 2)

    queries = (dot(obs_in, a_query) * (factor_a[:, :1] * score_scale)).astype(BF16)
    queries, a_far0 = tied(queries, a_far0)
    a_far1 = swap(a_far0, "sec", 1)
    state = attend_call(queries, pieces_k[:-1], left[:-1], [])
    *state, c_a0 = tied(*state, c_a0)
    c_a1 = swap(c_a0, "sec", 1)
    attended = attend_call(queries, pieces_k[-1:], left[-1:], state)
    attended_near = swap(attended, "mdl", 1)
    attended_far = swap(attended, "mdl", 2)
    attended_near, c_b0 = tied(attended_near, c_b0)
    c_b1 = swap(c_b0, "sec", 1)
    attended_parts = [attended, attended_near, attended_far, swap(attended_far, "mdl", 1)]
    a_halves = [a_far0, a_far1, swap(a_far0, "mdl", 1), swap(a_far1, "mdl", 1)]
    hidden = hidden_rows(place, obs_in, attended_parts, [a_out, a_near], a_halves)
    hidden, c_b1 = tied(hidden, c_b1)
    c_far = [c_a0, c_b0, c_a1, c_b1]
    c_far = c_far + [swap(item, "mdl", 1) for item in c_far]

    attended_far, c_out_src = tied(attended_far, c_out)
    c_out_far = swap(c_out_src, "mdl", 2)

    embedded, critic_keyval, factor_c = embed_rows(place, hidden, [c_in, c_near], c_far, c_keyval)
    pieces_c = gather_blocks(critic_keyval, "rep")
    critic_queries = (dot(embedded, c_query) * (factor_c[:, :1] * score_scale)).astype(BF16)

    late_hidden, critic_keyval = tied(hidden, critic_keyval)
    source = late_hidden.astype(F32)
    factor_h = row_factor(source)
    logits = dot(late_hidden, w_policy) * factor_h
    log_probs = jax.nn.log_softmax(logits, axis=-1)
    onehot = (
        actions[0][:, None] == lax.broadcasted_iota(jnp.int32, logits.shape, 1)
    ).astype(F32)
    chosen = jnp.sum(onehot * log_probs, axis=-1)
    prob_ratio = jnp.exp(chosen - old_logp[0])
    plain_term = prob_ratio * advantages[0]
    bounded = jnp.clip(prob_ratio, 1.0 - clip_range, 1.0 + clip_range) * advantages[0]
    slope = jnp.where(live_mask & (plain_term <= bounded), -plain_term / live_total, F32(0.0))
    dlogits = slope[:, None] * (onehot - jnp.exp(log_probs))
    along = jnp.sum(dlogits * logits, axis=-1, keepdims=True) / source.shape[1]
    dnormed = dot(dlogits.astype(BF16), w_policy.T)
    dhidden = (factor_h * (dnormed - source * (factor_h * along))).astype(BF16)
    half_a = dhidden.shape[1] // 2
    got_a = swap(
        product(attended, lax.dynamic_slice_in_dim(dhidden, (1 - batch_index) * half_a, half_a, 1))
        .astype(BF16),
        "sec",
        1,
    )
    own_a = product(attended, lax.dynamic_slice_in_dim(dhidden, batch_index * half_a, half_a, 1))

    state_c = attend_call(critic_queries, pieces_c[:-1], left[:-1], [])
    *state_c, got_a = tied(*state_c, got_a)
    keep_a, send_a = split_sum(rep_place, own_a, got_a, rep_count)
    moved_a = swap(send_a.astype(BF16), "rep", 1)
    critic_attended = attend_call(critic_queries, pieces_c[-1:], left[-1:], state_c)
    critic_attended, moved_a, c_out_far = tied(critic_attended, moved_a, c_out_far)
    critic_parts, critic_far = gather_parts(critic_attended)
    mine_a = gather_blocks(scatter_rest(keep_a, moved_a), "rep")
    critic_parts[3], *mine_a = tied(critic_parts[3], *mine_a)
    c_out_all = [c_out, swap(c_out, "mdl", 1), c_out_far, swap(c_out_far, "mdl", 1)]
    pieces_a = mine_a + [swap(block, "sec", 1) for block in mine_a]
    value_wide, d_other, d_own = mixed_rows(
        place, embedded, critic_parts, c_out_all, w_value, returns[0]
    )

    strip = d_own.shape[1] // CHUNKS
    spans = [slice(c * strip, (c + 1) * strip) for c in range(CHUNKS)]
    got = [
        swap(product(critic_attended, d_other[:, span]).astype(BF16), "sec", 1) for span in spans
    ]
    own = [product(critic_attended, d_own[:, span]) for span in spans]
    pieces = []
    for c in range(CHUNKS):
        keep, send = split_sum(rep_place, own[c], got[c], rep_count)
        moved = swap(send.astype(BF16), "rep", 1)
        mine = gather_blocks(scatter_rest(keep, moved), "rep")
        pieces += mine + [swap(block, "sec", 1) for block in mine]
    corner = jnp.stack([batch_index, rep_index]).astype(jnp.int32)
    actor_summed = assemble(corner, pieces_a, rep_count, 1)
    critic_summed = assemble(corner, pieces, rep_count, CHUNKS)

    value_part = lax.dynamic_slice_in_dim(value_wide, row_start, part_rows, 0)[:, 0]
    return (value_part[None, :], actor_summed, critic_summed)


def solution(mesh):
    return jax.shard_map(
        on_device,
        mesh=mesh,
        in_specs=(
            P("sec", "rep", None),
            P(None, "mdl"),
            P(None, None, "mdl"),
            P("mdl", None),
            P(),
            P(None, "mdl"),
            P(None, "mdl"),
            P(None, None, "mdl"),
            P("mdl", None),
            P(),
            P("sec", "rep"),
            P("sec", "rep"),
            P("sec", "rep"),
            P("sec", "rep"),
            P(),
        ),
        out_specs=(P("sec", ("rep", "mdl")), P("mdl", None), P("mdl", None)),
        check_vma=False,
    )
```

```python
import functools
import math

import jax
import jax.numpy as jnp
from jax import lax
from jax.experimental import pallas as pl
from jax.experimental.pallas import tpu as pltpu
from jax.sharding import PartitionSpec as P

HEAD = 128
epsilon = 1e-05
clip_range = 0.2
masked_score = -1e30
LOG2E = 1.4426950408889634
F32 = jnp.float32
BF16 = jnp.bfloat16
CHUNKS = 2
TABLE = 6
LIMIT = 40 * 2**20
VMEM = pl.BlockSpec(memory_space=pltpu.VMEM)
SMEM = pl.BlockSpec(memory_space=pltpu.SMEM)
HBM = pl.BlockSpec(memory_space=pltpu.HBM)


def dot(a, b):
    return jnp.dot(a, b, preferred_element_type=F32)


def tied(*items):
    return lax.optimization_barrier(items)


def row_factor(source):
    return lax.rsqrt(jnp.mean(source * source, axis=-1, keepdims=True) + epsilon)


def start_copies(pairs, sems):
    copies = [
        pltpu.make_async_copy(source, target, sems.at[i])
        for i, (source, target) in enumerate(pairs)
    ]
    for copy in copies:
        copy.start()
    return copies


def first_kernel(obs_hbm, w_hbm, kv_ref, factor_ref, obs_ref, w_ref, sems):
    rows, depth = obs_ref.shape
    width = w_hbm.shape[2]
    block = rows // 2
    spans = [slice(i * block, (i + 1) * block) for i in range(2)]
    copies = start_copies(
        [(w_hbm.at[c], w_ref.at[:, c * width : (c + 1) * width]) for c in range(2)]
        + [(obs_hbm.at[span], obs_ref.at[span]) for span in spans],
        sems,
    )
    for i, span in enumerate(spans):
        copies[2 + i].wait()
        part = obs_ref[span, :]
        factor = row_factor(part.astype(F32))
        if i == 0:
            copies[0].wait()
            copies[1].wait()
        both = dot(part, w_ref[...]) * factor
        kv_ref[0, span, :] = both[:, :width].astype(BF16)
        kv_ref[1, span, :] = both[:, width:].astype(BF16)
        factor_ref[span, :] = jnp.broadcast_to(factor, (block, HEAD))


def first_projection(obs, w_keyval):
    rows, depth = obs.shape
    width = w_keyval.shape[2]
    return pl.pallas_call(
        first_kernel,
        in_specs=[HBM] * 2,
        out_specs=[VMEM] * 2,
        out_shape=[
            jax.ShapeDtypeStruct((2, rows, width), BF16),
            jax.ShapeDtypeStruct((rows, HEAD), F32),
        ],
        scratch_shapes=[
            pltpu.VMEM((rows, depth), BF16),
            pltpu.VMEM((depth, 2 * width), BF16),
            pltpu.SemaphoreType.DMA((4,)),
        ],
        compiler_params=pltpu.CompilerParams(vmem_limit_bytes=LIMIT),
        cost_estimate=pl.CostEstimate(
            flops=4 * rows * depth * width, bytes_accessed=2 * rows * depth, transcendentals=0
        ),
        name="first_projection",
    )(obs, w_keyval)


def attend_blocks(groups, units, first, left_ref, q_ref, kv_refs):
    def fetch(head, span):
        kv_head = head // groups
        columns = slice(kv_head * HEAD, (kv_head + 1) * HEAD)
        query = q_ref[span, head * HEAD : (head + 1) * HEAD]
        lane = lax.broadcasted_iota(jnp.int32, query.shape, 1)
        query = jnp.concatenate([query, (lane == 0).astype(BF16)], axis=1)
        scores = []
        for p, ref in enumerate(kv_refs):
            keys = ref[0, :, columns]
            key = lax.broadcasted_iota(jnp.int32, keys.shape, 0)
            lane = lax.broadcasted_iota(jnp.int32, keys.shape, 1)
            dead = (key >= left_ref[first + p]) & (lane == 0)
            bias = jnp.where(dead, F32(masked_score), F32(0.0)).astype(BF16)
            keys = jnp.concatenate([keys, bias], axis=1)
            scores.append(
                lax.dot_general(
                    query, keys, (((1,), (1,)), ((), ())), preferred_element_type=F32
                )
            )
        return scores

    def values(head, p):
        kv_head = head // groups
        vals = kv_refs[p][1, :, kv_head * HEAD : (kv_head + 1) * HEAD]
        return jnp.concatenate([vals, jnp.ones_like(vals)], axis=1)

    ahead = fetch(*units[0])
    for i, (head, span) in enumerate(units):
        scores = ahead
        if i + 1 < len(units):
            ahead = fetch(*units[i + 1])
        yield head, span, scores, functools.partial(values, head)


def weigh(scores, top, values):
    total = None
    for p, part in enumerate(scores):
        both = dot(jnp.exp2(part - top).astype(BF16), values(p))
        total = both if total is None else total + both
    return total


def highest(scores):
    return functools.reduce(
        jnp.maximum, [jnp.max(part, axis=-1, keepdims=True) for part in scores]
    )


def open_kernel(groups, units, first, left_ref, q_ref, *refs):
    *kv_refs, wide_ref, top_ref = refs
    for head, span, scores, values in attend_blocks(
        groups, units, first, left_ref, q_ref, kv_refs
    ):
        top = highest(scores)
        wide_ref[span, head * 2 * HEAD : (head + 1) * 2 * HEAD] = weigh(scores, top, values)
        top_ref[span, head * HEAD : (head + 1) * HEAD] = jnp.broadcast_to(
            top, (top.shape[0], HEAD)
        )


def close_kernel(groups, units, first, left_ref, q_ref, wide_ref, top_ref, *refs):
    *kv_refs, o_ref = refs
    for head, span, scores, values in attend_blocks(
        groups, units, first, left_ref, q_ref, kv_refs
    ):
        before = top_ref[span, head * HEAD : head * HEAD + 1]
        top = jnp.maximum(before, highest(scores))
        wide = wide_ref[span, head * 2 * HEAD : (head + 1) * 2 * HEAD]
        wide = wide * jnp.exp2(before - top) + weigh(scores, top, values)
        o_ref[span, head * HEAD : (head + 1) * HEAD] = (
            wide[:, :HEAD] / wide[:, HEAD:]
        ).astype(BF16)


def attend_call(queries, pieces, first, place, state):
    rows, width = queries.shape
    heads = width // HEAD
    groups = heads // (pieces[0].shape[2] // HEAD)
    block = min(rows, 256)
    units = [
        (head, slice(i, i + block)) for head in range(heads) for i in range(0, rows, block)
    ]
    count = len(pieces) * pieces[0].shape[1]
    weight = 1 if state else 24
    if state:
        body, name = close_kernel, "attend_close"
        out = jax.ShapeDtypeStruct((rows, width), BF16)
    else:
        body, name = open_kernel, "attend_open"
        out = [
            jax.ShapeDtypeStruct((rows, 2 * width), F32),
            jax.ShapeDtypeStruct((rows, width), F32),
        ]
    return pl.pallas_call(
        functools.partial(body, groups, units, TABLE + first),
        in_specs=[SMEM] + [VMEM] * (1 + len(state) + len(pieces)),
        out_specs=VMEM if state else [VMEM] * 2,
        out_shape=out,
        compiler_params=pltpu.CompilerParams(vmem_limit_bytes=LIMIT),
        cost_estimate=pl.CostEstimate(
            flops=weight * rows * count * width,
            bytes_accessed=4 * rows * width,
            transcendentals=rows * count,
        ),
        name=name,
    )(place, queries, *state, *pieces)


def hidden_kernel(
    place_ref, obs_hbm, t0, t1, t2, t3, w0, w1, w20, w21, w30, w31, o_ref, obs_ref, w_ref, sems
):
    inner, half = w20.shape
    starts = [pl.multiple_of((place_ref[0] ^ side) * half, HEAD) for side in range(2)]
    pairs = []
    for side, (w2, w3) in enumerate(((w20, w30), (w21, w31))):
        columns = pl.ds(starts[side], half)
        for k, source in enumerate((w0.at[:, columns], w1.at[:, columns], w2, w3)):
            pairs.append((source, w_ref.at[side, k * inner : (k + 1) * inner]))
        pairs.append((obs_hbm.at[:, columns], obs_ref.at[side]))
    copies = start_copies(pairs, sems)
    tile = half // 3
    for side in range(2):
        for copy in copies[side * 5 : (side + 1) * 5]:
            copy.wait()
        for i in range(3):
            strip = slice(i * tile, (i + 1) * tile)
            parts = jnp.concatenate([t0[...], t1[...], t2[...], t3[...]], axis=1)
            total = obs_ref[side, :, strip].astype(F32) + dot(parts, w_ref[side, :, strip])
            column = pl.multiple_of(starts[side] + i * tile, HEAD)
            o_ref[:, pl.ds(column, tile)] = total.astype(BF16)


def hidden_rows(place, obs, parts, full, halves):
    rows, depth = obs.shape
    inner, half = halves[0].shape
    return pl.pallas_call(
        hidden_kernel,
        in_specs=[SMEM, HBM] + [VMEM] * 4 + [HBM] * 6,
        out_specs=VMEM,
        out_shape=jax.ShapeDtypeStruct((rows, depth), BF16),
        scratch_shapes=[
            pltpu.VMEM((2, rows, half), BF16),
            pltpu.VMEM((2, 4 * inner, half), BF16),
            pltpu.SemaphoreType.DMA((10,)),
        ],
        compiler_params=pltpu.CompilerParams(vmem_limit_bytes=LIMIT),
        cost_estimate=pl.CostEstimate(
            flops=8 * rows * depth * inner, bytes_accessed=8 * depth * inner, transcendentals=0
        ),
        name="hidden_rows",
    )(place, obs, *parts, *full, *halves)


def embed_kernel(place_ref, h_ref, w0, w1, *refs):
    far, (wkv_hbm, emb_ref, kv_ref, factor_ref, w_ref, wkv_ref, sems) = refs[:-7], refs[-7:]
    chunks = len(far) // 4
    cut, half = far[0].shape
    rows = h_ref.shape[0]
    width = wkv_hbm.shape[2]
    starts = [pl.multiple_of((place_ref[0] ^ side) * half, half) for side in range(2)]
    pairs, tiles = [], []
    for code in range(4):
        for side in range(2):
            before = len(pairs)
            target = w_ref.at[code * 2 + side]
            if code < 2:
                pairs.append(((w0, w1)[code].at[:, pl.ds(starts[side], half)], target))
            else:
                for c in range(chunks):
                    source = far[((code - 2) * 2 + side) * chunks + c]
                    pairs.append((source, target.at[c * cut : (c + 1) * cut]))
            tiles.append((code, side, before, len(pairs)))
    pairs += [(wkv_hbm.at[c], wkv_ref.at[:, c * width : (c + 1) * width]) for c in range(2)]
    copies = start_copies(pairs, sems)
    for code, side, first, last in tiles:
        for copy in copies[first:last]:
            copy.wait()
        column = (place_ref[1] ^ code) * 2 * half + starts[side]
        emb_ref[:, pl.ds(pl.multiple_of(column, half), half)] = dot(
            h_ref[...], w_ref[code * 2 + side]
        ).astype(BF16)
    for copy in copies[-2:]:
        copy.wait()
    block = rows // 2
    for i in range(2):
        span = slice(i * block, (i + 1) * block)
        emb = emb_ref[span, :]
        factor = row_factor(emb.astype(F32))
        both = dot(emb, wkv_ref[...]) * factor
        kv_ref[0, span, :] = both[:, :width].astype(BF16)
        kv_ref[1, span, :] = both[:, width:].astype(BF16)
        factor_ref[span, :] = jnp.broadcast_to(factor, (block, HEAD))


def embed_rows(place, hidden, full, far, w_keyval):
    rows, depth = hidden.shape
    half = far[0].shape[1]
    wide = half * 8
    width = w_keyval.shape[2]
    return pl.pallas_call(
        embed_kernel,
        in_specs=[SMEM, VMEM] + [HBM] * (3 + len(far)),
        out_specs=[VMEM] * 3,
        out_shape=[
            jax.ShapeDtypeStruct((rows, wide), BF16),
            jax.ShapeDtypeStruct((2, rows, width), BF16),
            jax.ShapeDtypeStruct((rows, HEAD), F32),
        ],
        scratch_shapes=[
            pltpu.VMEM((8, depth, half), BF16),
            pltpu.VMEM((wide, 2 * width), BF16),
            pltpu.SemaphoreType.DMA((6 + len(far),)),
        ],
        compiler_params=pltpu.CompilerParams(vmem_limit_bytes=LIMIT),
        cost_estimate=pl.CostEstimate(
            flops=2 * rows * depth * wide, bytes_accessed=2 * depth * wide, transcendentals=0
        ),
        name="embed_rows",
    )(place, hidden, *full, *far, w_keyval)


def mixed_kernel(place_ref, emb_ref, t0, t1, t2, t3, wv_ref, ret_ref, *refs):
    weights, (value_ref, other_ref, own_ref, mixed_ref, w_ref, sems) = refs[:-6], refs[-6:]
    rows, wide = mixed_ref.shape
    strips, _, strip = w_ref.shape
    copies = []
    for j in range(strips):
        columns = slice(j * strip, (j + 1) * strip)
        pairs = []
        for i, weight in enumerate(weights):
            height = weight.shape[0]
            if i < 2:
                top = i * height
            else:
                code, side, cut = 2 + (i - 2) // 4, (i - 2) // 2 % 2, (i - 2) % 2
                top = (code * 2 + (place_ref[0] ^ side)) * 2 * height + cut * height
                top = pl.multiple_of(top, height)
            pairs.append((weight.at[:, columns], w_ref.at[j, pl.ds(top, height)]))
        copies.append(start_copies(pairs, sems.at[j]))
    for j in range(strips):
        for copy in copies[j]:
            copy.wait()
        columns = slice(j * strip, (j + 1) * strip)
        parts = jnp.concatenate([t0[...], t1[...], t2[...], t3[...]], axis=1)
        mixed_ref[:, columns] = emb_ref[:, columns].astype(F32) + dot(parts, w_ref[j])

    half = wide // 2
    block = 32
    live_total = place_ref[4].astype(F32)

    @pl.loop(0, rows // block)
    def _(i):
        start = pl.multiple_of(i * block, block)
        span = pl.ds(start, block)
        mixed = mixed_ref[span, :]
        factor = row_factor(mixed)
        value = factor * jnp.sum(mixed * wv_ref[...].astype(F32), axis=-1, keepdims=True)
        row = place_ref[2] + start + lax.broadcasted_iota(jnp.int32, (block, 1), 0)
        gap = jnp.where(row < place_ref[3], value - ret_ref[span, :], F32(0.0)) / live_total
        lead = factor * gap
        pull = lead * factor * value / wide
        value_ref[span, :] = jnp.broadcast_to(value, (block, HEAD))
        for out, side in ((own_ref, place_ref[0]), (other_ref, 1 - place_ref[0])):
            columns = pl.ds(pl.multiple_of(side * half, half), half)
            part = mixed_ref[span, columns]
            out[span, :] = (lead * wv_ref[:, columns].astype(F32) - part * pull).astype(BF16)


def mixed_rows(place, embedded, parts, weights, w_value, returns):
    rows, wide = embedded.shape
    depth = sum(weight.shape[0] for weight in weights)
    return pl.pallas_call(
        mixed_kernel,
        in_specs=[SMEM] + [VMEM] * 7 + [HBM] * len(weights),
        out_specs=[VMEM] * 3,
        out_shape=[
            jax.ShapeDtypeStruct((rows, HEAD), F32),
            jax.ShapeDtypeStruct((rows, wide // 2), BF16),
            jax.ShapeDtypeStruct((rows, wide // 2), BF16),
        ],
        scratch_shapes=[
            pltpu.VMEM((rows, wide), F32),
            pltpu.VMEM((8, depth, wide // 8), BF16),
            pltpu.SemaphoreType.DMA((8, len(weights))),
        ],
        compiler_params=pltpu.CompilerParams(vmem_limit_bytes=LIMIT),
        cost_estimate=pl.CostEstimate(
            flops=2 * rows * wide * depth, bytes_accessed=2 * wide * depth, transcendentals=0
        ),
        name="mixed_rows",
    )(
        place, embedded, *parts, w_value.reshape(1, wide), returns.reshape(rows, 1), *weights
    )


def gather_codes(size):
    codes, bit = [0], size // 2
    while bit >= 1:
        codes = codes + [code ^ bit for code in codes]
        bit //= 2
    return codes


def split_kernel(codes, index_ref, own_ref, got_ref, keep_ref, send_ref):
    block = own_ref.shape[0] // len(codes)
    side = len(codes) // 2
    for k, code in enumerate(codes):
        span = pl.ds(pl.multiple_of((index_ref[0] ^ code) * block, block), block)
        out = (keep_ref, send_ref)[k // side]
        at = k % side * block
        total = own_ref[span, :] + got_ref[span, :].astype(F32)
        out[at : at + block, :] = total.astype(out.dtype)


def split_sum(index, own, got, count):
    rows, wide = own.shape
    if (rows // count) % 16:
        got = got.astype(F32)
    return pl.pallas_call(
        functools.partial(split_kernel, gather_codes(count)),
        in_specs=[SMEM, VMEM, VMEM],
        out_specs=[VMEM] * 2,
        out_shape=[
            jax.ShapeDtypeStruct((rows // 2, wide), F32),
            jax.ShapeDtypeStruct((rows // 2, wide), got.dtype),
        ],
        compiler_params=pltpu.CompilerParams(vmem_limit_bytes=LIMIT),
        cost_estimate=pl.CostEstimate(
            flops=rows * wide, bytes_accessed=8 * rows * wide, transcendentals=0
        ),
        name="split_sum",
    )(index, own, got)


def assemble_kernel(codes, chunks, place_ref, *refs):
    parts = refs[: len(codes) * 2 * chunks]
    out, got_ref, wide_ref, got_sems, sems = refs[len(parts) :]
    block, strip = parts[0].shape
    got = start_copies([(part, got_ref.at[i]) for i, part in enumerate(parts)], got_sems)
    copies = []
    for c in range(chunks):
        for side in range(2):
            for k, code in enumerate(codes):
                at = (c * 2 + side) * len(codes) + k
                row = pl.multiple_of((place_ref[5] ^ code) * block, block)
                column = pl.multiple_of(((place_ref[0] ^ side) * chunks + c) * strip, strip)
                got[at].wait()
                wide_ref[at] = got_ref[at].astype(F32)
                copy = pltpu.make_async_copy(
                    wide_ref.at[at],
                    out.at[pl.ds(row, block), pl.ds(column, strip)],
                    sems.at[at],
                )
                copy.start()
                copies.append(copy)
    for copy in copies:
        copy.wait()


def assemble(place, parts, count, chunks):
    block, strip = parts[0].shape
    rows, wide = block * count, strip * 2 * chunks
    return pl.pallas_call(
        functools.partial(assemble_kernel, gather_codes(count), chunks),
        in_specs=[SMEM] + [HBM] * len(parts),
        out_specs=pl.BlockSpec(memory_space=pl.ANY),
        out_shape=jax.ShapeDtypeStruct((rows, wide), F32),
        scratch_shapes=[
            pltpu.VMEM((len(parts), block, strip), BF16),
            pltpu.VMEM((len(parts), block, strip), F32),
            pltpu.SemaphoreType.DMA((len(parts),)),
            pltpu.SemaphoreType.DMA((len(parts),)),
        ],
        compiler_params=pltpu.CompilerParams(vmem_limit_bytes=LIMIT),
        cost_estimate=pl.CostEstimate(
            flops=rows * wide, bytes_accessed=6 * rows * wide, transcendentals=0
        ),
        name="assemble",
    )(place, *parts)


def swap(block, axis, bit):
    size = lax.axis_size(axis)
    return lax.ppermute(block, axis, [(i, i ^ bit) for i in range(size)])


def gather_blocks(block, axis):
    blocks, bit = [block], lax.axis_size(axis) // 2
    while bit >= 1:
        blocks = blocks + [swap(item, axis, bit) for item in blocks]
        bit //= 2
    return blocks


def gather_parts(part):
    far = swap(part, "mdl", 2)
    return [part, swap(part, "mdl", 1), far, swap(far, "mdl", 1)], far


def product(left, right):
    return jnp.einsum("rh,rd->hd", left, right, preferred_element_type=F32)


def halve(keep, got):
    total = keep + got.astype(F32)
    side = total.shape[0] // 2
    return total[:side], total[side:].astype(BF16)


def half_of(weight, side):
    half = weight.shape[1] // 2
    return lax.dynamic_slice_in_dim(weight, side * half, half, 1)


def on_device(
    obs,
    a_query,
    a_keyval,
    a_out,
    w_policy,
    c_in,
    c_query,
    c_keyval,
    c_out,
    w_value,
    actions,
    advantages,
    old_logp,
    returns,
    robot_count,
):
    row_count = obs.shape[1]
    batch_index = lax.axis_index("sec")
    rep_index = lax.axis_index("rep")
    rep_count = lax.axis_size("rep")
    robot_total = robot_count[batch_index]
    live_sum = jnp.sum(robot_count)
    live_total = live_sum.astype(F32)
    first_row = rep_index * row_count
    live_mask = first_row + lax.iota(jnp.int32, row_count) < robot_total
    mdl_count = lax.axis_size("mdl")
    assert mdl_count == 4 and lax.axis_size("sec") == 2
    mdl_index = lax.axis_index("mdl")
    part_rows = row_count // mdl_count
    row_start = mdl_index * part_rows
    score_scale = HEAD ** (-0.5) * LOG2E
    rep_place = rep_index.reshape(1).astype(jnp.int32)

    place = jnp.stack(
        [batch_index, mdl_index, first_row, robot_total, live_sum, rep_index]
        + [
            jnp.clip(robot_total - (rep_index ^ code) * row_count, 0, row_count)
            for code in gather_codes(rep_count)
        ]
    ).astype(jnp.int32)

    obs_in = obs[0]
    keyval, factor_a = first_projection(obs_in, a_keyval)
    pieces_k = gather_blocks(keyval, "rep")

    a_near = swap(a_out, "mdl", 1)
    c_near = swap(c_in, "mdl", 1)
    a_far0 = swap(half_of(a_out, batch_index), "mdl", 2)
    c_half = half_of(c_in, batch_index)
    c_cut = c_half.shape[0] // 2
    c_a0 = swap(c_half[:c_cut], "mdl", 2)
    c_b0 = swap(c_half[c_cut:], "mdl", 2)

    queries = (dot(obs_in, a_query) * (factor_a[:, :1] * score_scale)).astype(BF16)
    queries, a_far0 = tied(queries, a_far0)
    a_far1 = swap(a_far0, "sec", 1)
    state = attend_call(queries, pieces_k[:-1], 0, place, [])
    *state, c_a0 = tied(*state, c_a0)
    c_a1 = swap(c_a0, "sec", 1)
    *state, c_b0, a_far1 = tied(*state, c_b0, a_far1)
    c_b1 = swap(c_b0, "sec", 1)
    attended = attend_call(queries, pieces_k[-1:], rep_count - 1, place, state)
    attended_far = swap(attended, "mdl", 2)
    attended, attended_far, c_a1 = tied(attended, attended_far, c_a1)
    attended_near = swap(attended, "mdl", 1)
    attended_parts = [attended, attended_near, attended_far, swap(attended_far, "mdl", 1)]
    a_halves = [a_far0, a_far1, swap(a_far0, "mdl", 1), swap(a_far1, "mdl", 1)]
    hidden = hidden_rows(place, obs_in, attended_parts, [a_out, a_near], a_halves)
    c_far = [c_a0, c_b0, c_a1, c_b1]
    c_far = c_far + [swap(item, "mdl", 1) for item in c_far]

    out_half = c_out.shape[0] // 2
    out_cut = out_half // 2
    out_src = lax.dynamic_slice_in_dim(c_out, batch_index * out_half, out_half, 0)
    attended_far, out_src = tied(attended_far, out_src)
    out_a0 = swap(out_src[:out_cut], "mdl", 2)
    out_b0 = swap(out_src[out_cut:], "mdl", 2)

    embedded, critic_keyval, factor_c = embed_rows(place, hidden, [c_in, c_near], c_far, c_keyval)
    pieces_c = gather_blocks(critic_keyval, "rep")
    critic_queries = (dot(embedded, c_query) * (factor_c[:, :1] * score_scale)).astype(BF16)

    late_hidden, critic_keyval = tied(hidden, critic_keyval)
    source = late_hidden.astype(F32)
    factor_h = row_factor(source)
    logits = dot(late_hidden, w_policy) * factor_h
    log_probs = jax.nn.log_softmax(logits, axis=-1)
    onehot = (
        actions[0][:, None] == lax.broadcasted_iota(jnp.int32, logits.shape, 1)
    ).astype(F32)
    chosen = jnp.sum(onehot * log_probs, axis=-1)
    prob_ratio = jnp.exp(chosen - old_logp[0])
    plain_term = prob_ratio * advantages[0]
    bounded = jnp.clip(prob_ratio, 1.0 - clip_range, 1.0 + clip_range) * advantages[0]
    slope = jnp.where(live_mask & (plain_term <= bounded), -plain_term / live_total, F32(0.0))
    dlogits = slope[:, None] * (onehot - jnp.exp(log_probs))
    along = jnp.sum(dlogits * logits, axis=-1, keepdims=True) / source.shape[1]
    dnormed = dot(dlogits.astype(BF16), w_policy.T)
    dhidden = (factor_h * (dnormed - source * (factor_h * along))).astype(BF16)
    half_a = dhidden.shape[1] // 2
    got_a = swap(
        product(attended, lax.dynamic_slice_in_dim(dhidden, (1 - batch_index) * half_a, half_a, 1))
        .astype(BF16),
        "sec",
        1,
    )
    own_a = product(attended, lax.dynamic_slice_in_dim(dhidden, batch_index * half_a, half_a, 1))

    critic_queries, out_a0 = tied(critic_queries, out_a0)
    out_a1 = swap(out_a0, "sec", 1)
    state_c = attend_call(critic_queries, pieces_c[:-1], 0, place, [])
    *state_c, got_a, pieces_c[-1], out_b0 = tied(*state_c, got_a, pieces_c[-1], out_b0)
    out_b1 = swap(out_b0, "sec", 1)
    keep_a, send_a = split_sum(rep_place, own_a, got_a, rep_count)
    moved_a = swap(send_a.astype(BF16), "rep", 1)
    critic_attended = attend_call(critic_queries, pieces_c[-1:], rep_count - 1, place, state_c)
    critic_attended, moved_a = tied(critic_attended, moved_a)
    critic_far = swap(critic_attended, "mdl", 2)
    critic_near = swap(critic_attended, "mdl", 1)
    bit = 2
    while bit < rep_count:
        keep_a, send_a = halve(keep_a, moved_a)
        moved_a = swap(send_a, "rep", bit)
        bit *= 2
    critic_near, out_a1, moved_a = tied(critic_near, out_a1, moved_a)
    mine_a = gather_blocks((keep_a + moved_a.astype(F32)).astype(BF16), "rep")
    critic_parts = [critic_attended, critic_near, critic_far, swap(critic_far, "mdl", 1)]
    out_far = [out_a0, out_b0, out_a1, out_b1]
    c_out_all = [c_out, swap(c_out, "mdl", 1)] + out_far
    c_out_all += [swap(item, "mdl", 1) for item in out_far]
    value_wide, d_other, d_own = mixed_rows(
        place, embedded, critic_parts, c_out_all, w_value, returns[0]
    )
    theirs_a = [swap(block, "sec", 1) for block in mine_a]
    d_other, *theirs_a[:-1] = tied(d_other, *theirs_a[:-1])
    pieces_a = mine_a + theirs_a

    strip = d_own.shape[1] // CHUNKS
    spans = [slice(c * strip, (c + 1) * strip) for c in range(CHUNKS)]
    got = [
        swap(product(critic_attended, d_other[:, span]).astype(BF16), "sec", 1) for span in spans
    ]
    own = [product(critic_attended, d_own[:, span]) for span in spans]
    value_part = lax.dynamic_slice_in_dim(value_wide, row_start, part_rows, 0)[:, 0]
    got[0], value_part = tied(got[0], value_part)
    actor_summed = assemble(place, pieces_a, rep_count, 1)
    got[1], actor_summed = tied(got[1], actor_summed)
    pieces, marks = [], []
    for c in range(CHUNKS):
        arrived = got[c]
        if c > 0:
            arrived, _ = tied(arrived, marks[0])
        keep, send = split_sum(rep_place, own[c], arrived, rep_count)
        bit, trail = 1, []
        while bit < rep_count:
            arrived = swap(send.astype(BF16), "rep", bit)
            bit *= 2
            if c > 0:
                arrived, _ = tied(arrived, marks[min(len(trail) + 1, len(marks) - 1)])
            if bit < rep_count:
                keep, send = halve(keep, arrived)
                trail.append(keep)
        total = (keep + arrived.astype(F32)).astype(BF16)
        trail.append(total)
        mine = gather_blocks(total, "rep")
        trail.append(mine[1])
        marks = trail
        pieces += mine + [swap(block, "sec", 1) for block in mine]
    critic_summed = assemble(place, pieces, rep_count, CHUNKS)

    return (value_part[None, :], actor_summed, critic_summed)


def solution(mesh):
    return jax.shard_map(
        on_device,
        mesh=mesh,
        in_specs=(
            P("sec", "rep", None),
            P(None, "mdl"),
            P(None, None, "mdl"),
            P("mdl", None),
            P(),
            P(None, "mdl"),
            P(None, "mdl"),
            P(None, None, "mdl"),
            P("mdl", None),
            P(),
            P("sec", "rep"),
            P("sec", "rep"),
            P("sec", "rep"),
            P("sec", "rep"),
            P(),
        ),
        out_specs=(P("sec", ("rep", "mdl")), P("mdl", None), P("mdl", None)),
        check_vma=False,
    )
```

```python
import functools
import math

import jax
import jax.numpy as jnp
from jax import lax
from jax.experimental import pallas as pl
from jax.experimental.pallas import tpu as pltpu
from jax.sharding import PartitionSpec as P

HEAD = 128
epsilon = 1e-05
clip_range = 0.2
masked_score = -1e30
LOG2E = 1.4426950408889634
F32 = jnp.float32
BF16 = jnp.bfloat16
CHUNKS = 2
TABLE = 6
LIMIT = 40 * 2**20
VMEM = pl.BlockSpec(memory_space=pltpu.VMEM)
SMEM = pl.BlockSpec(memory_space=pltpu.SMEM)
ANY = pl.BlockSpec(memory_space=pl.ANY)


def dot(a, b):
    return jnp.dot(a, b, preferred_element_type=F32)


def tied(*items):
    return lax.optimization_barrier(items)


def row_factor(source):
    return lax.rsqrt(jnp.mean(source * source, axis=-1, keepdims=True) + epsilon)


def start_copies(pairs, sems):
    copies = [
        pltpu.make_async_copy(source, target, sems.at[i])
        for i, (source, target) in enumerate(pairs)
    ]
    for copy in copies:
        copy.start()
    return copies


def first_kernel(obs_hbm, w_hbm, kv_ref, factor_ref, obs_ref, w_ref, sems):
    rows, depth = obs_ref.shape
    width = w_hbm.shape[2]
    block = rows // 2
    spans = [slice(i * block, (i + 1) * block) for i in range(2)]
    copies = start_copies(
        [(w_hbm.at[c], w_ref.at[:, c * width : (c + 1) * width]) for c in range(2)]
        + [(obs_hbm.at[span], obs_ref.at[span]) for span in spans],
        sems,
    )
    for i, span in enumerate(spans):
        copies[2 + i].wait()
        part = obs_ref[span, :]
        factor = row_factor(part.astype(F32))
        if i == 0:
            copies[0].wait()
            copies[1].wait()
        both = dot(part, w_ref[...]) * factor
        kv_ref[0, span, :] = both[:, :width].astype(BF16)
        kv_ref[1, span, :] = both[:, width:].astype(BF16)
        factor_ref[span, :] = jnp.broadcast_to(factor, (block, HEAD))


def first_projection(obs, w_keyval):
    rows, depth = obs.shape
    width = w_keyval.shape[2]
    return pl.pallas_call(
        first_kernel,
        in_specs=[ANY] * 2,
        out_specs=[VMEM] * 2,
        out_shape=[
            jax.ShapeDtypeStruct((2, rows, width), BF16),
            jax.ShapeDtypeStruct((rows, HEAD), F32),
        ],
        scratch_shapes=[
            pltpu.VMEM((rows, depth), BF16),
            pltpu.VMEM((depth, 2 * width), BF16),
            pltpu.SemaphoreType.DMA((4,)),
        ],
        compiler_params=pltpu.CompilerParams(vmem_limit_bytes=LIMIT),
        cost_estimate=pl.CostEstimate(
            flops=4 * rows * depth * width, bytes_accessed=2 * rows * depth, transcendentals=0
        ),
        name="first_projection",
    )(obs, w_keyval)


def attend_blocks(groups, units, first, left_ref, q_ref, kv_refs):
    def fetch(head, span):
        kv_head = head // groups
        columns = slice(kv_head * HEAD, (kv_head + 1) * HEAD)
        query = q_ref[span, head * HEAD : (head + 1) * HEAD]
        lane = lax.broadcasted_iota(jnp.int32, query.shape, 1)
        query = jnp.concatenate([query, (lane == 0).astype(BF16)], axis=1)
        scores = []
        for p, ref in enumerate(kv_refs):
            keys = ref[0, :, columns]
            key = lax.broadcasted_iota(jnp.int32, keys.shape, 0)
            lane = lax.broadcasted_iota(jnp.int32, keys.shape, 1)
            dead = (key >= left_ref[first + p]) & (lane == 0)
            bias = jnp.where(dead, F32(masked_score), F32(0.0)).astype(BF16)
            keys = jnp.concatenate([keys, bias], axis=1)
            scores.append(
                lax.dot_general(
                    query, keys, (((1,), (1,)), ((), ())), preferred_element_type=F32
                )
            )
        return scores

    def values(head, p):
        kv_head = head // groups
        vals = kv_refs[p][1, :, kv_head * HEAD : (kv_head + 1) * HEAD]
        return jnp.concatenate([vals, jnp.ones_like(vals)], axis=1)

    ahead = fetch(*units[0])
    for i, (head, span) in enumerate(units):
        scores = ahead
        if i + 1 < len(units):
            ahead = fetch(*units[i + 1])
        yield head, span, scores, functools.partial(values, head)


def weigh(scores, top, values):
    total = None
    for p, part in enumerate(scores):
        both = dot(jnp.exp2(part - top).astype(BF16), values(p))
        total = both if total is None else total + both
    return total


def highest(scores):
    return functools.reduce(
        jnp.maximum, [jnp.max(part, axis=-1, keepdims=True) for part in scores]
    )


def open_kernel(groups, units, first, left_ref, q_ref, *refs):
    *kv_refs, wide_ref, top_ref = refs
    for head, span, scores, values in attend_blocks(
        groups, units, first, left_ref, q_ref, kv_refs
    ):
        top = highest(scores)
        wide_ref[span, head * 2 * HEAD : (head + 1) * 2 * HEAD] = weigh(scores, top, values)
        top_ref[span, head * HEAD : (head + 1) * HEAD] = jnp.broadcast_to(
            top, (top.shape[0], HEAD)
        )


def close_kernel(groups, units, first, left_ref, q_ref, wide_ref, top_ref, *refs):
    *kv_refs, o_ref = refs
    for head, span, scores, values in attend_blocks(
        groups, units, first, left_ref, q_ref, kv_refs
    ):
        before = top_ref[span, head * HEAD : head * HEAD + 1]
        top = jnp.maximum(before, highest(scores))
        wide = wide_ref[span, head * 2 * HEAD : (head + 1) * 2 * HEAD]
        wide = wide * jnp.exp2(before - top) + weigh(scores, top, values)
        o_ref[span, head * HEAD : (head + 1) * HEAD] = (
            wide[:, :HEAD] / wide[:, HEAD:]
        ).astype(BF16)


def attend_call(queries, pieces, first, place, state):
    rows, width = queries.shape
    heads = width // HEAD
    groups = heads // (pieces[0].shape[2] // HEAD)
    block = min(rows, 256)
    units = [
        (head, slice(i, i + block)) for head in range(heads) for i in range(0, rows, block)
    ]
    count = len(pieces) * pieces[0].shape[1]
    weight = 1 if state else 24
    if state:
        body, name = close_kernel, "attend_close"
        out = jax.ShapeDtypeStruct((rows, width), BF16)
    else:
        body, name = open_kernel, "attend_open"
        out = [
            jax.ShapeDtypeStruct((rows, 2 * width), F32),
            jax.ShapeDtypeStruct((rows, width), F32),
        ]
    return pl.pallas_call(
        functools.partial(body, groups, units, TABLE + first),
        in_specs=[SMEM] + [VMEM] * (1 + len(state) + len(pieces)),
        out_specs=VMEM if state else [VMEM] * 2,
        out_shape=out,
        compiler_params=pltpu.CompilerParams(vmem_limit_bytes=LIMIT),
        cost_estimate=pl.CostEstimate(
            flops=weight * rows * count * width,
            bytes_accessed=4 * rows * width,
            transcendentals=rows * count,
        ),
        name=name,
    )(place, queries, *state, *pieces)


def hidden_kernel(
    obs_any, t0, t1, t2, t3, w0, w1, w2, w3, c_any, o_ref, emb_ref, obs_ref, w_ref, c_ref, sum_ref, sems
):
    inner, depth = w0.shape
    tile = depth // 3
    pairs = [(obs_any, obs_ref)]
    pairs += [
        (w, w_ref.at[k * inner : (k + 1) * inner]) for k, w in enumerate((w0, w1, w2, w3))
    ]
    copies = start_copies(pairs + [(c_any, c_ref)], sems)
    for copy in copies[:3]:
        copy.wait()
    tiles = [slice(i * tile, (i + 1) * tile) for i in range(3)]
    for strip in tiles:
        parts = jnp.concatenate([t0[...], t1[...]], axis=1)
        sum_ref[:, strip] = obs_ref[:, strip].astype(F32) + dot(parts, w_ref[: 2 * inner, strip])
    for copy in copies[3:5]:
        copy.wait()
    for strip in tiles:
        parts = jnp.concatenate([t2[...], t3[...]], axis=1)
        total = sum_ref[:, strip] + dot(parts, w_ref[2 * inner :, strip])
        o_ref[:, strip] = total.astype(BF16)
    copies[5].wait()
    emb_ref[...] = dot(o_ref[...], c_ref[...]).astype(BF16)


def hidden_rows(obs, parts, weights, c_in):
    rows, depth = obs.shape
    inner = weights[0].shape[0]
    width = c_in.shape[1]
    return pl.pallas_call(
        hidden_kernel,
        in_specs=[ANY] + [VMEM] * 4 + [ANY] * 5,
        out_specs=[VMEM] * 2,
        out_shape=[
            jax.ShapeDtypeStruct((rows, depth), BF16),
            jax.ShapeDtypeStruct((rows, width), BF16),
        ],
        scratch_shapes=[
            pltpu.VMEM((rows, depth), BF16),
            pltpu.VMEM((4 * inner, depth), BF16),
            pltpu.VMEM((depth, width), BF16),
            pltpu.VMEM((rows, depth), F32),
            pltpu.SemaphoreType.DMA((6,)),
        ],
        compiler_params=pltpu.CompilerParams(vmem_limit_bytes=LIMIT),
        cost_estimate=pl.CostEstimate(
            flops=8 * rows * depth * inner, bytes_accessed=8 * depth * inner, transcendentals=0
        ),
        name="hidden_rows",
    )(obs, *parts, *weights, c_in)


def join_kernel(place_ref, e0, e1, e2, e3, wkv_any, kv_ref, factor_ref, emb_ref, wkv_ref, sems):
    rows, wide = emb_ref.shape
    width = wkv_any.shape[2]
    strip = e0.shape[1]
    copies = start_copies(
        [(wkv_any.at[c], wkv_ref.at[:, c * width : (c + 1) * width]) for c in range(2)], sems
    )
    starts = [pl.multiple_of((place_ref[1] ^ code) * strip, strip) for code in range(4)]
    parts = (e0, e1, e2, e3)
    for copy in copies:
        copy.wait()
    block = rows // 2
    for i in range(2):
        span = slice(i * block, (i + 1) * block)
        square, both = 0.0, 0.0
        for part, start in zip(parts, starts):
            emb = part[span, :]
            wide_emb = emb.astype(F32)
            square = square + jnp.sum(wide_emb * wide_emb, axis=-1, keepdims=True)
            both = both + dot(emb, wkv_ref[pl.ds(start, strip), :])
            emb_ref[span, pl.ds(start, strip)] = emb
        factor = lax.rsqrt(square / wide + epsilon)
        both = both * factor
        kv_ref[0, span, :] = both[:, :width].astype(BF16)
        kv_ref[1, span, :] = both[:, width:].astype(BF16)
        factor_ref[span, :] = jnp.broadcast_to(factor, (block, HEAD))


def join_rows(place, parts, w_keyval):
    rows, strip = parts[0].shape
    wide = 4 * strip
    width = w_keyval.shape[2]
    return pl.pallas_call(
        join_kernel,
        in_specs=[SMEM] + [VMEM] * 4 + [ANY],
        out_specs=[VMEM] * 3,
        out_shape=[
            jax.ShapeDtypeStruct((2, rows, width), BF16),
            jax.ShapeDtypeStruct((rows, HEAD), F32),
            jax.ShapeDtypeStruct((rows, wide), BF16),
        ],
        scratch_shapes=[pltpu.VMEM((wide, 2 * width), BF16), pltpu.SemaphoreType.DMA((2,))],
        compiler_params=pltpu.CompilerParams(vmem_limit_bytes=LIMIT),
        cost_estimate=pl.CostEstimate(
            flops=4 * rows * wide * width, bytes_accessed=4 * rows * wide, transcendentals=0
        ),
        name="join_rows",
    )(place, *parts, w_keyval)


def part_kernel(
    place_ref, att_ref, c_any, send_ref, keep_ref, their_ref, my_ref, c_ref, sems
):
    rows, inner = att_ref.shape
    wide = c_ref.shape[1]
    block = rows // 4
    half = inner // 2
    core = place_ref[1] % 2
    copies = start_copies(
        [
            (c_any.at[i * half : (i + 1) * half], c_ref.at[i * half : (i + 1) * half])
            for i in range(2)
        ],
        sems,
    )
    for out, side in ((their_ref, 1 - core), (my_ref, core)):
        for i in range(2):
            span = pl.ds(pl.multiple_of((side + 2 * i) * block, block), block)
            out[i * block : (i + 1) * block, :] = att_ref[span, :]
    for copy in copies:
        copy.wait()
    tile = 512
    for out, source in ((send_ref, their_ref), (keep_ref, my_ref)):
        for j in range(wide // tile):
            columns = slice(j * tile, (j + 1) * tile)
            out[:, columns] = dot(source[...], c_ref[:, columns]).astype(out.dtype)


def part_rows(place, attended, c_out):
    rows, inner = attended.shape
    wide = c_out.shape[1]
    return pl.pallas_call(
        part_kernel,
        in_specs=[SMEM, VMEM, ANY],
        out_specs=[VMEM] * 4,
        out_shape=[
            jax.ShapeDtypeStruct((rows // 2, wide), BF16),
            jax.ShapeDtypeStruct((rows // 2, wide), F32),
            jax.ShapeDtypeStruct((rows // 2, inner), BF16),
            jax.ShapeDtypeStruct((rows // 2, inner), BF16),
        ],
        scratch_shapes=[pltpu.VMEM((inner, wide), BF16), pltpu.SemaphoreType.DMA((2,))],
        compiler_params=pltpu.CompilerParams(vmem_limit_bytes=LIMIT),
        cost_estimate=pl.CostEstimate(
            flops=2 * rows * wide * inner, bytes_accessed=8 * wide * inner, transcendentals=0
        ),
        name="part_rows",
    )(place, attended, c_out)


def mixed_kernel(
    place_ref, emb_ref, mine_ref, got_ref, wv_ref, ret_ref, value_ref, other_ref, own_ref, mixed_ref
):
    rows, wide = mine_ref.shape
    half = wide // 2
    piece = rows // 2
    block = 32
    core = place_ref[1] % 2
    live_total = place_ref[4].astype(F32)

    @pl.loop(0, rows // block)
    def _(i):
        start = pl.multiple_of(i * block, block)
        span = pl.ds(start, block)
        place = (core + start // piece * 2) * piece + start % piece
        there = pl.ds(pl.multiple_of(place, block), block)
        mixed = (
            emb_ref[there, :].astype(F32)
            + mine_ref[span, :].astype(F32)
            + got_ref[span, :].astype(F32)
        )
        mixed_ref[...] = mixed
        factor = row_factor(mixed)
        value = factor * jnp.sum(mixed * wv_ref[...].astype(F32), axis=-1, keepdims=True)
        row = place_ref[2] + place + lax.broadcasted_iota(jnp.int32, (block, 1), 0)
        gap = jnp.where(row < place_ref[3], value - ret_ref[there, :], F32(0.0)) / live_total
        lead = factor * gap
        pull = lead * factor * value / wide
        value_ref[span, :] = jnp.broadcast_to(value, (block, HEAD))
        for out, side in ((own_ref, place_ref[0]), (other_ref, 1 - place_ref[0])):
            columns = pl.ds(pl.multiple_of(side * half, half), half)
            part = mixed_ref[:, columns]
            out[span, :] = (lead * wv_ref[:, columns].astype(F32) - part * pull).astype(BF16)


def mixed_rows(place, embedded, mine, got, w_value, returns):
    rows, wide = mine.shape
    return pl.pallas_call(
        mixed_kernel,
        in_specs=[SMEM] + [VMEM] * 5,
        out_specs=[VMEM] * 3,
        out_shape=[
            jax.ShapeDtypeStruct((rows, HEAD), F32),
            jax.ShapeDtypeStruct((rows, wide // 2), BF16),
            jax.ShapeDtypeStruct((rows, wide // 2), BF16),
        ],
        scratch_shapes=[pltpu.VMEM((32, wide), F32)],
        compiler_params=pltpu.CompilerParams(vmem_limit_bytes=LIMIT),
        cost_estimate=pl.CostEstimate(
            flops=10 * rows * wide, bytes_accessed=12 * rows * wide, transcendentals=0
        ),
        name="mixed_rows",
    )(place, embedded, mine, got, w_value.reshape(1, wide), returns.reshape(-1, 1))


def gather_codes(size):
    codes, bit = [0], size // 2
    while bit >= 1:
        codes = codes + [code ^ bit for code in codes]
        bit //= 2
    return codes


def split_kernel(codes, index_ref, own_ref, got_ref, keep_ref, send_ref):
    block = own_ref.shape[0] // len(codes)
    side = len(codes) // 2
    for k, code in enumerate(codes):
        span = pl.ds(pl.multiple_of((index_ref[0] ^ code) * block, block), block)
        out = (keep_ref, send_ref)[k // side]
        at = k % side * block
        total = own_ref[span, :] + got_ref[span, :].astype(F32)
        out[at : at + block, :] = total.astype(out.dtype)


def split_sum(index, own, got, count):
    rows, wide = own.shape
    if (rows // count) % 16:
        got = got.astype(F32)
    return pl.pallas_call(
        functools.partial(split_kernel, gather_codes(count)),
        in_specs=[SMEM, VMEM, VMEM],
        out_specs=[VMEM] * 2,
        out_shape=[
            jax.ShapeDtypeStruct((rows // 2, wide), F32),
            jax.ShapeDtypeStruct((rows // 2, wide), got.dtype),
        ],
        compiler_params=pltpu.CompilerParams(vmem_limit_bytes=LIMIT),
        cost_estimate=pl.CostEstimate(
            flops=rows * wide, bytes_accessed=8 * rows * wide, transcendentals=0
        ),
        name="split_sum",
    )(index, own, got)


def assemble_kernel(codes, chunk, chunks, place_ref, *refs):
    parts = refs[: len(codes) * 2]
    out, got_ref, wide_ref, got_sems, sems = refs[-5:]
    block, strip = parts[0].shape
    got = start_copies([(part, got_ref.at[i]) for i, part in enumerate(parts)], got_sems)
    copies = []
    for side in range(2):
        for k, code in enumerate(codes):
            at = side * len(codes) + k
            row = pl.multiple_of((place_ref[5] ^ code) * block, block)
            column = pl.multiple_of(((place_ref[0] ^ side) * chunks + chunk) * strip, strip)
            got[at].wait()
            wide_ref[at] = got_ref[at].astype(F32)
            copy = pltpu.make_async_copy(
                wide_ref.at[at],
                out.at[pl.ds(row, block), pl.ds(column, strip)],
                sems.at[at],
            )
            copy.start()
            copies.append(copy)
    for copy in copies:
        copy.wait()


def assemble(place, parts, count, chunk, chunks, before):
    block, strip = parts[0].shape
    rows, wide = block * count, strip * 2 * chunks
    return pl.pallas_call(
        functools.partial(assemble_kernel, gather_codes(count), chunk, chunks),
        in_specs=[SMEM] + [ANY] * (len(parts) + len(before)),
        out_specs=ANY,
        out_shape=jax.ShapeDtypeStruct((rows, wide), F32),
        input_output_aliases={1 + len(parts): 0} if before else {},
        scratch_shapes=[
            pltpu.VMEM((len(parts), block, strip), BF16),
            pltpu.VMEM((len(parts), block, strip), F32),
            pltpu.SemaphoreType.DMA((len(parts),)),
            pltpu.SemaphoreType.DMA((len(parts),)),
        ],
        compiler_params=pltpu.CompilerParams(vmem_limit_bytes=LIMIT),
        cost_estimate=pl.CostEstimate(
            flops=rows * wide, bytes_accessed=6 * rows * wide, transcendentals=0
        ),
        name="assemble",
    )(place, *parts, *before)


def swap(block, axis, bit):
    size = lax.axis_size(axis)
    return lax.ppermute(block, axis, [(i, i ^ bit) for i in range(size)])


def gather_blocks(block, axis):
    blocks, bit = [block], lax.axis_size(axis) // 2
    while bit >= 1:
        blocks = blocks + [swap(item, axis, bit) for item in blocks]
        bit //= 2
    return blocks


def gather_parts(part):
    far = swap(part, "mdl", 2)
    return [part, swap(part, "mdl", 1), far, swap(far, "mdl", 1)], far


def product(left, right):
    return jnp.einsum("rh,rd->hd", left, right, preferred_element_type=F32)


def halve(keep, got):
    total = keep + got.astype(F32)
    side = total.shape[0] // 2
    return total[:side], total[side:].astype(BF16)


def on_device(
    obs,
    a_query,
    a_keyval,
    a_out,
    w_policy,
    c_in,
    c_query,
    c_keyval,
    c_out,
    w_value,
    actions,
    advantages,
    old_logp,
    returns,
    robot_count,
):
    row_count = obs.shape[1]
    batch_index = lax.axis_index("sec")
    rep_index = lax.axis_index("rep")
    rep_count = lax.axis_size("rep")
    robot_total = robot_count[batch_index]
    live_sum = jnp.sum(robot_count)
    live_total = live_sum.astype(F32)
    first_row = rep_index * row_count
    live_mask = first_row + lax.iota(jnp.int32, row_count) < robot_total
    mdl_count = lax.axis_size("mdl")
    assert mdl_count == 4 and lax.axis_size("sec") == 2
    mdl_index = lax.axis_index("mdl")
    value_rows = row_count // mdl_count
    score_scale = HEAD ** (-0.5) * LOG2E
    rep_place = rep_index.reshape(1).astype(jnp.int32)

    place = jnp.stack(
        [batch_index, mdl_index, first_row, robot_total, live_sum, rep_index]
        + [
            jnp.clip(robot_total - (rep_index ^ code) * row_count, 0, row_count)
            for code in gather_codes(rep_count)
        ]
    ).astype(jnp.int32)

    obs_in = obs[0]
    keyval, factor_a = first_projection(obs_in, a_keyval)
    pieces_k = gather_blocks(keyval, "rep")

    a_far = swap(a_out, "mdl", 2)
    queries = (dot(obs_in, a_query) * (factor_a[:, :1] * score_scale)).astype(BF16)
    state = attend_call(queries, pieces_k[:-1], 0, place, [])
    attended = attend_call(queries, pieces_k[-1:], rep_count - 1, place, state)
    attended, a_far = tied(attended, a_far)
    attended_far = swap(attended, "mdl", 2)
    a_all = [a_out, swap(a_out, "mdl", 1), a_far, swap(a_far, "mdl", 1)]
    attended_parts = [
        attended,
        swap(attended, "mdl", 1),
        attended_far,
        swap(attended_far, "mdl", 1),
    ]
    hidden, embed_part = hidden_rows(obs_in, attended_parts, a_all, c_in)

    embed_parts, _ = gather_parts(embed_part)
    critic_keyval, factor_c, embedded = join_rows(place, embed_parts, c_keyval)
    pieces_c = gather_blocks(critic_keyval, "rep")
    critic_queries = (dot(embedded, c_query) * (factor_c[:, :1] * score_scale)).astype(BF16)

    late_hidden, critic_keyval = tied(hidden, critic_keyval)
    source = late_hidden.astype(F32)
    factor_h = row_factor(source)
    logits = dot(late_hidden, w_policy) * factor_h
    log_probs = jax.nn.log_softmax(logits, axis=-1)
    onehot = (
        actions[0][:, None] == lax.broadcasted_iota(jnp.int32, logits.shape, 1)
    ).astype(F32)
    chosen = jnp.sum(onehot * log_probs, axis=-1)
    prob_ratio = jnp.exp(chosen - old_logp[0])
    plain_term = prob_ratio * advantages[0]
    bounded = jnp.clip(prob_ratio, 1.0 - clip_range, 1.0 + clip_range) * advantages[0]
    slope = jnp.where(live_mask & (plain_term <= bounded), -plain_term / live_total, F32(0.0))
    dlogits = slope[:, None] * (onehot - jnp.exp(log_probs))
    along = jnp.sum(dlogits * logits, axis=-1, keepdims=True) / source.shape[1]
    dnormed = dot(dlogits.astype(BF16), w_policy.T)
    dhidden = (factor_h * (dnormed - source * (factor_h * along))).astype(BF16)
    half_a = dhidden.shape[1] // 2
    got_a = swap(
        product(attended, lax.dynamic_slice_in_dim(dhidden, (1 - batch_index) * half_a, half_a, 1))
        .astype(BF16),
        "sec",
        1,
    )
    own_a = product(attended, lax.dynamic_slice_in_dim(dhidden, batch_index * half_a, half_a, 1))

    state_c = attend_call(critic_queries, pieces_c[:-1], 0, place, [])
    *state_c, got_a, pieces_c[-1] = tied(*state_c, got_a, pieces_c[-1])
    keep_a, send_a = split_sum(rep_place, own_a, got_a, rep_count)
    moved_a = swap(send_a.astype(BF16), "rep", 1)
    critic_attended = attend_call(critic_queries, pieces_c[-1:], rep_count - 1, place, state_c)

    send_m, keep_m, their_att, my_att = part_rows(place, critic_attended, c_out)
    got_m = swap(send_m, "mdl", 1)
    got_m, moved_a = tied(got_m, moved_a)
    mine_m = (keep_m + got_m.astype(F32)).astype(BF16)
    bit = 2
    while bit < rep_count:
        keep_a, send_a = halve(keep_a, moved_a)
        moved_a = swap(send_a, "rep", bit)
        bit *= 2
    theirs_m = swap(mine_m, "mdl", 2)
    mine_a = gather_blocks((keep_a + moved_a.astype(F32)).astype(BF16), "rep")
    theirs_a = [swap(block, "sec", 1) for block in mine_a]
    theirs_m, *theirs_a[:-1] = tied(theirs_m, *theirs_a[:-1])
    value_wide, d_other, d_own = mixed_rows(
        place, embedded, mine_m, theirs_m, w_value, returns[0]
    )
    e_other = swap(d_other, "mdl", 1)
    e_own = swap(d_own, "mdl", 1)

    strip = d_own.shape[1] // CHUNKS
    spans = [slice(c * strip, (c + 1) * strip) for c in range(CHUNKS)]

    def both(mine, other, span):
        return product(my_att, mine[:, span]) + product(their_att, other[:, span])

    got = [swap(both(d_other, e_other, span).astype(BF16), "sec", 1) for span in spans]
    own = [both(d_own, e_own, span) for span in spans]
    value_part = lax.dynamic_slice_in_dim(value_wide, mdl_index // 2 * value_rows, value_rows, 0)[:, 0]
    got[0], value_part = tied(got[0], value_part)
    actor_summed = assemble(place, mine_a + theirs_a, rep_count, 0, 1, [])
    marks, result = [], []
    for c in range(CHUNKS):
        arrived = got[c]
        keep, send = split_sum(rep_place, own[c], arrived, rep_count)
        bit, trail = 1, []
        while bit < rep_count:
            arrived = swap(send.astype(BF16), "rep", bit)
            bit *= 2
            if c > 0:
                arrived, _ = tied(arrived, marks[min(len(trail) + 1, len(marks) - 1)])
            elif not trail:
                arrived, actor_summed, *got[1:] = tied(arrived, actor_summed, *got[1:])
            if bit < rep_count:
                keep, send = halve(keep, arrived)
                trail.append(keep)
        total = (keep + arrived.astype(F32)).astype(BF16)
        trail.append(total)
        mine = gather_blocks(total, "rep")
        trail.append(mine[1])
        marks = trail
        theirs = [swap(block, "sec", 1) for block in mine]
        result = [assemble(place, mine + theirs, rep_count, c, CHUNKS, result)]

    return (value_part[None, :], actor_summed, result[0])


def solution(mesh):
    return jax.shard_map(
        on_device,
        mesh=mesh,
        in_specs=(
            P("sec", "rep", None),
            P(None, "mdl"),
            P(None, None, "mdl"),
            P("mdl", None),
            P(),
            P(None, "mdl"),
            P(None, "mdl"),
            P(None, None, "mdl"),
            P("mdl", None),
            P(),
            P("sec", "rep"),
            P("sec", "rep"),
            P("sec", "rep"),
            P("sec", "rep"),
            P(),
        ),
        out_specs=(P("sec", ("rep", "mdl")), P("mdl", None), P("mdl", None)),
        check_vma=False,
    )
```

```python
import functools
import math

import jax
import jax.numpy as jnp
from jax import lax
from jax.experimental import pallas as pl
from jax.experimental.pallas import tpu as pltpu
from jax.sharding import PartitionSpec as P

HEAD = 128
epsilon = 1e-05
clip_range = 0.2
masked_score = -1e30
LOG2E = 1.4426950408889634
F32 = jnp.float32
BF16 = jnp.bfloat16
CHUNKS = 2
TABLE = 6
ROWS = (0, 2, 1, 3)
LIMIT = 40 * 2**20
VMEM = pl.BlockSpec(memory_space=pltpu.VMEM)
SMEM = pl.BlockSpec(memory_space=pltpu.SMEM)
ANY = pl.BlockSpec(memory_space=pl.ANY)
HBM = pl.BlockSpec(memory_space=pltpu.HBM)


def dot(a, b):
    return jnp.dot(a, b, preferred_element_type=F32)


def tied(*items):
    return lax.optimization_barrier(items)


def row_factor(source):
    return lax.rsqrt(jnp.mean(source * source, axis=-1, keepdims=True) + epsilon)


def start_copies(pairs, sems):
    copies = [
        pltpu.make_async_copy(source, target, sems.at[i])
        for i, (source, target) in enumerate(pairs)
    ]
    for copy in copies:
        copy.start()
    return copies


def first_kernel(obs_hbm, w_hbm, kv_ref, factor_ref, obs_ref, w_ref, sems):
    rows, depth = obs_ref.shape
    width = w_hbm.shape[2]
    block = rows // 2
    spans = [slice(i * block, (i + 1) * block) for i in range(2)]
    copies = start_copies(
        [(w_hbm.at[c], w_ref.at[:, c * width : (c + 1) * width]) for c in range(2)]
        + [(obs_hbm.at[span], obs_ref.at[span]) for span in spans],
        sems,
    )
    for i, span in enumerate(spans):
        copies[2 + i].wait()
        part = obs_ref[span, :]
        factor = row_factor(part.astype(F32))
        if i == 0:
            copies[0].wait()
            copies[1].wait()
        both = dot(part, w_ref[...]) * factor
        kv_ref[0, span, :] = both[:, :width].astype(BF16)
        kv_ref[1, span, :] = both[:, width:].astype(BF16)
        factor_ref[span, :] = jnp.broadcast_to(factor, (block, HEAD))


def first_projection(obs, w_keyval):
    rows, depth = obs.shape
    width = w_keyval.shape[2]
    return pl.pallas_call(
        first_kernel,
        in_specs=[HBM] * 2,
        out_specs=[VMEM] * 2,
        out_shape=[
            jax.ShapeDtypeStruct((2, rows, width), BF16),
            jax.ShapeDtypeStruct((rows, HEAD), F32),
        ],
        scratch_shapes=[
            pltpu.VMEM((rows, depth), BF16),
            pltpu.VMEM((depth, 2 * width), BF16),
            pltpu.SemaphoreType.DMA((4,)),
        ],
        compiler_params=pltpu.CompilerParams(vmem_limit_bytes=LIMIT),
        cost_estimate=pl.CostEstimate(
            flops=4 * rows * depth * width, bytes_accessed=2 * rows * depth, transcendentals=0
        ),
        name="first_projection",
    )(obs, w_keyval)


def query_kernel(scale, obs_hbm, w_hbm, factor_ref, q_ref, obs_ref, w_ref, sems):
    for copy in start_copies([(w_hbm, w_ref), (obs_hbm, obs_ref)], sems):
        copy.wait()
    q_ref[...] = (dot(obs_ref[...], w_ref[...]) * (factor_ref[:, :1] * scale)).astype(BF16)


def query_projection(obs, w_query, factor, scale):
    rows, depth = obs.shape
    width = w_query.shape[1]
    return pl.pallas_call(
        functools.partial(query_kernel, scale),
        in_specs=[HBM, HBM, VMEM],
        out_specs=VMEM,
        out_shape=jax.ShapeDtypeStruct((rows, width), BF16),
        scratch_shapes=[
            pltpu.VMEM((rows, depth), BF16),
            pltpu.VMEM((depth, width), BF16),
            pltpu.SemaphoreType.DMA((2,)),
        ],
        compiler_params=pltpu.CompilerParams(vmem_limit_bytes=LIMIT),
        cost_estimate=pl.CostEstimate(
            flops=2 * rows * depth * width, bytes_accessed=2 * rows * depth, transcendentals=0
        ),
        name="query_projection",
    )(obs, w_query, factor)


def attend_blocks(groups, units, first, left_ref, q_ref, kv_refs):
    def fetch(head, span):
        kv_head = head // groups
        columns = slice(kv_head * HEAD, (kv_head + 1) * HEAD)
        query = q_ref[span, head * HEAD : (head + 1) * HEAD]
        lane = lax.broadcasted_iota(jnp.int32, query.shape, 1)
        query = jnp.concatenate([query, (lane == 0).astype(BF16)], axis=1)
        scores = []
        for p, ref in enumerate(kv_refs):
            keys = ref[0, :, columns]
            key = lax.broadcasted_iota(jnp.int32, keys.shape, 0)
            lane = lax.broadcasted_iota(jnp.int32, keys.shape, 1)
            dead = (key >= left_ref[first + p]) & (lane == 0)
            bias = jnp.where(dead, F32(masked_score), F32(0.0)).astype(BF16)
            keys = jnp.concatenate([keys, bias], axis=1)
            scores.append(
                lax.dot_general(
                    query, keys, (((1,), (1,)), ((), ())), preferred_element_type=F32
                )
            )
        return scores

    def values(head, p):
        kv_head = head // groups
        vals = kv_refs[p][1, :, kv_head * HEAD : (kv_head + 1) * HEAD]
        return jnp.concatenate([vals, jnp.ones_like(vals)], axis=1)

    ahead = fetch(*units[0])
    for i, (head, span) in enumerate(units):
        scores = ahead
        if i + 1 < len(units):
            ahead = fetch(*units[i + 1])
        yield head, span, scores, functools.partial(values, head)


def weigh(scores, top, values):
    total = None
    for p, part in enumerate(scores):
        both = dot(jnp.exp2(part - top).astype(BF16), values(p))
        total = both if total is None else total + both
    return total


def highest(scores):
    return functools.reduce(
        jnp.maximum, [jnp.max(part, axis=-1, keepdims=True) for part in scores]
    )


def open_kernel(groups, units, first, left_ref, q_ref, *refs):
    *kv_refs, wide_ref, top_ref = refs
    for head, span, scores, values in attend_blocks(
        groups, units, first, left_ref, q_ref, kv_refs
    ):
        top = highest(scores)
        wide_ref[span, head * 2 * HEAD : (head + 1) * 2 * HEAD] = weigh(scores, top, values)
        top_ref[span, head * HEAD : (head + 1) * HEAD] = jnp.broadcast_to(
            top, (top.shape[0], HEAD)
        )


def close_kernel(groups, units, first, left_ref, q_ref, wide_ref, top_ref, *refs):
    *kv_refs, o_ref = refs
    for head, span, scores, values in attend_blocks(
        groups, units, first, left_ref, q_ref, kv_refs
    ):
        before = top_ref[span, head * HEAD : head * HEAD + 1]
        top = jnp.maximum(before, highest(scores))
        wide = wide_ref[span, head * 2 * HEAD : (head + 1) * 2 * HEAD]
        wide = wide * jnp.exp2(before - top) + weigh(scores, top, values)
        o_ref[span, head * HEAD : (head + 1) * HEAD] = (
            wide[:, :HEAD] / wide[:, HEAD:]
        ).astype(BF16)


def attend_call(queries, pieces, first, place, state):
    rows, width = queries.shape
    heads = width // HEAD
    groups = heads // (pieces[0].shape[2] // HEAD)
    block = min(rows, 256)
    units = [
        (head, slice(i, i + block)) for head in range(heads) for i in range(0, rows, block)
    ]
    count = len(pieces) * pieces[0].shape[1]
    weight = 1 if state else 24
    if state:
        body, name = close_kernel, "attend_close"
        out = jax.ShapeDtypeStruct((rows, width), BF16)
    else:
        body, name = open_kernel, "attend_open"
        out = [
            jax.ShapeDtypeStruct((rows, 2 * width), F32),
            jax.ShapeDtypeStruct((rows, width), F32),
        ]
    return pl.pallas_call(
        functools.partial(body, groups, units, TABLE + first),
        in_specs=[SMEM] + [VMEM] * (1 + len(state) + len(pieces)),
        out_specs=VMEM if state else [VMEM] * 2,
        out_shape=out,
        compiler_params=pltpu.CompilerParams(vmem_limit_bytes=LIMIT),
        cost_estimate=pl.CostEstimate(
            flops=weight * rows * count * width,
            bytes_accessed=4 * rows * width,
            transcendentals=rows * count,
        ),
        name=name,
    )(place, queries, *state, *pieces)


def near_kernel(obs_hbm, t0, t1, w0, w1, sum_ref, obs_ref, w_ref, sems):
    inner, depth = w0.shape
    tile = depth // 3
    pairs = [(obs_hbm, obs_ref), (w0, w_ref.at[:inner]), (w1, w_ref.at[inner:])]
    for copy in start_copies(pairs, sems):
        copy.wait()
    for i in range(3):
        strip = slice(i * tile, (i + 1) * tile)
        parts = jnp.concatenate([t0[...], t1[...]], axis=1)
        sum_ref[:, strip] = obs_ref[:, strip].astype(F32) + dot(parts, w_ref[:, strip])


def near_rows(obs, parts, weights):
    rows, depth = obs.shape
    inner = weights[0].shape[0]
    return pl.pallas_call(
        near_kernel,
        in_specs=[HBM] + [VMEM] * 2 + [HBM, ANY],
        out_specs=VMEM,
        out_shape=jax.ShapeDtypeStruct((rows, depth), F32),
        scratch_shapes=[
            pltpu.VMEM((rows, depth), BF16),
            pltpu.VMEM((2 * inner, depth), BF16),
            pltpu.SemaphoreType.DMA((3,)),
        ],
        compiler_params=pltpu.CompilerParams(vmem_limit_bytes=LIMIT),
        cost_estimate=pl.CostEstimate(
            flops=4 * rows * depth * inner, bytes_accessed=4 * depth * inner, transcendentals=0
        ),
        name="near_rows",
    )(obs, *parts, *weights)


def hidden_kernel(sum_ref, t2, t3, w2, w3, c_hbm, o_ref, emb_ref, w_ref, c_ref, sems):
    inner, depth = w2.shape
    tile = depth // 3
    copies = start_copies(
        [(w2, w_ref.at[:inner]), (w3, w_ref.at[inner:]), (c_hbm, c_ref)], sems
    )
    copies[0].wait()
    copies[1].wait()
    for i in range(3):
        strip = slice(i * tile, (i + 1) * tile)
        parts = jnp.concatenate([t2[...], t3[...]], axis=1)
        o_ref[:, strip] = (sum_ref[:, strip] + dot(parts, w_ref[:, strip])).astype(BF16)
    copies[2].wait()
    emb_ref[...] = dot(o_ref[...], c_ref[...]).astype(BF16)


def hidden_rows(near_sum, parts, weights, c_in):
    rows, depth = near_sum.shape
    inner = weights[0].shape[0]
    width = c_in.shape[1]
    return pl.pallas_call(
        hidden_kernel,
        in_specs=[VMEM] * 3 + [ANY] * 2 + [HBM],
        out_specs=[VMEM] * 2,
        out_shape=[
            jax.ShapeDtypeStruct((rows, depth), BF16),
            jax.ShapeDtypeStruct((rows, width), BF16),
        ],
        scratch_shapes=[
            pltpu.VMEM((2 * inner, depth), BF16),
            pltpu.VMEM((depth, width), BF16),
            pltpu.SemaphoreType.DMA((3,)),
        ],
        compiler_params=pltpu.CompilerParams(vmem_limit_bytes=LIMIT),
        cost_estimate=pl.CostEstimate(
            flops=8 * rows * depth * inner, bytes_accessed=8 * depth * inner, transcendentals=0
        ),
        name="hidden_rows",
    )(near_sum, *parts, *weights, c_in)


def join_kernel(place_ref, e0, e1, e2, e3, wkv_any, kv_ref, factor_ref, emb_ref, wkv_ref, sems):
    rows, wide = emb_ref.shape
    width = wkv_any.shape[2]
    strip = e0.shape[1]
    copies = start_copies(
        [(wkv_any.at[c], wkv_ref.at[:, c * width : (c + 1) * width]) for c in range(2)], sems
    )
    starts = [pl.multiple_of((place_ref[1] ^ code) * strip, strip) for code in range(4)]
    parts = (e0, e1, e2, e3)
    for copy in copies:
        copy.wait()
    block = rows // 2
    for i in range(2):
        span = slice(i * block, (i + 1) * block)
        square, both = 0.0, 0.0
        for part, start in zip(parts, starts):
            emb = part[span, :]
            wide_emb = emb.astype(F32)
            square = square + jnp.sum(wide_emb * wide_emb, axis=-1, keepdims=True)
            both = both + dot(emb, wkv_ref[pl.ds(start, strip), :])
            emb_ref[span, pl.ds(start, strip)] = emb
        factor = lax.rsqrt(square / wide + epsilon)
        both = both * factor
        kv_ref[0, span, :] = both[:, :width].astype(BF16)
        kv_ref[1, span, :] = both[:, width:].astype(BF16)
        factor_ref[span, :] = jnp.broadcast_to(factor, (block, HEAD))


def join_rows(place, parts, w_keyval):
    rows, strip = parts[0].shape
    wide = 4 * strip
    width = w_keyval.shape[2]
    return pl.pallas_call(
        join_kernel,
        in_specs=[SMEM] + [VMEM] * 4 + [HBM],
        out_specs=[VMEM] * 3,
        out_shape=[
            jax.ShapeDtypeStruct((2, rows, width), BF16),
            jax.ShapeDtypeStruct((rows, HEAD), F32),
            jax.ShapeDtypeStruct((rows, wide), BF16),
        ],
        scratch_shapes=[pltpu.VMEM((wide, 2 * width), BF16), pltpu.SemaphoreType.DMA((2,))],
        compiler_params=pltpu.CompilerParams(vmem_limit_bytes=LIMIT),
        cost_estimate=pl.CostEstimate(
            flops=4 * rows * wide * width, bytes_accessed=4 * rows * wide, transcendentals=0
        ),
        name="join_rows",
    )(place, *parts, w_keyval)


def part_kernel(place_ref, att_ref, c_hbm, send_ref, keep_ref, order_ref, c_ref, sems):
    rows, inner = att_ref.shape
    wide = c_ref.shape[1]
    block = rows // 4
    half = inner // 2
    spans = [slice(i * half, (i + 1) * half) for i in range(2)]
    copies = start_copies([(c_hbm.at[span], c_ref.at[span]) for span in spans], sems)
    for at, code in enumerate(ROWS):
        start = pl.multiple_of((place_ref[1] ^ code) * block, block)
        order_ref[at * block : (at + 1) * block, :] = att_ref[pl.ds(start, block), :]
    for copy in copies:
        copy.wait()
    tile = 512
    for out, source in ((send_ref, order_ref[2 * block :, :]), (keep_ref, order_ref[: 2 * block, :])):
        for j in range(wide // tile):
            columns = slice(j * tile, (j + 1) * tile)
            out[:, columns] = dot(source, c_ref[:, columns]).astype(out.dtype)


def part_rows(place, attended, c_out):
    rows, inner = attended.shape
    wide = c_out.shape[1]
    return pl.pallas_call(
        part_kernel,
        in_specs=[SMEM, VMEM, HBM],
        out_specs=[VMEM] * 3,
        out_shape=[
            jax.ShapeDtypeStruct((rows // 2, wide), BF16),
            jax.ShapeDtypeStruct((rows // 2, wide), F32),
            jax.ShapeDtypeStruct((rows, inner), BF16),
        ],
        scratch_shapes=[pltpu.VMEM((inner, wide), BF16), pltpu.SemaphoreType.DMA((2,))],
        compiler_params=pltpu.CompilerParams(vmem_limit_bytes=LIMIT),
        cost_estimate=pl.CostEstimate(
            flops=2 * rows * wide * inner, bytes_accessed=8 * wide * inner, transcendentals=0
        ),
        name="part_rows",
    )(place, attended, c_out)


def mixed_kernel(
    place_ref, emb_any, keep_ref, near_ref, got_ref, wv_ref, ret_ref,
    value_ref, other_ref, own_ref, emb_ref, mixed_ref, sem,
):
    rows, wide = got_ref.shape
    half = wide // 2
    block = 32
    base = pl.multiple_of(place_ref[1] * rows, rows)
    copy = pltpu.make_async_copy(emb_any.at[pl.ds(base, rows)], emb_ref, sem)
    copy.start()
    live_total = place_ref[4].astype(F32)
    copy.wait()

    @pl.loop(0, rows // block)
    def _(i):
        start = pl.multiple_of(i * block, block)
        span = pl.ds(start, block)
        mixed = emb_ref[span, :].astype(F32) + (
            keep_ref[span, :] + near_ref[span, :].astype(F32) + got_ref[span, :].astype(F32)
        )
        mixed_ref[...] = mixed
        factor = row_factor(mixed)
        value = factor * jnp.sum(mixed * wv_ref[...].astype(F32), axis=-1, keepdims=True)
        row = place_ref[2] + base + start + lax.broadcasted_iota(jnp.int32, (block, 1), 0)
        gap = jnp.where(row < place_ref[3], value - ret_ref[span, :], F32(0.0)) / live_total
        lead = factor * gap
        pull = lead * factor * value / wide
        value_ref[span, :] = jnp.broadcast_to(value, (block, HEAD))
        for out, side in ((own_ref, place_ref[0]), (other_ref, 1 - place_ref[0])):
            columns = pl.ds(pl.multiple_of(side * half, half), half)
            part = mixed_ref[:, columns]
            out[span, :] = (lead * wv_ref[:, columns].astype(F32) - part * pull).astype(BF16)


def mixed_rows(place, embedded, keep, near, got, w_value, returns):
    rows, wide = got.shape
    return pl.pallas_call(
        mixed_kernel,
        in_specs=[SMEM, ANY] + [VMEM] * 5,
        out_specs=[VMEM] * 3,
        out_shape=[
            jax.ShapeDtypeStruct((rows, HEAD), F32),
            jax.ShapeDtypeStruct((rows, wide // 2), BF16),
            jax.ShapeDtypeStruct((rows, wide // 2), BF16),
        ],
        scratch_shapes=[
            pltpu.VMEM((rows, wide), BF16),
            pltpu.VMEM((32, wide), F32),
            pltpu.SemaphoreType.DMA,
        ],
        compiler_params=pltpu.CompilerParams(vmem_limit_bytes=LIMIT),
        cost_estimate=pl.CostEstimate(
            flops=10 * rows * wide, bytes_accessed=12 * rows * wide, transcendentals=0
        ),
        name="mixed_rows",
    )(place, embedded, keep, near, got, w_value, returns)


def gather_codes(size):
    codes, bit = [0], size // 2
    while bit >= 1:
        codes = codes + [code ^ bit for code in codes]
        bit //= 2
    return codes


def split_kernel(codes, index_ref, own_ref, got_ref, keep_ref, send_ref):
    block = own_ref.shape[0] // len(codes)
    side = len(codes) // 2
    for k, code in enumerate(codes):
        span = pl.ds(pl.multiple_of((index_ref[0] ^ code) * block, block), block)
        out = (keep_ref, send_ref)[k // side]
        at = k % side * block
        total = own_ref[span, :] + got_ref[span, :].astype(F32)
        out[at : at + block, :] = total.astype(out.dtype)


def split_sum(index, own, got, count):
    rows, wide = own.shape
    if (rows // count) % 16:
        got = got.astype(F32)
    send_type = BF16 if (rows // count) % 16 == 0 else F32
    return pl.pallas_call(
        functools.partial(split_kernel, gather_codes(count)),
        in_specs=[SMEM, VMEM, VMEM],
        out_specs=[VMEM] * 2,
        out_shape=[
            jax.ShapeDtypeStruct((rows // 2, wide), F32),
            jax.ShapeDtypeStruct((rows // 2, wide), send_type),
        ],
        compiler_params=pltpu.CompilerParams(vmem_limit_bytes=LIMIT),
        cost_estimate=pl.CostEstimate(
            flops=rows * wide, bytes_accessed=8 * rows * wide, transcendentals=0
        ),
        name="split_sum",
    )(index, own, got)


def assemble_kernel(codes, chunk, chunks, place_ref, *refs):
    parts = refs[: len(codes) * 2]
    out, got_ref, wide_ref, got_sems, sems = refs[-5:]
    block, strip = parts[0].shape
    got = start_copies([(part, got_ref.at[i]) for i, part in enumerate(parts)], got_sems)
    copies = []
    for side in range(2):
        for k, code in enumerate(codes):
            at = side * len(codes) + k
            row = pl.multiple_of((place_ref[5] ^ code) * block, block)
            column = pl.multiple_of(((place_ref[0] ^ side) * chunks + chunk) * strip, strip)
            got[at].wait()
            wide_ref[at] = got_ref[at].astype(F32)
            copy = pltpu.make_async_copy(
                wide_ref.at[at],
                out.at[pl.ds(row, block), pl.ds(column, strip)],
                sems.at[at],
            )
            copy.start()
            copies.append(copy)
    for copy in copies:
        copy.wait()


def assemble(place, parts, count, chunk, chunks, before):
    block, strip = parts[0].shape
    rows, wide = block * count, strip * 2 * chunks
    return pl.pallas_call(
        functools.partial(assemble_kernel, gather_codes(count), chunk, chunks),
        in_specs=[SMEM] + [ANY] * (len(parts) + len(before)),
        out_specs=ANY,
        out_shape=jax.ShapeDtypeStruct((rows, wide), F32),
        input_output_aliases={1 + len(parts): 0} if before else {},
        scratch_shapes=[
            pltpu.VMEM((len(parts), block, strip), BF16),
            pltpu.VMEM((len(parts), block, strip), F32),
            pltpu.SemaphoreType.DMA((len(parts),)),
            pltpu.SemaphoreType.DMA((len(parts),)),
        ],
        compiler_params=pltpu.CompilerParams(vmem_limit_bytes=LIMIT),
        cost_estimate=pl.CostEstimate(
            flops=rows * wide, bytes_accessed=6 * rows * wide, transcendentals=0
        ),
        name="assemble",
    )(place, *parts, *before)


def swap(block, axis, bit):
    size = lax.axis_size(axis)
    return lax.ppermute(block, axis, [(i, i ^ bit) for i in range(size)])


def gather_blocks(block, axis, late=None):
    blocks, bit = [block], lax.axis_size(axis) // 2
    while bit >= 1:
        sources = blocks if bit > 1 or late is None else [late] + blocks[1:]
        blocks = blocks + [swap(item, axis, bit) for item in sources]
        bit //= 2
    return blocks


def gather_parts(part):
    far = swap(part, "mdl", 2)
    return [part, swap(part, "mdl", 1), far, swap(far, "mdl", 1)], far


def product(left, right):
    return jnp.einsum("rh,rd->hd", left, right, preferred_element_type=F32)


def halve(keep, got):
    total = keep + got.astype(F32)
    side = total.shape[0] // 2
    return total[:side], total[side:].astype(BF16)


def on_device(
    obs,
    a_query,
    a_keyval,
    a_out,
    w_policy,
    c_in,
    c_query,
    c_keyval,
    c_out,
    w_value,
    actions,
    advantages,
    old_logp,
    returns,
    robot_count,
):
    row_count = obs.shape[1]
    batch_index = lax.axis_index("sec")
    rep_index = lax.axis_index("rep")
    rep_count = lax.axis_size("rep")
    robot_total = robot_count[batch_index]
    live_sum = jnp.sum(robot_count)
    live_total = live_sum.astype(F32)
    first_row = rep_index * row_count
    live_mask = first_row + lax.iota(jnp.int32, row_count) < robot_total
    mdl_count = lax.axis_size("mdl")
    assert mdl_count == 4 and lax.axis_size("sec") == 2
    mdl_index = lax.axis_index("mdl")
    value_rows = row_count // mdl_count
    score_scale = HEAD ** (-0.5) * LOG2E
    rep_place = rep_index.reshape(1).astype(jnp.int32)

    place = jnp.stack(
        [batch_index, mdl_index, first_row, robot_total, live_sum, rep_index]
        + [
            jnp.clip(robot_total - (rep_index ^ code) * row_count, 0, row_count)
            for code in gather_codes(rep_count)
        ]
    ).astype(jnp.int32)

    obs_in = obs[0]
    keyval, factor_a = first_projection(obs_in, a_keyval)
    a_far = swap(a_out, "mdl", 2)
    queries = query_projection(obs_in, a_query, factor_a, score_scale)
    late_keyval, queries = tied(keyval, queries)
    pieces_k = gather_blocks(keyval, "rep", late_keyval)
    state = attend_call(queries, pieces_k[:-1], 0, place, [])
    attended = attend_call(queries, pieces_k[-1:], rep_count - 1, place, state)
    attended, a_far = tied(attended, a_far)
    attended_far = swap(attended, "mdl", 2)
    attended_near = swap(attended, "mdl", 1)
    near_sum = near_rows(obs_in, [attended, attended_near], [a_out, swap(a_out, "mdl", 1)])
    hidden, embed_part = hidden_rows(
        near_sum,
        [attended_far, swap(attended_far, "mdl", 1)],
        [a_far, swap(a_far, "mdl", 1)],
        c_in,
    )

    embed_parts, _ = gather_parts(embed_part)
    critic_keyval, factor_c, embedded = join_rows(place, embed_parts, c_keyval)
    critic_queries = (dot(embedded, c_query) * (factor_c[:, :1] * score_scale)).astype(BF16)
    late_keyval, critic_queries = tied(critic_keyval, critic_queries)
    pieces_c = gather_blocks(critic_keyval, "rep", late_keyval)

    late_hidden, critic_keyval = tied(hidden, critic_keyval)
    source = late_hidden.astype(F32)
    factor_h = row_factor(source)
    logits = dot(late_hidden, w_policy) * factor_h
    log_probs = jax.nn.log_softmax(logits, axis=-1)
    onehot = (
        actions[0][:, None] == lax.broadcasted_iota(jnp.int32, logits.shape, 1)
    ).astype(F32)
    chosen = jnp.sum(onehot * log_probs, axis=-1)
    prob_ratio = jnp.exp(chosen - old_logp[0])
    plain_term = prob_ratio * advantages[0]
    bounded = jnp.clip(prob_ratio, 1.0 - clip_range, 1.0 + clip_range) * advantages[0]
    slope = jnp.where(live_mask & (plain_term <= bounded), -plain_term / live_total, F32(0.0))
    dlogits = slope[:, None] * (onehot - jnp.exp(log_probs))
    along = jnp.sum(dlogits * logits, axis=-1, keepdims=True) / source.shape[1]
    dnormed = dot(dlogits.astype(BF16), w_policy.T)
    dhidden = (factor_h * (dnormed - source * (factor_h * along))).astype(BF16)
    half_a = dhidden.shape[1] // 2
    got_a = swap(
        product(attended, lax.dynamic_slice_in_dim(dhidden, (1 - batch_index) * half_a, half_a, 1))
        .astype(BF16),
        "sec",
        1,
    )
    own_a = product(attended, lax.dynamic_slice_in_dim(dhidden, batch_index * half_a, half_a, 1))

    wide = w_value.shape[0]
    target = lax.dynamic_slice_in_dim(returns[0], mdl_index * value_rows, value_rows, 0)
    critic_queries, own_a, w_row, target = tied(
        critic_queries, own_a, w_value.reshape(1, wide), target.reshape(value_rows, 1)
    )
    state_c = attend_call(critic_queries, pieces_c[:-1], 0, place, [])
    *state_c, got_a, pieces_c[-1] = tied(*state_c, got_a, pieces_c[-1])
    keep_a, send_a = split_sum(rep_place, own_a, got_a, rep_count)
    *state_c, send_a = tied(*state_c, send_a)
    moved_a = swap(send_a.astype(BF16), "rep", 1)
    critic_attended = attend_call(critic_queries, pieces_c[-1:], rep_count - 1, place, state_c)

    send_m, keep_m, att_rows = part_rows(place, critic_attended, c_out)
    near_m = swap(send_m, "mdl", 1)
    send_y = (keep_m[value_rows:] + near_m[value_rows:].astype(F32)).astype(BF16)
    got_y = swap(send_y, "mdl", 2)
    att_there = swap(critic_attended, "sec", 1)
    got_y, moved_a = tied(got_y, moved_a)
    value_wide, d_other, d_own = mixed_rows(
        place, embedded, keep_m, near_m, got_y, w_row, target
    )

    d_there = swap(d_other, "sec", 1)
    d_far = swap(d_own, "mdl", 2)
    d_near = swap(d_own, "mdl", 1)
    bit = 2
    while bit < rep_count:
        keep_a, send_a = halve(keep_a, moved_a)
        moved_a = swap(send_a, "rep", bit)
        bit *= 2
    there_far = swap(d_there, "mdl", 2)
    there_near = swap(d_there, "mdl", 1)
    own_rows = jnp.concatenate([d_own, d_far, d_near, swap(d_far, "mdl", 1)], axis=0)
    there_far, moved_a = tied(there_far, moved_a)
    there_rows = jnp.concatenate(
        [d_there, there_far, there_near, swap(there_far, "mdl", 1)], axis=0
    )
    att_there = jnp.concatenate(
        [
            lax.dynamic_slice_in_dim(att_there, (mdl_index ^ code) * value_rows, value_rows, 0)
            for code in ROWS
        ],
        axis=0,
    )
    value_part, there_rows = tied(value_wide[:, 0], there_rows)
    mine_a = gather_blocks((keep_a + moved_a.astype(F32)).astype(BF16), "rep")
    theirs_a = [swap(block, "sec", 1) for block in mine_a]
    actor_summed = assemble(place, mine_a + theirs_a, rep_count, 0, 1, [])

    strip = d_own.shape[1] // CHUNKS
    marks, result = [], []
    for c in range(CHUNKS):
        span = slice(c * strip, (c + 1) * strip)
        keep, send = split_sum(
            rep_place,
            product(att_rows, own_rows[:, span]),
            product(att_there, there_rows[:, span]),
            rep_count,
        )
        bit, trail = 1, []
        while bit < rep_count:
            arrived = swap(send.astype(BF16), "rep", bit)
            bit *= 2
            if c > 0:
                arrived, _ = tied(arrived, marks[min(len(trail) + 1, len(marks) - 1)])
            if bit < rep_count:
                keep, send = halve(keep, arrived)
                trail.append(keep)
        total = (keep + arrived.astype(F32)).astype(BF16)
        trail.append(total)
        mine = gather_blocks(total, "rep")
        trail.append(mine[1])
        marks = trail
        theirs = [swap(block, "sec", 1) for block in mine]
        result = [assemble(place, mine + theirs, rep_count, c, CHUNKS, result)]

    return (value_part[None, :], actor_summed, result[0])


def solution(mesh):
    return jax.shard_map(
        on_device,
        mesh=mesh,
        in_specs=(
            P("sec", "rep", None),
            P(None, "mdl"),
            P(None, None, "mdl"),
            P("mdl", None),
            P(),
            P(None, "mdl"),
            P(None, "mdl"),
            P(None, None, "mdl"),
            P("mdl", None),
            P(),
            P("sec", "rep"),
            P("sec", "rep"),
            P("sec", "rep"),
            P("sec", "rep"),
            P(),
        ),
        out_specs=(P("sec", ("rep", "mdl")), P("mdl", None), P("mdl", None)),
        check_vma=False,
    )
```

```python
import functools
import math

import jax
import jax.numpy as jnp
from jax import lax
from jax.experimental import pallas as pl
from jax.experimental.pallas import tpu as pltpu
from jax.sharding import PartitionSpec as P

HEAD = 128
epsilon = 1e-05
clip_range = 0.2
masked_score = -1e30
LOG2E = 1.4426950408889634
F32 = jnp.float32
BF16 = jnp.bfloat16
CHUNKS = 2
TABLE = 6
ROWS = (0, 2, 1, 3)
LIMIT = 40 * 2**20
HIGH = 56 * 2**20
VMEM = pl.BlockSpec(memory_space=pltpu.VMEM)
SMEM = pl.BlockSpec(memory_space=pltpu.SMEM)
ANY = pl.BlockSpec(memory_space=pl.ANY)
HBM = pl.BlockSpec(memory_space=pltpu.HBM)


def dot(a, b):
    return jnp.dot(a, b, preferred_element_type=F32)


def tied(*items):
    return lax.optimization_barrier(items)


def row_factor(source):
    return lax.rsqrt(jnp.mean(source * source, axis=-1, keepdims=True) + epsilon)


def start_copies(pairs, sems):
    copies = [
        pltpu.make_async_copy(source, target, sems.at[i])
        for i, (source, target) in enumerate(pairs)
    ]
    for copy in copies:
        copy.start()
    return copies


def first_kernel(obs_hbm, w_hbm, kv_ref, factor_ref, obs_ref, w_ref, sems):
    rows, depth = obs_ref.shape
    width = w_hbm.shape[2]
    block = rows // 2
    spans = [slice(i * block, (i + 1) * block) for i in range(2)]
    copies = start_copies(
        [(w_hbm.at[c], w_ref.at[:, c * width : (c + 1) * width]) for c in range(2)]
        + [(obs_hbm.at[span], obs_ref.at[span]) for span in spans],
        sems,
    )
    for i, span in enumerate(spans):
        copies[2 + i].wait()
        part = obs_ref[span, :]
        factor = row_factor(part.astype(F32))
        if i == 0:
            copies[0].wait()
            copies[1].wait()
        both = dot(part, w_ref[...]) * factor
        kv_ref[0, span, :] = both[:, :width].astype(BF16)
        kv_ref[1, span, :] = both[:, width:].astype(BF16)
        factor_ref[span, :] = jnp.broadcast_to(factor, (block, HEAD))


def first_projection(obs, w_keyval):
    rows, depth = obs.shape
    width = w_keyval.shape[2]
    return pl.pallas_call(
        first_kernel,
        in_specs=[HBM] * 2,
        out_specs=[VMEM] * 2,
        out_shape=[
            jax.ShapeDtypeStruct((2, rows, width), BF16),
            jax.ShapeDtypeStruct((rows, HEAD), F32),
        ],
        scratch_shapes=[
            pltpu.VMEM((rows, depth), BF16),
            pltpu.VMEM((depth, 2 * width), BF16),
            pltpu.SemaphoreType.DMA((4,)),
        ],
        compiler_params=pltpu.CompilerParams(vmem_limit_bytes=HIGH),
        cost_estimate=pl.CostEstimate(
            flops=4 * rows * depth * width, bytes_accessed=2 * rows * depth, transcendentals=0
        ),
        name="first_projection",
    )(obs, w_keyval)


def query_kernel(scale, obs_hbm, w_hbm, factor_ref, q_ref, obs_ref, w_ref, sems):
    for copy in start_copies([(w_hbm, w_ref), (obs_hbm, obs_ref)], sems):
        copy.wait()
    q_ref[...] = (dot(obs_ref[...], w_ref[...]) * (factor_ref[:, :1] * scale)).astype(BF16)


def query_projection(obs, w_query, factor, scale):
    rows, depth = obs.shape
    width = w_query.shape[1]
    return pl.pallas_call(
        functools.partial(query_kernel, scale),
        in_specs=[HBM, HBM, VMEM],
        out_specs=VMEM,
        out_shape=jax.ShapeDtypeStruct((rows, width), BF16),
        scratch_shapes=[
            pltpu.VMEM((rows, depth), BF16),
            pltpu.VMEM((depth, width), BF16),
            pltpu.SemaphoreType.DMA((2,)),
        ],
        compiler_params=pltpu.CompilerParams(vmem_limit_bytes=HIGH),
        cost_estimate=pl.CostEstimate(
            flops=2 * rows * depth * width, bytes_accessed=2 * rows * depth, transcendentals=0
        ),
        name="query_projection",
    )(obs, w_query, factor)


def attend_blocks(groups, units, first, left_ref, q_ref, kv_refs):
    def fetch(head, span):
        kv_head = head // groups
        columns = slice(kv_head * HEAD, (kv_head + 1) * HEAD)
        query = q_ref[span, head * HEAD : (head + 1) * HEAD]
        lane = lax.broadcasted_iota(jnp.int32, query.shape, 1)
        query = jnp.concatenate([query, (lane == 0).astype(BF16)], axis=1)
        scores = []
        for p, ref in enumerate(kv_refs):
            keys = ref[0, :, columns]
            key = lax.broadcasted_iota(jnp.int32, keys.shape, 0)
            lane = lax.broadcasted_iota(jnp.int32, keys.shape, 1)
            dead = (key >= left_ref[first + p]) & (lane == 0)
            bias = jnp.where(dead, F32(masked_score), F32(0.0)).astype(BF16)
            keys = jnp.concatenate([keys, bias], axis=1)
            scores.append(
                lax.dot_general(
                    query, keys, (((1,), (1,)), ((), ())), preferred_element_type=F32
                )
            )
        return scores

    def values(head, p):
        kv_head = head // groups
        vals = kv_refs[p][1, :, kv_head * HEAD : (kv_head + 1) * HEAD]
        return jnp.concatenate([vals, jnp.ones_like(vals)], axis=1)

    ahead = fetch(*units[0])
    for i, (head, span) in enumerate(units):
        scores = ahead
        if i + 1 < len(units):
            ahead = fetch(*units[i + 1])
        yield head, span, scores, functools.partial(values, head)


def weigh(scores, top, values):
    total = None
    for p, part in enumerate(scores):
        both = dot(jnp.exp2(part - top).astype(BF16), values(p))
        total = both if total is None else total + both
    return total


def highest(scores):
    return functools.reduce(
        jnp.maximum, [jnp.max(part, axis=-1, keepdims=True) for part in scores]
    )


def open_kernel(groups, units, first, left_ref, q_ref, *refs):
    *kv_refs, wide_ref, top_ref = refs
    for head, span, scores, values in attend_blocks(
        groups, units, first, left_ref, q_ref, kv_refs
    ):
        top = highest(scores)
        wide_ref[span, head * 2 * HEAD : (head + 1) * 2 * HEAD] = weigh(scores, top, values)
        top_ref[span, head * HEAD : (head + 1) * HEAD] = jnp.broadcast_to(
            top, (top.shape[0], HEAD)
        )


def close_kernel(groups, units, first, left_ref, q_ref, wide_ref, top_ref, *refs):
    *kv_refs, o_ref = refs
    for head, span, scores, values in attend_blocks(
        groups, units, first, left_ref, q_ref, kv_refs
    ):
        before = top_ref[span, head * HEAD : head * HEAD + 1]
        top = jnp.maximum(before, highest(scores))
        wide = wide_ref[span, head * 2 * HEAD : (head + 1) * 2 * HEAD]
        wide = wide * jnp.exp2(before - top) + weigh(scores, top, values)
        o_ref[span, head * HEAD : (head + 1) * HEAD] = (
            wide[:, :HEAD] / wide[:, HEAD:]
        ).astype(BF16)


def attend_call(queries, pieces, first, place, state):
    rows, width = queries.shape
    heads = width // HEAD
    groups = heads // (pieces[0].shape[2] // HEAD)
    block = min(rows, 256)
    units = [
        (head, slice(i, i + block)) for head in range(heads) for i in range(0, rows, block)
    ]
    count = len(pieces) * pieces[0].shape[1]
    weight = 1 if state else 24
    if state:
        body, name = close_kernel, "attend_close"
        out = jax.ShapeDtypeStruct((rows, width), BF16)
    else:
        body, name = open_kernel, "attend_open"
        out = [
            jax.ShapeDtypeStruct((rows, 2 * width), F32),
            jax.ShapeDtypeStruct((rows, width), F32),
        ]
    return pl.pallas_call(
        functools.partial(body, groups, units, TABLE + first),
        in_specs=[SMEM] + [VMEM] * (1 + len(state) + len(pieces)),
        out_specs=VMEM if state else [VMEM] * 2,
        out_shape=out,
        compiler_params=pltpu.CompilerParams(vmem_limit_bytes=LIMIT),
        cost_estimate=pl.CostEstimate(
            flops=weight * rows * count * width,
            bytes_accessed=4 * rows * width,
            transcendentals=rows * count,
        ),
        name=name,
    )(place, queries, *state, *pieces)


def near_kernel(obs_hbm, t0, t1, w0, w1, sum_ref, obs_ref, w_ref, sems):
    inner, depth = w0.shape
    tile = depth // 3
    pairs = [(obs_hbm, obs_ref), (w0, w_ref.at[:inner]), (w1, w_ref.at[inner:])]
    for copy in start_copies(pairs, sems):
        copy.wait()
    for i in range(3):
        strip = slice(i * tile, (i + 1) * tile)
        parts = jnp.concatenate([t0[...], t1[...]], axis=1)
        sum_ref[:, strip] = obs_ref[:, strip].astype(F32) + dot(parts, w_ref[:, strip])


def near_rows(obs, parts, weights):
    rows, depth = obs.shape
    inner = weights[0].shape[0]
    return pl.pallas_call(
        near_kernel,
        in_specs=[HBM] + [VMEM] * 2 + [HBM, ANY],
        out_specs=VMEM,
        out_shape=jax.ShapeDtypeStruct((rows, depth), F32),
        scratch_shapes=[
            pltpu.VMEM((rows, depth), BF16),
            pltpu.VMEM((2 * inner, depth), BF16),
            pltpu.SemaphoreType.DMA((3,)),
        ],
        compiler_params=pltpu.CompilerParams(vmem_limit_bytes=LIMIT),
        cost_estimate=pl.CostEstimate(
            flops=4 * rows * depth * inner, bytes_accessed=4 * depth * inner, transcendentals=0
        ),
        name="near_rows",
    )(obs, *parts, *weights)


def hidden_kernel(sum_ref, t2, t3, w2, w3, c_hbm, o_ref, emb_ref, w_ref, c_ref, sems):
    inner, depth = w2.shape
    tile = depth // 3
    copies = start_copies(
        [(w2, w_ref.at[:inner]), (w3, w_ref.at[inner:]), (c_hbm, c_ref)], sems
    )
    copies[0].wait()
    copies[1].wait()
    for i in range(3):
        strip = slice(i * tile, (i + 1) * tile)
        parts = jnp.concatenate([t2[...], t3[...]], axis=1)
        o_ref[:, strip] = (sum_ref[:, strip] + dot(parts, w_ref[:, strip])).astype(BF16)
    copies[2].wait()
    emb_ref[...] = dot(o_ref[...], c_ref[...]).astype(BF16)


def hidden_rows(near_sum, parts, weights, c_in):
    rows, depth = near_sum.shape
    inner = weights[0].shape[0]
    width = c_in.shape[1]
    return pl.pallas_call(
        hidden_kernel,
        in_specs=[VMEM] * 3 + [ANY] * 2 + [HBM],
        out_specs=[VMEM] * 2,
        out_shape=[
            jax.ShapeDtypeStruct((rows, depth), BF16),
            jax.ShapeDtypeStruct((rows, width), BF16),
        ],
        scratch_shapes=[
            pltpu.VMEM((2 * inner, depth), BF16),
            pltpu.VMEM((depth, width), BF16),
            pltpu.SemaphoreType.DMA((3,)),
        ],
        compiler_params=pltpu.CompilerParams(vmem_limit_bytes=LIMIT),
        cost_estimate=pl.CostEstimate(
            flops=8 * rows * depth * inner, bytes_accessed=8 * depth * inner, transcendentals=0
        ),
        name="hidden_rows",
    )(near_sum, *parts, *weights, c_in)


def join_kernel(place_ref, e0, e1, e2, e3, wkv_any, kv_ref, factor_ref, emb_ref, wkv_ref, sems):
    rows, wide = emb_ref.shape
    width = wkv_any.shape[2]
    strip = e0.shape[1]
    copies = start_copies(
        [(wkv_any.at[c], wkv_ref.at[:, c * width : (c + 1) * width]) for c in range(2)], sems
    )
    starts = [pl.multiple_of((place_ref[1] ^ code) * strip, strip) for code in range(4)]
    parts = (e0, e1, e2, e3)
    for copy in copies:
        copy.wait()
    block = rows // 2
    for i in range(2):
        span = slice(i * block, (i + 1) * block)
        square, both = 0.0, 0.0
        for part, start in zip(parts, starts):
            emb = part[span, :]
            wide_emb = emb.astype(F32)
            square = square + jnp.sum(wide_emb * wide_emb, axis=-1, keepdims=True)
            both = both + dot(emb, wkv_ref[pl.ds(start, strip), :])
            emb_ref[span, pl.ds(start, strip)] = emb
        factor = lax.rsqrt(square / wide + epsilon)
        both = both * factor
        kv_ref[0, span, :] = both[:, :width].astype(BF16)
        kv_ref[1, span, :] = both[:, width:].astype(BF16)
        factor_ref[span, :] = jnp.broadcast_to(factor, (block, HEAD))


def join_rows(place, parts, w_keyval):
    rows, strip = parts[0].shape
    wide = 4 * strip
    width = w_keyval.shape[2]
    return pl.pallas_call(
        join_kernel,
        in_specs=[SMEM] + [VMEM] * 4 + [HBM],
        out_specs=[VMEM] * 3,
        out_shape=[
            jax.ShapeDtypeStruct((2, rows, width), BF16),
            jax.ShapeDtypeStruct((rows, HEAD), F32),
            jax.ShapeDtypeStruct((rows, wide), BF16),
        ],
        scratch_shapes=[pltpu.VMEM((wide, 2 * width), BF16), pltpu.SemaphoreType.DMA((2,))],
        compiler_params=pltpu.CompilerParams(vmem_limit_bytes=LIMIT),
        cost_estimate=pl.CostEstimate(
            flops=4 * rows * wide * width, bytes_accessed=4 * rows * wide, transcendentals=0
        ),
        name="join_rows",
    )(place, *parts, w_keyval)


def part_kernel(place_ref, att_ref, c_hbm, send_ref, keep_ref, order_ref, c_ref, sems):
    rows, inner = att_ref.shape
    wide = c_ref.shape[1]
    block = rows // 4
    half = inner // 2
    spans = [slice(i * half, (i + 1) * half) for i in range(2)]
    copies = start_copies([(c_hbm.at[span], c_ref.at[span]) for span in spans], sems)
    for at, code in enumerate(ROWS):
        start = pl.multiple_of((place_ref[1] ^ code) * block, block)
        order_ref[at * block : (at + 1) * block, :] = att_ref[pl.ds(start, block), :]
    for copy in copies:
        copy.wait()
    tile = 512
    for out, source in ((send_ref, order_ref[2 * block :, :]), (keep_ref, order_ref[: 2 * block, :])):
        for j in range(wide // tile):
            columns = slice(j * tile, (j + 1) * tile)
            out[:, columns] = dot(source, c_ref[:, columns]).astype(out.dtype)


def part_rows(place, attended, c_out):
    rows, inner = attended.shape
    wide = c_out.shape[1]
    return pl.pallas_call(
        part_kernel,
        in_specs=[SMEM, VMEM, HBM],
        out_specs=[VMEM] * 3,
        out_shape=[
            jax.ShapeDtypeStruct((rows // 2, wide), BF16),
            jax.ShapeDtypeStruct((rows // 2, wide), F32),
            jax.ShapeDtypeStruct((rows, inner), BF16),
        ],
        scratch_shapes=[pltpu.VMEM((inner, wide), BF16), pltpu.SemaphoreType.DMA((2,))],
        compiler_params=pltpu.CompilerParams(vmem_limit_bytes=LIMIT),
        cost_estimate=pl.CostEstimate(
            flops=2 * rows * wide * inner, bytes_accessed=8 * wide * inner, transcendentals=0
        ),
        name="part_rows",
    )(place, attended, c_out)


def mixed_kernel(
    place_ref, emb_ref, keep_ref, near_ref, got_ref, wv_ref, ret_ref,
    value_ref, other_ref, own_ref, mixed_ref,
):
    rows, wide = got_ref.shape
    half = wide // 2
    block = 32
    base = place_ref[1] * rows
    live_total = place_ref[4].astype(F32)

    @pl.loop(0, rows // block)
    def _(i):
        start = pl.multiple_of(i * block, block)
        span = pl.ds(start, block)
        mixed = emb_ref[span, :].astype(F32) + (
            keep_ref[span, :] + near_ref[span, :].astype(F32) + got_ref[span, :].astype(F32)
        )
        mixed_ref[...] = mixed
        factor = row_factor(mixed)
        value = factor * jnp.sum(mixed * wv_ref[...].astype(F32), axis=-1, keepdims=True)
        row = place_ref[2] + base + start + lax.broadcasted_iota(jnp.int32, (block, 1), 0)
        gap = jnp.where(row < place_ref[3], value - ret_ref[span, :], F32(0.0)) / live_total
        lead = factor * gap
        pull = lead * factor * value / wide
        value_ref[span, :] = jnp.broadcast_to(value, (block, HEAD))
        for out, side in ((own_ref, place_ref[0]), (other_ref, 1 - place_ref[0])):
            columns = pl.ds(pl.multiple_of(side * half, half), half)
            part = mixed_ref[:, columns]
            out[span, :] = (lead * wv_ref[:, columns].astype(F32) - part * pull).astype(BF16)


def mixed_rows(place, embedded, keep, near, got, w_value, returns):
    rows, wide = got.shape
    return pl.pallas_call(
        mixed_kernel,
        in_specs=[SMEM] + [VMEM] * 6,
        out_specs=[VMEM] * 3,
        out_shape=[
            jax.ShapeDtypeStruct((rows, HEAD), F32),
            jax.ShapeDtypeStruct((rows, wide // 2), BF16),
            jax.ShapeDtypeStruct((rows, wide // 2), BF16),
        ],
        scratch_shapes=[pltpu.VMEM((32, wide), F32)],
        compiler_params=pltpu.CompilerParams(vmem_limit_bytes=LIMIT),
        cost_estimate=pl.CostEstimate(
            flops=10 * rows * wide, bytes_accessed=12 * rows * wide, transcendentals=0
        ),
        name="mixed_rows",
    )(place, embedded, keep, near, got, w_value, returns)


def gather_codes(size):
    codes, bit = [0], size // 2
    while bit >= 1:
        codes = codes + [code ^ bit for code in codes]
        bit //= 2
    return codes


def split_kernel(codes, index_ref, own_ref, got_ref, keep_ref, send_ref):
    block = own_ref.shape[0] // len(codes)
    side = len(codes) // 2
    for k, code in enumerate(codes):
        span = pl.ds(pl.multiple_of((index_ref[0] ^ code) * block, block), block)
        out = (keep_ref, send_ref)[k // side]
        at = k % side * block
        total = own_ref[span, :] + got_ref[span, :].astype(F32)
        out[at : at + block, :] = total.astype(out.dtype)


def split_sum(index, own, got, count):
    rows, wide = own.shape
    if (rows // count) % 16:
        got = got.astype(F32)
    send_type = BF16 if (rows // count) % 16 == 0 else F32
    return pl.pallas_call(
        functools.partial(split_kernel, gather_codes(count)),
        in_specs=[SMEM, VMEM, VMEM],
        out_specs=[VMEM] * 2,
        out_shape=[
            jax.ShapeDtypeStruct((rows // 2, wide), F32),
            jax.ShapeDtypeStruct((rows // 2, wide), send_type),
        ],
        compiler_params=pltpu.CompilerParams(vmem_limit_bytes=LIMIT),
        cost_estimate=pl.CostEstimate(
            flops=rows * wide, bytes_accessed=8 * rows * wide, transcendentals=0
        ),
        name="split_sum",
    )(index, own, got)


def assemble_kernel(codes, chunk, chunks, place_ref, *refs):
    parts = refs[: len(codes) * 2]
    out, got_ref, wide_ref, got_sems, sems = refs[-5:]
    block, strip = parts[0].shape
    got = start_copies([(part, got_ref.at[i]) for i, part in enumerate(parts)], got_sems)
    copies = []
    for side in range(2):
        for k, code in enumerate(codes):
            at = side * len(codes) + k
            row = pl.multiple_of((place_ref[5] ^ code) * block, block)
            column = pl.multiple_of(((place_ref[0] ^ side) * chunks + chunk) * strip, strip)
            got[at].wait()
            wide_ref[at] = got_ref[at].astype(F32)
            copy = pltpu.make_async_copy(
                wide_ref.at[at],
                out.at[pl.ds(row, block), pl.ds(column, strip)],
                sems.at[at],
            )
            copy.start()
            copies.append(copy)
    for copy in copies:
        copy.wait()


def assemble(place, parts, count, chunk, chunks, before):
    block, strip = parts[0].shape
    rows, wide = block * count, strip * 2 * chunks
    return pl.pallas_call(
        functools.partial(assemble_kernel, gather_codes(count), chunk, chunks),
        in_specs=[SMEM] + [ANY] * (len(parts) + len(before)),
        out_specs=ANY,
        out_shape=jax.ShapeDtypeStruct((rows, wide), F32),
        input_output_aliases={1 + len(parts): 0} if before else {},
        scratch_shapes=[
            pltpu.VMEM((len(parts), block, strip), BF16),
            pltpu.VMEM((len(parts), block, strip), F32),
            pltpu.SemaphoreType.DMA((len(parts),)),
            pltpu.SemaphoreType.DMA((len(parts),)),
        ],
        compiler_params=pltpu.CompilerParams(vmem_limit_bytes=LIMIT),
        cost_estimate=pl.CostEstimate(
            flops=rows * wide, bytes_accessed=6 * rows * wide, transcendentals=0
        ),
        name="assemble",
    )(place, *parts, *before)


def swap(block, axis, bit):
    size = lax.axis_size(axis)
    return lax.ppermute(block, axis, [(i, i ^ bit) for i in range(size)])


def gather_blocks(block, axis, late=None):
    blocks, bit = [block], lax.axis_size(axis) // 2
    while bit >= 1:
        sources = blocks if bit > 1 or late is None else [late] + blocks[1:]
        blocks = blocks + [swap(item, axis, bit) for item in sources]
        bit //= 2
    return blocks


def gather_parts(part):
    far = swap(part, "mdl", 2)
    return [part, swap(part, "mdl", 1), far, swap(far, "mdl", 1)], far


def product(left, right):
    return jnp.einsum("rh,rd->hd", left, right, preferred_element_type=F32)


def halve(keep, got):
    total = keep + got.astype(F32)
    side = total.shape[0] // 2
    return total[:side], total[side:].astype(BF16)


def on_device(
    obs,
    a_query,
    a_keyval,
    a_out,
    w_policy,
    c_in,
    c_query,
    c_keyval,
    c_out,
    w_value,
    actions,
    advantages,
    old_logp,
    returns,
    robot_count,
):
    row_count = obs.shape[1]
    batch_index = lax.axis_index("sec")
    rep_index = lax.axis_index("rep")
    rep_count = lax.axis_size("rep")
    robot_total = robot_count[batch_index]
    live_sum = jnp.sum(robot_count)
    live_total = live_sum.astype(F32)
    first_row = rep_index * row_count
    live_mask = first_row + lax.iota(jnp.int32, row_count) < robot_total
    mdl_count = lax.axis_size("mdl")
    assert mdl_count == 4 and lax.axis_size("sec") == 2
    mdl_index = lax.axis_index("mdl")
    value_rows = row_count // mdl_count
    score_scale = HEAD ** (-0.5) * LOG2E
    rep_place = rep_index.reshape(1).astype(jnp.int32)

    place = jnp.stack(
        [batch_index, mdl_index, first_row, robot_total, live_sum, rep_index]
        + [
            jnp.clip(robot_total - (rep_index ^ code) * row_count, 0, row_count)
            for code in gather_codes(rep_count)
        ]
    ).astype(jnp.int32)

    obs_in = obs[0]
    keyval, factor_a = first_projection(obs_in, a_keyval)
    a_far = swap(a_out, "mdl", 2)
    queries = query_projection(obs_in, a_query, factor_a, score_scale)
    late_keyval, queries = tied(keyval, queries)
    pieces_k = gather_blocks(keyval, "rep", late_keyval)
    state = attend_call(queries, pieces_k[:-1], 0, place, [])
    attended = attend_call(queries, pieces_k[-1:], rep_count - 1, place, state)
    attended, a_far = tied(attended, a_far)
    attended_far = swap(attended, "mdl", 2)
    attended_near = swap(attended, "mdl", 1)
    near_sum = near_rows(obs_in, [attended, attended_near], [a_out, swap(a_out, "mdl", 1)])
    attended_far, near_sum = tied(attended_far, near_sum)
    hidden, embed_part = hidden_rows(
        near_sum,
        [attended_far, swap(attended_far, "mdl", 1)],
        [a_far, swap(a_far, "mdl", 1)],
        c_in,
    )

    embed_parts, _ = gather_parts(embed_part)
    critic_keyval, factor_c, embedded = join_rows(place, embed_parts, c_keyval)
    critic_queries = (dot(embedded, c_query) * (factor_c[:, :1] * score_scale)).astype(BF16)

    late_hidden, critic_keyval = tied(hidden, critic_keyval)
    source = late_hidden.astype(F32)
    factor_h = row_factor(source)
    late_keyval, factor_h = tied(critic_keyval, factor_h)
    pieces_c = gather_blocks(critic_keyval, "rep", late_keyval)
    logits = dot(late_hidden, w_policy) * factor_h
    log_probs = jax.nn.log_softmax(logits, axis=-1)
    onehot = (
        actions[0][:, None] == lax.broadcasted_iota(jnp.int32, logits.shape, 1)
    ).astype(F32)
    chosen = jnp.sum(onehot * log_probs, axis=-1)
    prob_ratio = jnp.exp(chosen - old_logp[0])
    plain_term = prob_ratio * advantages[0]
    bounded = jnp.clip(prob_ratio, 1.0 - clip_range, 1.0 + clip_range) * advantages[0]
    slope = jnp.where(live_mask & (plain_term <= bounded), -plain_term / live_total, F32(0.0))
    dlogits = slope[:, None] * (onehot - jnp.exp(log_probs))
    along = jnp.sum(dlogits * logits, axis=-1, keepdims=True) / source.shape[1]
    dnormed = dot(dlogits.astype(BF16), w_policy.T)
    dhidden = (factor_h * (dnormed - source * (factor_h * along))).astype(BF16)
    half_a = dhidden.shape[1] // 2
    got_a = swap(
        product(attended, lax.dynamic_slice_in_dim(dhidden, (1 - batch_index) * half_a, half_a, 1))
        .astype(BF16),
        "sec",
        1,
    )
    own_a = product(attended, lax.dynamic_slice_in_dim(dhidden, batch_index * half_a, half_a, 1))

    wide = w_value.shape[0]
    target = lax.dynamic_slice_in_dim(returns[0], mdl_index * value_rows, value_rows, 0)
    emb_mine = lax.dynamic_slice_in_dim(embedded, mdl_index * value_rows, value_rows, 0)
    critic_queries, own_a, w_row, target, emb_mine = tied(
        critic_queries,
        own_a,
        w_value.reshape(1, wide),
        target.reshape(value_rows, 1),
        emb_mine,
    )
    state_c = attend_call(critic_queries, pieces_c[:-1], 0, place, [])
    *state_c, got_a, pieces_c[-1] = tied(*state_c, got_a, pieces_c[-1])
    keep_a, send_a = split_sum(rep_place, own_a, got_a, rep_count)
    *state_c, send_a = tied(*state_c, send_a)
    moved_a = swap(send_a.astype(BF16), "rep", 1)
    critic_attended = attend_call(critic_queries, pieces_c[-1:], rep_count - 1, place, state_c)

    send_m, keep_m, att_rows = part_rows(place, critic_attended, c_out)
    near_m = swap(send_m, "mdl", 1)
    near_m, moved_a = tied(near_m, moved_a)
    bit = 2
    while bit < rep_count:
        keep_a, send_a = halve(keep_a, moved_a)
        moved_a = swap(send_a, "rep", bit)
        bit *= 2
    send_y = (keep_m[value_rows:] + near_m[value_rows:].astype(F32)).astype(BF16)
    got_y = swap(send_y, "mdl", 2)
    att_there = swap(critic_attended, "sec", 1)
    mine_a = gather_blocks((keep_a + moved_a.astype(F32)).astype(BF16), "rep")
    got_y, *mine_a[1:-1] = tied(got_y, *mine_a[1:-1])
    value_wide, d_other, d_own = mixed_rows(
        place, emb_mine, keep_m, near_m, got_y, w_row, target
    )

    d_there = swap(d_other, "sec", 1)
    d_far = swap(d_own, "mdl", 2)
    there_far = swap(d_other, ("sec", "mdl"), mdl_count | 2)
    d_far, mine_a[-1] = tied(d_far, mine_a[-1])
    own_rows = jnp.concatenate(
        [d_own, d_far, swap(d_own, "mdl", 1), swap(d_far, "mdl", 1)], axis=0
    )
    there_rows = jnp.concatenate(
        [d_there, there_far, swap(d_there, "mdl", 1), swap(there_far, "mdl", 1)], axis=0
    )
    att_there = jnp.concatenate(
        [
            lax.dynamic_slice_in_dim(att_there, (mdl_index ^ code) * value_rows, value_rows, 0)
            for code in ROWS
        ],
        axis=0,
    )
    value_part, there_rows = tied(value_wide[:, 0], there_rows)
    theirs_a = [swap(block, "sec", 1) for block in mine_a]
    actor_summed = assemble(place, mine_a + theirs_a, rep_count, 0, 1, [])

    strip = d_own.shape[1] // CHUNKS
    chunks = []
    for c in range(CHUNKS):
        span = slice(c * strip, (c + 1) * strip)
        keep, send = split_sum(
            rep_place,
            product(att_rows, own_rows[:, span]),
            product(att_there, there_rows[:, span]),
            rep_count,
        )
        chunks.append([keep, [swap(send.astype(BF16), "rep", 1)], [], [], []])
    levels = rep_count.bit_length() - 1
    for tick in range(2 * levels + CHUNKS - 1):
        turn = [c for c in range(CHUNKS) if 0 <= tick - c < 2 * levels]
        waited = [item for c in turn for item in chunks[c][1] + chunks[c][3]]
        extra = []
        if tick == 0:
            extra = [chunks[c][0] for c in range(1, CHUNKS)] + theirs_a
        if tick == levels:
            extra = [actor_summed]
        outs = list(tied(*waited, *extra))
        if tick == 0:
            for c in range(1, CHUNKS):
                chunks[c][0] = outs[len(waited) + c - 1]
        if tick == levels:
            actor_summed = outs[-1]
        for c in turn:
            keep, pending, mine, crossing, theirs = chunks[c]
            arrived, outs = outs[: len(pending)], outs[len(pending) :]
            crossed, outs = outs[: len(crossing)], outs[len(crossing) :]
            theirs = theirs + crossed
            level = tick - c + 1
            if level < levels:
                keep, send = halve(keep, arrived[0])
                pending = [swap(send, "rep", 1 << level)]
            else:
                fresh = arrived
                if level == levels:
                    fresh = [(keep + arrived[0].astype(F32)).astype(BF16)]
                mine = mine + fresh
                crossing = [swap(block, "sec", 1) for block in fresh]
                bit = rep_count >> (level - levels + 1)
                pending = [swap(block, "rep", bit) for block in mine] if bit else []
            chunks[c] = [keep, pending, mine, crossing, theirs]
    result = []
    for c in range(CHUNKS):
        _, _, mine, crossing, theirs = chunks[c]
        result = [assemble(place, mine + theirs + crossing, rep_count, c, CHUNKS, result)]

    return (value_part[None, :], actor_summed, result[0])


def solution(mesh):
    return jax.shard_map(
        on_device,
        mesh=mesh,
        in_specs=(
            P("sec", "rep", None),
            P(None, "mdl"),
            P(None, None, "mdl"),
            P("mdl", None),
            P(),
            P(None, "mdl"),
            P(None, "mdl"),
            P(None, None, "mdl"),
            P("mdl", None),
            P(),
            P("sec", "rep"),
            P("sec", "rep"),
            P("sec", "rep"),
            P("sec", "rep"),
            P(),
        ),
        out_specs=(P("sec", ("rep", "mdl")), P("mdl", None), P("mdl", None)),
        check_vma=False,
    )
```

```python
import functools
import math

import jax
import jax.numpy as jnp
from jax import lax
from jax.experimental import pallas as pl
from jax.experimental.pallas import tpu as pltpu
from jax.sharding import PartitionSpec as P

HEAD = 128
epsilon = 1e-05
clip_range = 0.2
masked_score = -1e30
LOG2E = 1.4426950408889634
F32 = jnp.float32
BF16 = jnp.bfloat16
CHUNKS = 2
TABLE = 6
ROWS = (0, 2, 1, 3)
LIMIT = 40 * 2**20
HIGH = 56 * 2**20
VMEM = pl.BlockSpec(memory_space=pltpu.VMEM)
SMEM = pl.BlockSpec(memory_space=pltpu.SMEM)
ANY = pl.BlockSpec(memory_space=pl.ANY)
HBM = pl.BlockSpec(memory_space=pltpu.HBM)


def dot(a, b):
    return jnp.dot(a, b, preferred_element_type=F32)


def tied(*items):
    return lax.optimization_barrier(items)


def row_factor(source):
    return lax.rsqrt(jnp.mean(source * source, axis=-1, keepdims=True) + epsilon)


def start_copies(pairs, sems):
    copies = [
        pltpu.make_async_copy(source, target, sems.at[i])
        for i, (source, target) in enumerate(pairs)
    ]
    for copy in copies:
        copy.start()
    return copies


def first_kernel(obs_hbm, w_hbm, kv_ref, factor_ref, obs_ref, w_ref, sems):
    rows, depth = obs_ref.shape
    width = w_hbm.shape[2]
    block = rows // 2
    spans = [slice(i * block, (i + 1) * block) for i in range(2)]
    copies = start_copies(
        [(w_hbm.at[c], w_ref.at[:, c * width : (c + 1) * width]) for c in range(2)]
        + [(obs_hbm.at[span], obs_ref.at[span]) for span in spans],
        sems,
    )
    for i, span in enumerate(spans):
        copies[2 + i].wait()
        part = obs_ref[span, :]
        factor = row_factor(part.astype(F32))
        if i == 0:
            copies[0].wait()
            copies[1].wait()
        both = dot(part, w_ref[...]) * factor
        kv_ref[0, span, :] = both[:, :width].astype(BF16)
        kv_ref[1, span, :] = both[:, width:].astype(BF16)
        factor_ref[span, :] = jnp.broadcast_to(factor, (block, HEAD))


def first_projection(obs, w_keyval):
    rows, depth = obs.shape
    width = w_keyval.shape[2]
    return pl.pallas_call(
        first_kernel,
        in_specs=[HBM] * 2,
        out_specs=[VMEM] * 2,
        out_shape=[
            jax.ShapeDtypeStruct((2, rows, width), BF16),
            jax.ShapeDtypeStruct((rows, HEAD), F32),
        ],
        scratch_shapes=[
            pltpu.VMEM((rows, depth), BF16),
            pltpu.VMEM((depth, 2 * width), BF16),
            pltpu.SemaphoreType.DMA((4,)),
        ],
        compiler_params=pltpu.CompilerParams(vmem_limit_bytes=HIGH),
        cost_estimate=pl.CostEstimate(
            flops=4 * rows * depth * width, bytes_accessed=2 * rows * depth, transcendentals=0
        ),
        name="first_projection",
    )(obs, w_keyval)


def query_kernel(scale, obs_hbm, w_hbm, factor_ref, q_ref, obs_ref, w_ref, sems):
    for copy in start_copies([(w_hbm, w_ref), (obs_hbm, obs_ref)], sems):
        copy.wait()
    q_ref[...] = (dot(obs_ref[...], w_ref[...]) * (factor_ref[:, :1] * scale)).astype(BF16)


def query_projection(obs, w_query, factor, scale):
    rows, depth = obs.shape
    width = w_query.shape[1]
    return pl.pallas_call(
        functools.partial(query_kernel, scale),
        in_specs=[HBM, HBM, VMEM],
        out_specs=VMEM,
        out_shape=jax.ShapeDtypeStruct((rows, width), BF16),
        scratch_shapes=[
            pltpu.VMEM((rows, depth), BF16),
            pltpu.VMEM((depth, width), BF16),
            pltpu.SemaphoreType.DMA((2,)),
        ],
        compiler_params=pltpu.CompilerParams(vmem_limit_bytes=LIMIT),
        cost_estimate=pl.CostEstimate(
            flops=2 * rows * depth * width, bytes_accessed=2 * rows * depth, transcendentals=0
        ),
        name="query_projection",
    )(obs, w_query, factor)


def attend_blocks(groups, units, first, left_ref, q_ref, kv_refs):
    def fetch(head, span):
        kv_head = head // groups
        columns = slice(kv_head * HEAD, (kv_head + 1) * HEAD)
        query = q_ref[span, head * HEAD : (head + 1) * HEAD]
        lane = lax.broadcasted_iota(jnp.int32, query.shape, 1)
        query = jnp.concatenate([query, (lane == 0).astype(BF16)], axis=1)
        scores = []
        for p, ref in enumerate(kv_refs):
            keys = ref[0, :, columns]
            key = lax.broadcasted_iota(jnp.int32, keys.shape, 0)
            lane = lax.broadcasted_iota(jnp.int32, keys.shape, 1)
            dead = (key >= left_ref[first + p]) & (lane == 0)
            bias = jnp.where(dead, F32(masked_score), F32(0.0)).astype(BF16)
            keys = jnp.concatenate([keys, bias], axis=1)
            scores.append(
                lax.dot_general(
                    query, keys, (((1,), (1,)), ((), ())), preferred_element_type=F32
                )
            )
        return scores

    def values(head, p):
        kv_head = head // groups
        vals = kv_refs[p][1, :, kv_head * HEAD : (kv_head + 1) * HEAD]
        return jnp.concatenate([vals, jnp.ones_like(vals)], axis=1)

    ahead = fetch(*units[0])
    for i, (head, span) in enumerate(units):
        scores = ahead
        if i + 1 < len(units):
            ahead = fetch(*units[i + 1])
        yield head, span, scores, functools.partial(values, head)


def weigh(scores, top, values):
    total = None
    for p, part in enumerate(scores):
        both = dot(jnp.exp2(part - top).astype(BF16), values(p))
        total = both if total is None else total + both
    return total


def highest(scores):
    return functools.reduce(
        jnp.maximum, [jnp.max(part, axis=-1, keepdims=True) for part in scores]
    )


def open_kernel(groups, units, first, left_ref, q_ref, *refs):
    *kv_refs, wide_ref, top_ref = refs
    for head, span, scores, values in attend_blocks(
        groups, units, first, left_ref, q_ref, kv_refs
    ):
        top = highest(scores)
        wide_ref[span, head * 2 * HEAD : (head + 1) * 2 * HEAD] = weigh(scores, top, values)
        top_ref[span, head * HEAD : (head + 1) * HEAD] = jnp.broadcast_to(
            top, (top.shape[0], HEAD)
        )


def close_kernel(groups, units, first, left_ref, q_ref, wide_ref, top_ref, *refs):
    *kv_refs, o_ref = refs
    for head, span, scores, values in attend_blocks(
        groups, units, first, left_ref, q_ref, kv_refs
    ):
        before = top_ref[span, head * HEAD : head * HEAD + 1]
        top = jnp.maximum(before, highest(scores))
        wide = wide_ref[span, head * 2 * HEAD : (head + 1) * 2 * HEAD]
        wide = wide * jnp.exp2(before - top) + weigh(scores, top, values)
        o_ref[span, head * HEAD : (head + 1) * HEAD] = (
            wide[:, :HEAD] / wide[:, HEAD:]
        ).astype(BF16)


def attend_call(queries, pieces, first, place, state):
    rows, width = queries.shape
    heads = width // HEAD
    groups = heads // (pieces[0].shape[2] // HEAD)
    block = min(rows, 256)
    units = [
        (head, slice(i, i + block)) for head in range(heads) for i in range(0, rows, block)
    ]
    count = len(pieces) * pieces[0].shape[1]
    weight = 1 if state else 24
    if state:
        body, name = close_kernel, "attend_close"
        out = jax.ShapeDtypeStruct((rows, width), BF16)
    else:
        body, name = open_kernel, "attend_open"
        out = [
            jax.ShapeDtypeStruct((rows, 2 * width), F32),
            jax.ShapeDtypeStruct((rows, width), F32),
        ]
    return pl.pallas_call(
        functools.partial(body, groups, units, TABLE + first),
        in_specs=[SMEM] + [VMEM] * (1 + len(state) + len(pieces)),
        out_specs=VMEM if state else [VMEM] * 2,
        out_shape=out,
        compiler_params=pltpu.CompilerParams(vmem_limit_bytes=LIMIT),
        cost_estimate=pl.CostEstimate(
            flops=weight * rows * count * width,
            bytes_accessed=4 * rows * width,
            transcendentals=rows * count,
        ),
        name=name,
    )(place, queries, *state, *pieces)


def near_kernel(obs_hbm, t0, t1, w0, w1, sum_ref, obs_ref, w_ref, sems):
    inner, depth = w0.shape
    tile = depth // 3
    pairs = [(obs_hbm, obs_ref), (w0, w_ref.at[:inner]), (w1, w_ref.at[inner:])]
    for copy in start_copies(pairs, sems):
        copy.wait()
    for i in range(3):
        strip = slice(i * tile, (i + 1) * tile)
        parts = jnp.concatenate([t0[...], t1[...]], axis=1)
        sum_ref[:, strip] = obs_ref[:, strip].astype(F32) + dot(parts, w_ref[:, strip])


def near_rows(obs, parts, weights):
    rows, depth = obs.shape
    inner = weights[0].shape[0]
    return pl.pallas_call(
        near_kernel,
        in_specs=[HBM] + [VMEM] * 2 + [HBM, ANY],
        out_specs=VMEM,
        out_shape=jax.ShapeDtypeStruct((rows, depth), F32),
        scratch_shapes=[
            pltpu.VMEM((rows, depth), BF16),
            pltpu.VMEM((2 * inner, depth), BF16),
            pltpu.SemaphoreType.DMA((3,)),
        ],
        compiler_params=pltpu.CompilerParams(vmem_limit_bytes=LIMIT),
        cost_estimate=pl.CostEstimate(
            flops=4 * rows * depth * inner, bytes_accessed=4 * depth * inner, transcendentals=0
        ),
        name="near_rows",
    )(obs, *parts, *weights)


def hidden_kernel(sum_ref, t2, t3, w2, w3, c_hbm, o_ref, emb_ref, w_ref, c_ref, sems):
    inner, depth = w2.shape
    tile = depth // 3
    copies = start_copies(
        [(w2, w_ref.at[:inner]), (w3, w_ref.at[inner:]), (c_hbm, c_ref)], sems
    )
    copies[0].wait()
    copies[1].wait()
    for i in range(3):
        strip = slice(i * tile, (i + 1) * tile)
        parts = jnp.concatenate([t2[...], t3[...]], axis=1)
        o_ref[:, strip] = (sum_ref[:, strip] + dot(parts, w_ref[:, strip])).astype(BF16)
    copies[2].wait()
    emb_ref[...] = dot(o_ref[...], c_ref[...]).astype(BF16)


def hidden_rows(near_sum, parts, weights, c_in):
    rows, depth = near_sum.shape
    inner = weights[0].shape[0]
    width = c_in.shape[1]
    return pl.pallas_call(
        hidden_kernel,
        in_specs=[VMEM] * 3 + [ANY] * 2 + [HBM],
        out_specs=[VMEM] * 2,
        out_shape=[
            jax.ShapeDtypeStruct((rows, depth), BF16),
            jax.ShapeDtypeStruct((rows, width), BF16),
        ],
        scratch_shapes=[
            pltpu.VMEM((2 * inner, depth), BF16),
            pltpu.VMEM((depth, width), BF16),
            pltpu.SemaphoreType.DMA((3,)),
        ],
        compiler_params=pltpu.CompilerParams(vmem_limit_bytes=LIMIT),
        cost_estimate=pl.CostEstimate(
            flops=8 * rows * depth * inner, bytes_accessed=8 * depth * inner, transcendentals=0
        ),
        name="hidden_rows",
    )(near_sum, *parts, *weights, c_in)


def join_kernel(place_ref, e0, e1, e2, e3, wkv_any, kv_ref, factor_ref, emb_ref, wkv_ref, sems):
    rows, wide = emb_ref.shape
    width = wkv_any.shape[2]
    strip = e0.shape[1]
    copies = start_copies(
        [(wkv_any.at[c], wkv_ref.at[:, c * width : (c + 1) * width]) for c in range(2)], sems
    )
    starts = [pl.multiple_of((place_ref[1] ^ code) * strip, strip) for code in range(4)]
    parts = (e0, e1, e2, e3)
    for copy in copies:
        copy.wait()
    block = rows // 2
    for i in range(2):
        span = slice(i * block, (i + 1) * block)
        square, both = 0.0, 0.0
        for part, start in zip(parts, starts):
            emb = part[span, :]
            wide_emb = emb.astype(F32)
            square = square + jnp.sum(wide_emb * wide_emb, axis=-1, keepdims=True)
            both = both + dot(emb, wkv_ref[pl.ds(start, strip), :])
            emb_ref[span, pl.ds(start, strip)] = emb
        factor = lax.rsqrt(square / wide + epsilon)
        both = both * factor
        kv_ref[0, span, :] = both[:, :width].astype(BF16)
        kv_ref[1, span, :] = both[:, width:].astype(BF16)
        factor_ref[span, :] = jnp.broadcast_to(factor, (block, HEAD))


def join_rows(place, parts, w_keyval):
    rows, strip = parts[0].shape
    wide = 4 * strip
    width = w_keyval.shape[2]
    return pl.pallas_call(
        join_kernel,
        in_specs=[SMEM] + [VMEM] * 4 + [HBM],
        out_specs=[VMEM] * 3,
        out_shape=[
            jax.ShapeDtypeStruct((2, rows, width), BF16),
            jax.ShapeDtypeStruct((rows, HEAD), F32),
            jax.ShapeDtypeStruct((rows, wide), BF16),
        ],
        scratch_shapes=[pltpu.VMEM((wide, 2 * width), BF16), pltpu.SemaphoreType.DMA((2,))],
        compiler_params=pltpu.CompilerParams(vmem_limit_bytes=LIMIT),
        cost_estimate=pl.CostEstimate(
            flops=4 * rows * wide * width, bytes_accessed=4 * rows * wide, transcendentals=0
        ),
        name="join_rows",
    )(place, *parts, w_keyval)


def part_kernel(place_ref, att_ref, c_hbm, send_ref, keep_ref, order_ref, c_ref, sems):
    rows, inner = att_ref.shape
    wide = c_ref.shape[1]
    block = rows // 4
    half = inner // 2
    spans = [slice(i * half, (i + 1) * half) for i in range(2)]
    copies = start_copies([(c_hbm.at[span], c_ref.at[span]) for span in spans], sems)
    for at, code in enumerate(ROWS):
        start = pl.multiple_of((place_ref[1] ^ code) * block, block)
        order_ref[at * block : (at + 1) * block, :] = att_ref[pl.ds(start, block), :]
    for copy in copies:
        copy.wait()
    tile = 512
    for out, source in ((send_ref, order_ref[2 * block :, :]), (keep_ref, order_ref[: 2 * block, :])):
        for j in range(wide // tile):
            columns = slice(j * tile, (j + 1) * tile)
            out[:, columns] = dot(source, c_ref[:, columns]).astype(out.dtype)


def part_rows(place, attended, c_out):
    rows, inner = attended.shape
    wide = c_out.shape[1]
    return pl.pallas_call(
        part_kernel,
        in_specs=[SMEM, VMEM, HBM],
        out_specs=[VMEM] * 3,
        out_shape=[
            jax.ShapeDtypeStruct((rows // 2, wide), BF16),
            jax.ShapeDtypeStruct((rows // 2, wide), F32),
            jax.ShapeDtypeStruct((rows, inner), BF16),
        ],
        scratch_shapes=[pltpu.VMEM((inner, wide), BF16), pltpu.SemaphoreType.DMA((2,))],
        compiler_params=pltpu.CompilerParams(vmem_limit_bytes=LIMIT),
        cost_estimate=pl.CostEstimate(
            flops=2 * rows * wide * inner, bytes_accessed=8 * wide * inner, transcendentals=0
        ),
        name="part_rows",
    )(place, attended, c_out)


def mixed_kernel(
    place_ref, emb_ref, keep_ref, near_ref, got_ref, wv_ref, ret_ref,
    value_ref, other_ref, own_ref, mixed_ref,
):
    rows, wide = got_ref.shape
    half = wide // 2
    block = 32
    base = place_ref[1] * rows
    live_total = place_ref[4].astype(F32)

    @pl.loop(0, rows // block)
    def _(i):
        start = pl.multiple_of(i * block, block)
        span = pl.ds(start, block)
        mixed = emb_ref[span, :].astype(F32) + (
            keep_ref[span, :] + near_ref[span, :].astype(F32) + got_ref[span, :].astype(F32)
        )
        mixed_ref[...] = mixed
        factor = row_factor(mixed)
        value = factor * jnp.sum(mixed * wv_ref[...].astype(F32), axis=-1, keepdims=True)
        row = place_ref[2] + base + start + lax.broadcasted_iota(jnp.int32, (block, 1), 0)
        gap = jnp.where(row < place_ref[3], value - ret_ref[span, :], F32(0.0)) / live_total
        lead = factor * gap
        pull = lead * factor * value / wide
        value_ref[span, :] = jnp.broadcast_to(value, (block, HEAD))
        for out, side in ((own_ref, place_ref[0]), (other_ref, 1 - place_ref[0])):
            columns = pl.ds(pl.multiple_of(side * half, half), half)
            part = mixed_ref[:, columns]
            out[span, :] = (lead * wv_ref[:, columns].astype(F32) - part * pull).astype(BF16)


def mixed_rows(place, embedded, keep, near, got, w_value, returns):
    rows, wide = got.shape
    return pl.pallas_call(
        mixed_kernel,
        in_specs=[SMEM] + [VMEM] * 6,
        out_specs=[VMEM] * 3,
        out_shape=[
            jax.ShapeDtypeStruct((rows, HEAD), F32),
            jax.ShapeDtypeStruct((rows, wide // 2), BF16),
            jax.ShapeDtypeStruct((rows, wide // 2), BF16),
        ],
        scratch_shapes=[pltpu.VMEM((32, wide), F32)],
        compiler_params=pltpu.CompilerParams(vmem_limit_bytes=LIMIT),
        cost_estimate=pl.CostEstimate(
            flops=10 * rows * wide, bytes_accessed=12 * rows * wide, transcendentals=0
        ),
        name="mixed_rows",
    )(place, embedded, keep, near, got, w_value, returns)


def gather_codes(size):
    codes, bit = [0], size // 2
    while bit >= 1:
        codes = codes + [code ^ bit for code in codes]
        bit //= 2
    return codes


def split_kernel(codes, index_ref, own_ref, got_ref, keep_ref, send_ref):
    block = own_ref.shape[0] // len(codes)
    side = len(codes) // 2
    for k, code in enumerate(codes):
        span = pl.ds(pl.multiple_of((index_ref[0] ^ code) * block, block), block)
        out = (keep_ref, send_ref)[k // side]
        at = k % side * block
        total = own_ref[span, :] + got_ref[span, :].astype(F32)
        out[at : at + block, :] = total.astype(out.dtype)


def split_sum(index, own, got, count):
    rows, wide = own.shape
    if (rows // count) % 16:
        got = got.astype(F32)
    send_type = BF16 if (rows // count) % 16 == 0 else F32
    return pl.pallas_call(
        functools.partial(split_kernel, gather_codes(count)),
        in_specs=[SMEM, VMEM, VMEM],
        out_specs=[VMEM] * 2,
        out_shape=[
            jax.ShapeDtypeStruct((rows // 2, wide), F32),
            jax.ShapeDtypeStruct((rows // 2, wide), send_type),
        ],
        compiler_params=pltpu.CompilerParams(vmem_limit_bytes=LIMIT),
        cost_estimate=pl.CostEstimate(
            flops=rows * wide, bytes_accessed=8 * rows * wide, transcendentals=0
        ),
        name="split_sum",
    )(index, own, got)


def assemble_kernel(spots, chunks, place_ref, *refs):
    parts = refs[: len(spots)]
    out, got_ref, wide_ref, got_sems, sems = refs[-5:]
    block, strip = parts[0].shape
    got = start_copies([(part, got_ref.at[i]) for i, part in enumerate(parts)], got_sems)
    copies = []
    for i, (chunk, side, code) in enumerate(spots):
        row = pl.multiple_of((place_ref[5] ^ code) * block, block)
        column = pl.multiple_of(((place_ref[0] ^ side) * chunks + chunk) * strip, strip)
        got[i].wait()
        wide_ref[i] = got_ref[i].astype(F32)
        copy = pltpu.make_async_copy(
            wide_ref.at[i], out.at[pl.ds(row, block), pl.ds(column, strip)], sems.at[i]
        )
        copy.start()
        copies.append(copy)
    for copy in copies:
        copy.wait()


def assemble(place, parts, spots, count, chunks, before):
    block, strip = parts[0].shape
    rows, wide = block * count, strip * 2 * chunks
    return pl.pallas_call(
        functools.partial(assemble_kernel, spots, chunks),
        in_specs=[SMEM] + [ANY] * (len(parts) + len(before)),
        out_specs=ANY,
        out_shape=jax.ShapeDtypeStruct((rows, wide), F32),
        input_output_aliases={1 + len(parts): 0} if before else {},
        scratch_shapes=[
            pltpu.VMEM((len(parts), block, strip), BF16),
            pltpu.VMEM((len(parts), block, strip), F32),
            pltpu.SemaphoreType.DMA((len(parts),)),
            pltpu.SemaphoreType.DMA((len(parts),)),
        ],
        compiler_params=pltpu.CompilerParams(vmem_limit_bytes=LIMIT),
        cost_estimate=pl.CostEstimate(
            flops=rows * wide, bytes_accessed=6 * rows * wide, transcendentals=0
        ),
        name="assemble",
    )(place, *parts, *before)


def swap(block, axis, bit):
    size = lax.axis_size(axis)
    return lax.ppermute(block, axis, [(i, i ^ bit) for i in range(size)])


def gather_blocks(block, axis, late=None):
    blocks, bit = [block], lax.axis_size(axis) // 2
    while bit >= 1:
        sources = blocks if bit > 1 or late is None else [late] + blocks[1:]
        blocks = blocks + [swap(item, axis, bit) for item in sources]
        bit //= 2
    return blocks


def gather_parts(part):
    far = swap(part, "mdl", 2)
    return [part, swap(part, "mdl", 1), far, swap(far, "mdl", 1)], far


def product(left, right):
    return jnp.einsum("rh,rd->hd", left, right, preferred_element_type=F32)


def halve(keep, got):
    total = keep + got.astype(F32)
    side = total.shape[0] // 2
    return total[:side], total[side:].astype(BF16)


def on_device(
    obs,
    a_query,
    a_keyval,
    a_out,
    w_policy,
    c_in,
    c_query,
    c_keyval,
    c_out,
    w_value,
    actions,
    advantages,
    old_logp,
    returns,
    robot_count,
):
    row_count = obs.shape[1]
    batch_index = lax.axis_index("sec")
    rep_index = lax.axis_index("rep")
    rep_count = lax.axis_size("rep")
    robot_total = robot_count[batch_index]
    live_sum = jnp.sum(robot_count)
    live_total = live_sum.astype(F32)
    first_row = rep_index * row_count
    live_mask = first_row + lax.iota(jnp.int32, row_count) < robot_total
    mdl_count = lax.axis_size("mdl")
    assert mdl_count == 4 and lax.axis_size("sec") == 2
    mdl_index = lax.axis_index("mdl")
    value_rows = row_count // mdl_count
    score_scale = HEAD ** (-0.5) * LOG2E
    rep_place = rep_index.reshape(1).astype(jnp.int32)

    place = jnp.stack(
        [batch_index, mdl_index, first_row, robot_total, live_sum, rep_index]
        + [
            jnp.clip(robot_total - (rep_index ^ code) * row_count, 0, row_count)
            for code in gather_codes(rep_count)
        ]
    ).astype(jnp.int32)

    obs_in = obs[0]
    keyval, factor_a = first_projection(obs_in, a_keyval)
    a_far = swap(a_out, "mdl", 2)
    queries = query_projection(obs_in, a_query, factor_a, score_scale)
    late_keyval, queries = tied(keyval, queries)
    pieces_k = gather_blocks(keyval, "rep", late_keyval)
    state = attend_call(queries, pieces_k[:-1], 0, place, [])
    attended = attend_call(queries, pieces_k[-1:], rep_count - 1, place, state)
    attended, a_far = tied(attended, a_far)
    attended_far = swap(attended, "mdl", 2)
    attended_near = swap(attended, "mdl", 1)
    near_sum = near_rows(obs_in, [attended, attended_near], [a_out, swap(a_out, "mdl", 1)])
    attended_far, near_sum = tied(attended_far, near_sum)
    hidden, embed_part = hidden_rows(
        near_sum,
        [attended_far, swap(attended_far, "mdl", 1)],
        [a_far, swap(a_far, "mdl", 1)],
        c_in,
    )

    embed_parts, _ = gather_parts(embed_part)
    critic_keyval, factor_c, embedded = join_rows(place, embed_parts, c_keyval)
    critic_queries = (dot(embedded, c_query) * (factor_c[:, :1] * score_scale)).astype(BF16)

    late_hidden, critic_keyval = tied(hidden, critic_keyval)
    source = late_hidden.astype(F32)
    factor_h = row_factor(source)
    late_keyval, factor_h = tied(critic_keyval, factor_h)
    pieces_c = gather_blocks(critic_keyval, "rep", late_keyval)
    logits = dot(late_hidden, w_policy) * factor_h
    log_probs = jax.nn.log_softmax(logits, axis=-1)
    onehot = (
        actions[0][:, None] == lax.broadcasted_iota(jnp.int32, logits.shape, 1)
    ).astype(F32)
    chosen = jnp.sum(onehot * log_probs, axis=-1)
    prob_ratio = jnp.exp(chosen - old_logp[0])
    plain_term = prob_ratio * advantages[0]
    bounded = jnp.clip(prob_ratio, 1.0 - clip_range, 1.0 + clip_range) * advantages[0]
    slope = jnp.where(live_mask & (plain_term <= bounded), -plain_term / live_total, F32(0.0))
    dlogits = slope[:, None] * (onehot - jnp.exp(log_probs))
    along = jnp.sum(dlogits * logits, axis=-1, keepdims=True) / source.shape[1]
    dnormed = dot(dlogits.astype(BF16), w_policy.T)
    dhidden = (factor_h * (dnormed - source * (factor_h * along))).astype(BF16)
    half_a = dhidden.shape[1] // 2
    got_a = swap(
        product(attended, lax.dynamic_slice_in_dim(dhidden, (1 - batch_index) * half_a, half_a, 1))
        .astype(BF16),
        "sec",
        1,
    )
    own_a = product(attended, lax.dynamic_slice_in_dim(dhidden, batch_index * half_a, half_a, 1))

    wide = w_value.shape[0]
    target = lax.dynamic_slice_in_dim(returns[0], mdl_index * value_rows, value_rows, 0)
    emb_mine = lax.dynamic_slice_in_dim(embedded, mdl_index * value_rows, value_rows, 0)
    critic_queries, own_a, w_row, target, emb_mine = tied(
        critic_queries,
        own_a,
        w_value.reshape(1, wide),
        target.reshape(value_rows, 1),
        emb_mine,
    )
    state_c = attend_call(critic_queries, pieces_c[:-1], 0, place, [])
    *state_c, got_a, pieces_c[-1] = tied(*state_c, got_a, pieces_c[-1])
    keep_a, send_a = split_sum(rep_place, own_a, got_a, rep_count)
    *state_c, send_a = tied(*state_c, send_a)
    moved_a = swap(send_a.astype(BF16), "rep", 1)
    critic_attended = attend_call(critic_queries, pieces_c[-1:], rep_count - 1, place, state_c)

    send_m, keep_m, att_rows = part_rows(place, critic_attended, c_out)
    near_m = swap(send_m, "mdl", 1)
    send_y = (keep_m[value_rows:] + near_m[value_rows:].astype(F32)).astype(BF16)
    got_y = swap(send_y, "mdl", 2)
    att_there = swap(critic_attended, "sec", 1)
    got_y, moved_a = tied(got_y, moved_a)
    bit = 2
    while bit < rep_count:
        keep_a, send_a = halve(keep_a, moved_a)
        moved_a = swap(send_a, "rep", bit)
        bit *= 2
    value_wide, d_other, d_own = mixed_rows(
        place, emb_mine, keep_m, near_m, got_y, w_row, target
    )

    d_there = swap(d_other, "sec", 1)
    d_far = swap(d_own, "mdl", 2)
    there_far = swap(d_other, ("sec", "mdl"), mdl_count | 2)
    d_far, moved_a = tied(d_far, moved_a)
    mine_a = gather_blocks((keep_a + moved_a.astype(F32)).astype(BF16), "rep")
    d_there, *mine_a[1:-1] = tied(d_there, *mine_a[1:-1])
    own_rows = jnp.concatenate(
        [d_own, d_far, swap(d_own, "mdl", 1), swap(d_far, "mdl", 1)], axis=0
    )
    there_rows = jnp.concatenate(
        [d_there, there_far, swap(d_there, "mdl", 1), swap(there_far, "mdl", 1)], axis=0
    )
    att_there = jnp.concatenate(
        [
            lax.dynamic_slice_in_dim(att_there, (mdl_index ^ code) * value_rows, value_rows, 0)
            for code in ROWS
        ],
        axis=0,
    )
    value_part, there_rows = tied(value_wide[:, 0], there_rows)
    theirs_a = [swap(block, "sec", 1) for block in mine_a]
    codes = gather_codes(rep_count)
    spots = [(0, side, code) for side in range(2) for code in codes]
    actor_summed = assemble(place, mine_a + theirs_a, spots, rep_count, 1, [])

    strip = d_own.shape[1] // CHUNKS
    chunks = []
    for c in range(CHUNKS):
        span = slice(c * strip, (c + 1) * strip)
        keep, send = split_sum(
            rep_place,
            product(att_rows, own_rows[:, span]),
            product(att_there, there_rows[:, span]),
            rep_count,
        )
        chunks.append([keep, [swap(send.astype(BF16), "rep", 1)], [], [], []])
    levels = rep_count.bit_length() - 1
    for tick in range(2 * levels + CHUNKS - 1):
        turn = [c for c in range(CHUNKS) if 0 <= tick - c < 2 * levels]
        waited = [item for c in turn for item in chunks[c][1] + chunks[c][3]]
        extra = []
        if tick == 0:
            extra = [chunks[c][0] for c in range(1, CHUNKS)]
        if tick == 1:
            extra = mine_a[-1:]
        if tick == 2:
            extra = theirs_a
        if tick == 2 * levels - 1:
            extra = [actor_summed]
        if tick == 2 * levels + CHUNKS - 2:
            done = [
                (item, (c, side, code))
                for c in range(CHUNKS)
                for side in range(2)
                for item, code in zip(chunks[c][2 + 2 * side], codes)
            ]
            extra = [assemble(place, *zip(*done), rep_count, CHUNKS, [])]
        outs = list(tied(*waited, *extra))
        if tick == 0:
            for c in range(1, CHUNKS):
                chunks[c][0] = outs[len(waited) + c - 1]
        if tick == 2 * levels - 1:
            actor_summed = outs[-1]
        if tick == 2 * levels + CHUNKS - 2:
            result = outs[-1]
        for c in turn:
            keep, pending, mine, crossing, theirs = chunks[c]
            arrived, outs = outs[: len(pending)], outs[len(pending) :]
            crossed, outs = outs[: len(crossing)], outs[len(crossing) :]
            theirs = theirs + crossed
            level = tick - c + 1
            if level < levels:
                keep, send = halve(keep, arrived[0])
                pending = [swap(send, "rep", 1 << level)]
            else:
                fresh = arrived
                if level == levels:
                    fresh = [(keep + arrived[0].astype(F32)).astype(BF16)]
                mine = mine + fresh
                crossing = [swap(block, "sec", 1) for block in fresh]
                bit = rep_count >> (level - levels + 1)
                pending = [swap(block, "rep", bit) for block in mine] if bit else []
            chunks[c] = [keep, pending, mine, crossing, theirs]
    rest = [
        (item, (c, side, code))
        for c in range(CHUNKS)
        for side, group in enumerate((chunks[c][2], chunks[c][4] + chunks[c][3]))
        for item, code in zip(group, codes)
        if (c, side, code) not in [spot for _, spot in done]
    ]
    result = assemble(place, *zip(*rest), rep_count, CHUNKS, [result])

    return (value_part[None, :], actor_summed, result)


def solution(mesh):
    return jax.shard_map(
        on_device,
        mesh=mesh,
        in_specs=(
            P("sec", "rep", None),
            P(None, "mdl"),
            P(None, None, "mdl"),
            P("mdl", None),
            P(),
            P(None, "mdl"),
            P(None, "mdl"),
            P(None, None, "mdl"),
            P("mdl", None),
            P(),
            P("sec", "rep"),
            P("sec", "rep"),
            P("sec", "rep"),
            P("sec", "rep"),
            P(),
        ),
        out_specs=(P("sec", ("rep", "mdl")), P("mdl", None), P("mdl", None)),
        check_vma=False,
    )
```

```python
import functools
import math

import jax
import jax.numpy as jnp
from jax import lax
from jax.experimental import pallas as pl
from jax.experimental.pallas import tpu as pltpu
from jax.sharding import PartitionSpec as P

HEAD = 128
epsilon = 1e-05
clip_range = 0.2
masked_score = -1e30
LOG2E = 1.4426950408889634
F32 = jnp.float32
BF16 = jnp.bfloat16
CHUNKS = 2
TABLE = 6
ROWS = (0, 2, 1, 3)
LIMIT = 40 * 2**20
HIGH = 56 * 2**20
VMEM = pl.BlockSpec(memory_space=pltpu.VMEM)
SMEM = pl.BlockSpec(memory_space=pltpu.SMEM)
ANY = pl.BlockSpec(memory_space=pl.ANY)
HBM = pl.BlockSpec(memory_space=pltpu.HBM)


def dot(a, b):
    return jnp.dot(a, b, preferred_element_type=F32)


def tied(*items):
    return lax.optimization_barrier(items)


def row_factor(source):
    return lax.rsqrt(jnp.mean(source * source, axis=-1, keepdims=True) + epsilon)


def start_copies(pairs, sems):
    copies = [
        pltpu.make_async_copy(source, target, sems.at[i])
        for i, (source, target) in enumerate(pairs)
    ]
    for copy in copies:
        copy.start()
    return copies


def first_kernel(obs_hbm, w_hbm, kv_ref, factor_ref, obs_ref, w_ref, sems):
    rows, depth = obs_ref.shape
    width = w_hbm.shape[2]
    block = rows // 2
    spans = [slice(i * block, (i + 1) * block) for i in range(2)]
    copies = start_copies(
        [(w_hbm.at[c], w_ref.at[:, c * width : (c + 1) * width]) for c in range(2)]
        + [(obs_hbm.at[span], obs_ref.at[span]) for span in spans],
        sems,
    )
    for i, span in enumerate(spans):
        copies[2 + i].wait()
        part = obs_ref[span, :]
        factor = row_factor(part.astype(F32))
        if i == 0:
            copies[0].wait()
            copies[1].wait()
        both = dot(part, w_ref[...]) * factor
        kv_ref[0, span, :] = both[:, :width].astype(BF16)
        kv_ref[1, span, :] = both[:, width:].astype(BF16)
        factor_ref[span, :] = jnp.broadcast_to(factor, (block, HEAD))


def first_projection(obs, w_keyval):
    rows, depth = obs.shape
    width = w_keyval.shape[2]
    return pl.pallas_call(
        first_kernel,
        in_specs=[HBM] * 2,
        out_specs=[VMEM] * 2,
        out_shape=[
            jax.ShapeDtypeStruct((2, rows, width), BF16),
            jax.ShapeDtypeStruct((rows, HEAD), F32),
        ],
        scratch_shapes=[
            pltpu.VMEM((rows, depth), BF16),
            pltpu.VMEM((depth, 2 * width), BF16),
            pltpu.SemaphoreType.DMA((4,)),
        ],
        compiler_params=pltpu.CompilerParams(vmem_limit_bytes=HIGH),
        cost_estimate=pl.CostEstimate(
            flops=4 * rows * depth * width, bytes_accessed=2 * rows * depth, transcendentals=0
        ),
        name="first_projection",
    )(obs, w_keyval)


def query_kernel(scale, obs_hbm, w_hbm, factor_ref, q_ref, obs_ref, w_ref, sems):
    for copy in start_copies([(w_hbm, w_ref), (obs_hbm, obs_ref)], sems):
        copy.wait()
    q_ref[...] = (dot(obs_ref[...], w_ref[...]) * (factor_ref[:, :1] * scale)).astype(BF16)


def query_projection(obs, w_query, factor, scale):
    rows, depth = obs.shape
    width = w_query.shape[1]
    return pl.pallas_call(
        functools.partial(query_kernel, scale),
        in_specs=[HBM, HBM, VMEM],
        out_specs=VMEM,
        out_shape=jax.ShapeDtypeStruct((rows, width), BF16),
        scratch_shapes=[
            pltpu.VMEM((rows, depth), BF16),
            pltpu.VMEM((depth, width), BF16),
            pltpu.SemaphoreType.DMA((2,)),
        ],
        compiler_params=pltpu.CompilerParams(vmem_limit_bytes=LIMIT),
        cost_estimate=pl.CostEstimate(
            flops=2 * rows * depth * width, bytes_accessed=2 * rows * depth, transcendentals=0
        ),
        name="query_projection",
    )(obs, w_query, factor)


def attend_blocks(groups, units, first, left_ref, q_ref, kv_refs):
    def fetch(head, span):
        kv_head = head // groups
        columns = slice(kv_head * HEAD, (kv_head + 1) * HEAD)
        query = q_ref[span, head * HEAD : (head + 1) * HEAD]
        lane = lax.broadcasted_iota(jnp.int32, query.shape, 1)
        query = jnp.concatenate([query, (lane == 0).astype(BF16)], axis=1)
        scores = []
        for p, ref in enumerate(kv_refs):
            keys = ref[0, :, columns]
            key = lax.broadcasted_iota(jnp.int32, keys.shape, 0)
            lane = lax.broadcasted_iota(jnp.int32, keys.shape, 1)
            dead = (key >= left_ref[first + p]) & (lane == 0)
            bias = jnp.where(dead, F32(masked_score), F32(0.0)).astype(BF16)
            keys = jnp.concatenate([keys, bias], axis=1)
            scores.append(
                lax.dot_general(
                    query, keys, (((1,), (1,)), ((), ())), preferred_element_type=F32
                )
            )
        return scores

    def values(head, p):
        kv_head = head // groups
        vals = kv_refs[p][1, :, kv_head * HEAD : (kv_head + 1) * HEAD]
        return jnp.concatenate([vals, jnp.ones_like(vals)], axis=1)

    ahead = fetch(*units[0])
    for i, (head, span) in enumerate(units):
        scores = ahead
        if i + 1 < len(units):
            ahead = fetch(*units[i + 1])
        yield head, span, scores, functools.partial(values, head)


def weigh(scores, top, values):
    total = None
    for p, part in enumerate(scores):
        both = dot(jnp.exp2(part - top).astype(BF16), values(p))
        total = both if total is None else total + both
    return total


def highest(scores):
    return functools.reduce(
        jnp.maximum, [jnp.max(part, axis=-1, keepdims=True) for part in scores]
    )


def open_kernel(groups, units, first, left_ref, q_ref, *refs):
    *kv_refs, wide_ref, top_ref = refs
    for head, span, scores, values in attend_blocks(
        groups, units, first, left_ref, q_ref, kv_refs
    ):
        top = highest(scores)
        wide_ref[span, head * 2 * HEAD : (head + 1) * 2 * HEAD] = weigh(scores, top, values)
        top_ref[span, head * HEAD : (head + 1) * HEAD] = jnp.broadcast_to(
            top, (top.shape[0], HEAD)
        )


def close_kernel(groups, units, first, left_ref, q_ref, wide_ref, top_ref, *refs):
    *kv_refs, o_ref = refs
    for head, span, scores, values in attend_blocks(
        groups, units, first, left_ref, q_ref, kv_refs
    ):
        before = top_ref[span, head * HEAD : head * HEAD + 1]
        top = jnp.maximum(before, highest(scores))
        wide = wide_ref[span, head * 2 * HEAD : (head + 1) * 2 * HEAD]
        wide = wide * jnp.exp2(before - top) + weigh(scores, top, values)
        o_ref[span, head * HEAD : (head + 1) * HEAD] = (
            wide[:, :HEAD] / wide[:, HEAD:]
        ).astype(BF16)


def attend_call(queries, pieces, first, place, state):
    rows, width = queries.shape
    heads = width // HEAD
    groups = heads // (pieces[0].shape[2] // HEAD)
    block = min(rows, 256)
    units = [
        (head, slice(i, i + block)) for head in range(heads) for i in range(0, rows, block)
    ]
    count = len(pieces) * pieces[0].shape[1]
    weight = 1 if state else 24
    if state:
        body, name = close_kernel, "attend_close"
        out = jax.ShapeDtypeStruct((rows, width), BF16)
    else:
        body, name = open_kernel, "attend_open"
        out = [
            jax.ShapeDtypeStruct((rows, 2 * width), F32),
            jax.ShapeDtypeStruct((rows, width), F32),
        ]
    return pl.pallas_call(
        functools.partial(body, groups, units, TABLE + first),
        in_specs=[SMEM] + [VMEM] * (1 + len(state) + len(pieces)),
        out_specs=VMEM if state else [VMEM] * 2,
        out_shape=out,
        compiler_params=pltpu.CompilerParams(vmem_limit_bytes=LIMIT),
        cost_estimate=pl.CostEstimate(
            flops=weight * rows * count * width,
            bytes_accessed=4 * rows * width,
            transcendentals=rows * count,
        ),
        name=name,
    )(place, queries, *state, *pieces)


def near_kernel(obs_hbm, t0, t1, w0, w1, sum_ref, obs_ref, w_ref, sems):
    inner, depth = w0.shape
    tile = depth // 3
    pairs = [(obs_hbm, obs_ref), (w0, w_ref.at[:inner]), (w1, w_ref.at[inner:])]
    for copy in start_copies(pairs, sems):
        copy.wait()
    for i in range(3):
        strip = slice(i * tile, (i + 1) * tile)
        parts = jnp.concatenate([t0[...], t1[...]], axis=1)
        sum_ref[:, strip] = obs_ref[:, strip].astype(F32) + dot(parts, w_ref[:, strip])


def near_rows(obs, parts, weights):
    rows, depth = obs.shape
    inner = weights[0].shape[0]
    return pl.pallas_call(
        near_kernel,
        in_specs=[HBM] + [VMEM] * 2 + [HBM, ANY],
        out_specs=VMEM,
        out_shape=jax.ShapeDtypeStruct((rows, depth), F32),
        scratch_shapes=[
            pltpu.VMEM((rows, depth), BF16),
            pltpu.VMEM((2 * inner, depth), BF16),
            pltpu.SemaphoreType.DMA((3,)),
        ],
        compiler_params=pltpu.CompilerParams(vmem_limit_bytes=LIMIT),
        cost_estimate=pl.CostEstimate(
            flops=4 * rows * depth * inner, bytes_accessed=4 * depth * inner, transcendentals=0
        ),
        name="near_rows",
    )(obs, *parts, *weights)


def hidden_kernel(sum_ref, t2, t3, w2, w3, c_hbm, o_ref, emb_ref, w_ref, c_ref, sems):
    inner, depth = w2.shape
    tile = depth // 3
    copies = start_copies(
        [(w2, w_ref.at[:inner]), (w3, w_ref.at[inner:]), (c_hbm, c_ref)], sems
    )
    copies[0].wait()
    copies[1].wait()
    for i in range(3):
        strip = slice(i * tile, (i + 1) * tile)
        parts = jnp.concatenate([t2[...], t3[...]], axis=1)
        o_ref[:, strip] = (sum_ref[:, strip] + dot(parts, w_ref[:, strip])).astype(BF16)
    copies[2].wait()
    emb_ref[...] = dot(o_ref[...], c_ref[...]).astype(BF16)


def hidden_rows(near_sum, parts, weights, c_in):
    rows, depth = near_sum.shape
    inner = weights[0].shape[0]
    width = c_in.shape[1]
    return pl.pallas_call(
        hidden_kernel,
        in_specs=[VMEM] * 3 + [ANY] * 2 + [HBM],
        out_specs=[VMEM] * 2,
        out_shape=[
            jax.ShapeDtypeStruct((rows, depth), BF16),
            jax.ShapeDtypeStruct((rows, width), BF16),
        ],
        scratch_shapes=[
            pltpu.VMEM((2 * inner, depth), BF16),
            pltpu.VMEM((depth, width), BF16),
            pltpu.SemaphoreType.DMA((3,)),
        ],
        compiler_params=pltpu.CompilerParams(vmem_limit_bytes=LIMIT),
        cost_estimate=pl.CostEstimate(
            flops=8 * rows * depth * inner, bytes_accessed=8 * depth * inner, transcendentals=0
        ),
        name="hidden_rows",
    )(near_sum, *parts, *weights, c_in)


def join_kernel(place_ref, e0, e1, e2, e3, wkv_any, kv_ref, factor_ref, emb_ref, wkv_ref, sems):
    rows, wide = emb_ref.shape
    width = wkv_any.shape[2]
    strip = e0.shape[1]
    copies = start_copies(
        [(wkv_any.at[c], wkv_ref.at[:, c * width : (c + 1) * width]) for c in range(2)], sems
    )
    starts = [pl.multiple_of((place_ref[1] ^ code) * strip, strip) for code in range(4)]
    parts = (e0, e1, e2, e3)
    for copy in copies:
        copy.wait()
    block = rows // 2
    for i in range(2):
        span = slice(i * block, (i + 1) * block)
        square, both = 0.0, 0.0
        for part, start in zip(parts, starts):
            emb = part[span, :]
            wide_emb = emb.astype(F32)
            square = square + jnp.sum(wide_emb * wide_emb, axis=-1, keepdims=True)
            both = both + dot(emb, wkv_ref[pl.ds(start, strip), :])
            emb_ref[span, pl.ds(start, strip)] = emb
        factor = lax.rsqrt(square / wide + epsilon)
        both = both * factor
        kv_ref[0, span, :] = both[:, :width].astype(BF16)
        kv_ref[1, span, :] = both[:, width:].astype(BF16)
        factor_ref[span, :] = jnp.broadcast_to(factor, (block, HEAD))


def join_rows(place, parts, w_keyval):
    rows, strip = parts[0].shape
    wide = 4 * strip
    width = w_keyval.shape[2]
    return pl.pallas_call(
        join_kernel,
        in_specs=[SMEM] + [VMEM] * 4 + [HBM],
        out_specs=[VMEM] * 3,
        out_shape=[
            jax.ShapeDtypeStruct((2, rows, width), BF16),
            jax.ShapeDtypeStruct((rows, HEAD), F32),
            jax.ShapeDtypeStruct((rows, wide), BF16),
        ],
        scratch_shapes=[pltpu.VMEM((wide, 2 * width), BF16), pltpu.SemaphoreType.DMA((2,))],
        compiler_params=pltpu.CompilerParams(vmem_limit_bytes=LIMIT),
        cost_estimate=pl.CostEstimate(
            flops=4 * rows * wide * width, bytes_accessed=4 * rows * wide, transcendentals=0
        ),
        name="join_rows",
    )(place, *parts, w_keyval)


def part_kernel(place_ref, att_ref, c_hbm, send_ref, keep_ref, order_ref, c_ref, sems):
    rows, inner = att_ref.shape
    wide = c_ref.shape[1]
    block = rows // 4
    half = inner // 2
    spans = [slice(i * half, (i + 1) * half) for i in range(2)]
    copies = start_copies([(c_hbm.at[span], c_ref.at[span]) for span in spans], sems)
    for at, code in enumerate(ROWS):
        start = pl.multiple_of((place_ref[1] ^ code) * block, block)
        order_ref[at * block : (at + 1) * block, :] = att_ref[pl.ds(start, block), :]
    for copy in copies:
        copy.wait()
    tile = 512
    for out, source in ((send_ref, order_ref[2 * block :, :]), (keep_ref, order_ref[: 2 * block, :])):
        for j in range(wide // tile):
            columns = slice(j * tile, (j + 1) * tile)
            out[:, columns] = dot(source, c_ref[:, columns]).astype(out.dtype)


def part_rows(place, attended, c_out):
    rows, inner = attended.shape
    wide = c_out.shape[1]
    return pl.pallas_call(
        part_kernel,
        in_specs=[SMEM, VMEM, HBM],
        out_specs=[VMEM] * 3,
        out_shape=[
            jax.ShapeDtypeStruct((rows // 2, wide), BF16),
            jax.ShapeDtypeStruct((rows // 2, wide), F32),
            jax.ShapeDtypeStruct((rows, inner), BF16),
        ],
        scratch_shapes=[pltpu.VMEM((inner, wide), BF16), pltpu.SemaphoreType.DMA((2,))],
        compiler_params=pltpu.CompilerParams(vmem_limit_bytes=LIMIT),
        cost_estimate=pl.CostEstimate(
            flops=2 * rows * wide * inner, bytes_accessed=8 * wide * inner, transcendentals=0
        ),
        name="part_rows",
    )(place, attended, c_out)


def mixed_kernel(
    place_ref, emb_ref, keep_ref, near_ref, got_ref, wv_ref, ret_ref,
    value_ref, other_ref, own_ref, mixed_ref,
):
    rows, wide = got_ref.shape
    half = wide // 2
    block = 32
    base = place_ref[1] * rows
    live_total = place_ref[4].astype(F32)

    @pl.loop(0, rows // block)
    def _(i):
        start = pl.multiple_of(i * block, block)
        span = pl.ds(start, block)
        mixed = emb_ref[span, :].astype(F32) + (
            keep_ref[span, :] + near_ref[span, :].astype(F32) + got_ref[span, :].astype(F32)
        )
        mixed_ref[...] = mixed
        factor = row_factor(mixed)
        value = factor * jnp.sum(mixed * wv_ref[...].astype(F32), axis=-1, keepdims=True)
        row = place_ref[2] + base + start + lax.broadcasted_iota(jnp.int32, (block, 1), 0)
        gap = jnp.where(row < place_ref[3], value - ret_ref[span, :], F32(0.0)) / live_total
        lead = factor * gap
        pull = lead * factor * value / wide
        value_ref[span, :] = jnp.broadcast_to(value, (block, HEAD))
        for out, side in ((own_ref, place_ref[0]), (other_ref, 1 - place_ref[0])):
            columns = pl.ds(pl.multiple_of(side * half, half), half)
            part = mixed_ref[:, columns]
            out[span, :] = (lead * wv_ref[:, columns].astype(F32) - part * pull).astype(BF16)


def mixed_rows(place, embedded, keep, near, got, w_value, returns):
    rows, wide = got.shape
    return pl.pallas_call(
        mixed_kernel,
        in_specs=[SMEM] + [VMEM] * 6,
        out_specs=[VMEM] * 3,
        out_shape=[
            jax.ShapeDtypeStruct((rows, HEAD), F32),
            jax.ShapeDtypeStruct((rows, wide // 2), BF16),
            jax.ShapeDtypeStruct((rows, wide // 2), BF16),
        ],
        scratch_shapes=[pltpu.VMEM((32, wide), F32)],
        compiler_params=pltpu.CompilerParams(vmem_limit_bytes=LIMIT),
        cost_estimate=pl.CostEstimate(
            flops=10 * rows * wide, bytes_accessed=12 * rows * wide, transcendentals=0
        ),
        name="mixed_rows",
    )(place, embedded, keep, near, got, w_value, returns)


def gather_codes(size):
    codes, bit = [0], size // 2
    while bit >= 1:
        codes = codes + [code ^ bit for code in codes]
        bit //= 2
    return codes


def split_kernel(codes, index_ref, own_ref, got_ref, keep_ref, send_ref):
    block = own_ref.shape[0] // len(codes)
    side = len(codes) // 2
    for k, code in enumerate(codes):
        span = pl.ds(pl.multiple_of((index_ref[0] ^ code) * block, block), block)
        out = (keep_ref, send_ref)[k // side]
        at = k % side * block
        total = own_ref[span, :] + got_ref[span, :].astype(F32)
        out[at : at + block, :] = total.astype(out.dtype)


def split_sum(index, own, got, count):
    rows, wide = own.shape
    if (rows // count) % 16:
        got = got.astype(F32)
    send_type = BF16 if (rows // count) % 16 == 0 else F32
    return pl.pallas_call(
        functools.partial(split_kernel, gather_codes(count)),
        in_specs=[SMEM, VMEM, VMEM],
        out_specs=[VMEM] * 2,
        out_shape=[
            jax.ShapeDtypeStruct((rows // 2, wide), F32),
            jax.ShapeDtypeStruct((rows // 2, wide), send_type),
        ],
        compiler_params=pltpu.CompilerParams(vmem_limit_bytes=LIMIT),
        cost_estimate=pl.CostEstimate(
            flops=rows * wide, bytes_accessed=8 * rows * wide, transcendentals=0
        ),
        name="split_sum",
    )(index, own, got)


def assemble_kernel(spots, chunks, place_ref, *refs):
    parts = refs[: len(spots)]
    out, got_ref, wide_ref, got_sems, sems = refs[-5:]
    block, strip = parts[0].shape
    got = start_copies([(part, got_ref.at[i]) for i, part in enumerate(parts)], got_sems)
    copies = []
    for i, (chunk, side, code) in enumerate(spots):
        row = pl.multiple_of((place_ref[5] ^ code) * block, block)
        column = pl.multiple_of(((place_ref[0] ^ side) * chunks + chunk) * strip, strip)
        got[i].wait()
        wide_ref[i] = got_ref[i].astype(F32)
        copy = pltpu.make_async_copy(
            wide_ref.at[i], out.at[pl.ds(row, block), pl.ds(column, strip)], sems.at[i]
        )
        copy.start()
        copies.append(copy)
    for copy in copies:
        copy.wait()


def assemble(place, parts, spots, count, chunks, before):
    block, strip = parts[0].shape
    rows, wide = block * count, strip * 2 * chunks
    return pl.pallas_call(
        functools.partial(assemble_kernel, spots, chunks),
        in_specs=[SMEM] + [ANY] * (len(parts) + len(before)),
        out_specs=ANY,
        out_shape=jax.ShapeDtypeStruct((rows, wide), F32),
        input_output_aliases={1 + len(parts): 0} if before else {},
        scratch_shapes=[
            pltpu.VMEM((len(parts), block, strip), BF16),
            pltpu.VMEM((len(parts), block, strip), F32),
            pltpu.SemaphoreType.DMA((len(parts),)),
            pltpu.SemaphoreType.DMA((len(parts),)),
        ],
        compiler_params=pltpu.CompilerParams(vmem_limit_bytes=LIMIT),
        cost_estimate=pl.CostEstimate(
            flops=rows * wide, bytes_accessed=6 * rows * wide, transcendentals=0
        ),
        name="assemble",
    )(place, *parts, *before)


def swap(block, axis, bit):
    size = lax.axis_size(axis)
    return lax.ppermute(block, axis, [(i, i ^ bit) for i in range(size)])


def gather_blocks(block, axis, late=None):
    blocks, bit = [block], lax.axis_size(axis) // 2
    while bit >= 1:
        sources = blocks if bit > 1 or late is None else [late] + blocks[1:]
        blocks = blocks + [swap(item, axis, bit) for item in sources]
        bit //= 2
    return blocks


def gather_parts(part):
    far = swap(part, "mdl", 2)
    return [part, swap(part, "mdl", 1), far, swap(far, "mdl", 1)], far


def product(left, right):
    return jnp.einsum("rh,rd->hd", left, right, preferred_element_type=F32)


def halve(keep, got):
    total = keep + got.astype(F32)
    side = total.shape[0] // 2
    return total[:side], total[side:].astype(BF16)


def on_device(
    obs,
    a_query,
    a_keyval,
    a_out,
    w_policy,
    c_in,
    c_query,
    c_keyval,
    c_out,
    w_value,
    actions,
    advantages,
    old_logp,
    returns,
    robot_count,
):
    row_count = obs.shape[1]
    batch_index = lax.axis_index("sec")
    rep_index = lax.axis_index("rep")
    rep_count = lax.axis_size("rep")
    robot_total = robot_count[batch_index]
    live_sum = jnp.sum(robot_count)
    live_total = live_sum.astype(F32)
    first_row = rep_index * row_count
    live_mask = first_row + lax.iota(jnp.int32, row_count) < robot_total
    mdl_count = lax.axis_size("mdl")
    assert mdl_count == 4 and lax.axis_size("sec") == 2
    mdl_index = lax.axis_index("mdl")
    value_rows = row_count // mdl_count
    score_scale = HEAD ** (-0.5) * LOG2E
    rep_place = rep_index.reshape(1).astype(jnp.int32)

    place = jnp.stack(
        [batch_index, mdl_index, first_row, robot_total, live_sum, rep_index]
        + [
            jnp.clip(robot_total - (rep_index ^ code) * row_count, 0, row_count)
            for code in gather_codes(rep_count)
        ]
    ).astype(jnp.int32)

    obs_in = obs[0]
    keyval, factor_a = first_projection(obs_in, a_keyval)
    a_far = swap(a_out, "mdl", 2)
    queries = query_projection(obs_in, a_query, factor_a, score_scale)
    late_keyval, queries = tied(keyval, queries)
    pieces_k = gather_blocks(keyval, "rep", late_keyval)
    state = attend_call(queries, pieces_k[:-1], 0, place, [])
    attended = attend_call(queries, pieces_k[-1:], rep_count - 1, place, state)
    attended, a_far = tied(attended, a_far)
    attended_far = swap(attended, "mdl", 2)
    attended_near = swap(attended, "mdl", 1)
    near_sum = near_rows(obs_in, [attended, attended_near], [a_out, swap(a_out, "mdl", 1)])
    attended_far, near_sum = tied(attended_far, near_sum)
    hidden, embed_part = hidden_rows(
        near_sum,
        [attended_far, swap(attended_far, "mdl", 1)],
        [a_far, swap(a_far, "mdl", 1)],
        c_in,
    )

    source = hidden.astype(F32)
    factor_h = row_factor(source)
    logits = dot(hidden, w_policy) * factor_h
    log_probs = jax.nn.log_softmax(logits, axis=-1)
    onehot = (
        actions[0][:, None] == lax.broadcasted_iota(jnp.int32, logits.shape, 1)
    ).astype(F32)
    chosen = jnp.sum(onehot * log_probs, axis=-1)
    prob_ratio = jnp.exp(chosen - old_logp[0])
    plain_term = prob_ratio * advantages[0]
    bounded = jnp.clip(prob_ratio, 1.0 - clip_range, 1.0 + clip_range) * advantages[0]
    slope = jnp.where(live_mask & (plain_term <= bounded), -plain_term / live_total, F32(0.0))
    dlogits = slope[:, None] * (onehot - jnp.exp(log_probs))
    along = jnp.sum(dlogits * logits, axis=-1, keepdims=True) / source.shape[1]
    dnormed = dot(dlogits.astype(BF16), w_policy.T)
    dhidden = (factor_h * (dnormed - source * (factor_h * along))).astype(BF16)
    half_a = dhidden.shape[1] // 2
    send_a, own_a = [
        product(attended, lax.dynamic_slice_in_dim(dhidden, side * half_a, half_a, 1))
        for side in (1 - batch_index, batch_index)
    ]

    embed_far = swap(embed_part, "mdl", 2)
    embed_far, own_a = tied(embed_far, own_a)
    got_a = swap(send_a.astype(BF16), "sec", 1)
    embed_parts = [embed_part, swap(embed_part, "mdl", 1), embed_far, swap(embed_far, "mdl", 1)]
    critic_keyval, factor_c, embedded = join_rows(place, embed_parts, c_keyval)
    pieces_c = gather_blocks(critic_keyval, "rep")
    critic_queries = (dot(embedded, c_query) * (factor_c[:, :1] * score_scale)).astype(BF16)
    critic_queries, got_a = tied(critic_queries, got_a)
    keep_a, send_a = split_sum(rep_place, own_a, got_a, rep_count)
    moved_a = swap(send_a.astype(BF16), "rep", 1)

    wide = w_value.shape[0]
    target = lax.dynamic_slice_in_dim(returns[0], mdl_index * value_rows, value_rows, 0)
    emb_mine = lax.dynamic_slice_in_dim(embedded, mdl_index * value_rows, value_rows, 0)
    critic_queries, w_row, target, emb_mine = tied(
        critic_queries,
        w_value.reshape(1, wide),
        target.reshape(value_rows, 1),
        emb_mine,
    )
    state_c = attend_call(critic_queries, pieces_c[:-1], 0, place, [])
    critic_attended = attend_call(critic_queries, pieces_c[-1:], rep_count - 1, place, state_c)

    send_m, keep_m, att_rows = part_rows(place, critic_attended, c_out)
    near_m = swap(send_m, "mdl", 1)
    near_m, moved_a = tied(near_m, moved_a)
    bit = 2
    while bit < rep_count:
        keep_a, send_a = halve(keep_a, moved_a)
        moved_a = swap(send_a, "rep", bit)
        bit *= 2
    send_y = (keep_m[value_rows:] + near_m[value_rows:].astype(F32)).astype(BF16)
    got_y = swap(send_y, "mdl", 2)
    att_there = swap(critic_attended, "sec", 1)
    got_y, moved_a = tied(got_y, moved_a)
    mine_a = gather_blocks((keep_a + moved_a.astype(F32)).astype(BF16), "rep")
    value_wide, d_other, d_own = mixed_rows(
        place, emb_mine, keep_m, near_m, got_y, w_row, target
    )

    d_there = swap(d_other, "sec", 1)
    d_far = swap(d_own, "mdl", 2)
    there_far = swap(d_other, ("sec", "mdl"), mdl_count | 2)
    d_there, *mine_a[1:-1] = tied(d_there, *mine_a[1:-1])
    own_rows = jnp.concatenate(
        [d_own, d_far, swap(d_own, "mdl", 1), swap(d_far, "mdl", 1)], axis=0
    )
    there_rows = jnp.concatenate(
        [d_there, there_far, swap(d_there, "mdl", 1), swap(there_far, "mdl", 1)], axis=0
    )
    att_there = jnp.concatenate(
        [
            lax.dynamic_slice_in_dim(att_there, (mdl_index ^ code) * value_rows, value_rows, 0)
            for code in ROWS
        ],
        axis=0,
    )
    value_part, there_rows = tied(value_wide[:, 0], there_rows)
    theirs_a = [swap(block, "sec", 1) for block in mine_a]
    codes = gather_codes(rep_count)
    spots = [(0, side, code) for side in range(2) for code in codes]
    actor_summed = assemble(place, mine_a + theirs_a, spots, rep_count, 1, [])

    strip = d_own.shape[1] // CHUNKS
    chunks = []
    for c in range(CHUNKS):
        span = slice(c * strip, (c + 1) * strip)
        keep, send = split_sum(
            rep_place,
            product(att_rows, own_rows[:, span]),
            product(att_there, there_rows[:, span]),
            rep_count,
        )
        chunks.append([keep, [swap(send.astype(BF16), "rep", 1)], [], [], []])
    levels = rep_count.bit_length() - 1
    for tick in range(2 * levels + CHUNKS - 1):
        turn = [c for c in range(CHUNKS) if 0 <= tick - c < 2 * levels]
        waited = [item for c in turn for item in chunks[c][1] + chunks[c][3]]
        extra = []
        if tick == 0:
            extra = [chunks[c][0] for c in range(1, CHUNKS)] + mine_a[-1:]
        if tick == 1:
            extra = theirs_a
        if tick == 2 * levels - 1:
            extra = [actor_summed]
        if tick == 2 * levels + CHUNKS - 2:
            done = [
                (item, (c, side, code))
                for c in range(CHUNKS)
                for side in range(2)
                for item, code in zip(chunks[c][2 + 2 * side], codes)
            ]
            extra = [assemble(place, *zip(*done), rep_count, CHUNKS, [])]
        outs = list(tied(*waited, *extra))
        if tick == 0:
            for c in range(1, CHUNKS):
                chunks[c][0] = outs[len(waited) + c - 1]
        if tick == 2 * levels - 1:
            actor_summed = outs[-1]
        if tick == 2 * levels + CHUNKS - 2:
            result = outs[-1]
        for c in turn:
            keep, pending, mine, crossing, theirs = chunks[c]
            arrived, outs = outs[: len(pending)], outs[len(pending) :]
            crossed, outs = outs[: len(crossing)], outs[len(crossing) :]
            theirs = theirs + crossed
            level = tick - c + 1
            if level < levels:
                keep, send = halve(keep, arrived[0])
                pending = [swap(send, "rep", 1 << level)]
            else:
                fresh = arrived
                if level == levels:
                    fresh = [(keep + arrived[0].astype(F32)).astype(BF16)]
                mine = mine + fresh
                crossing = [swap(block, "sec", 1) for block in fresh]
                bit = rep_count >> (level - levels + 1)
                pending = [swap(block, "rep", bit) for block in mine] if bit else []
            chunks[c] = [keep, pending, mine, crossing, theirs]
    rest = [
        (item, (c, side, code))
        for c in range(CHUNKS)
        for side, group in enumerate((chunks[c][2], chunks[c][4] + chunks[c][3]))
        for item, code in zip(group, codes)
        if (c, side, code) not in [spot for _, spot in done]
    ]
    result = assemble(place, *zip(*rest), rep_count, CHUNKS, [result])

    return (value_part[None, :], actor_summed, result)


def solution(mesh):
    return jax.shard_map(
        on_device,
        mesh=mesh,
        in_specs=(
            P("sec", "rep", None),
            P(None, "mdl"),
            P(None, None, "mdl"),
            P("mdl", None),
            P(),
            P(None, "mdl"),
            P(None, "mdl"),
            P(None, None, "mdl"),
            P("mdl", None),
            P(),
            P("sec", "rep"),
            P("sec", "rep"),
            P("sec", "rep"),
            P("sec", "rep"),
            P(),
        ),
        out_specs=(P("sec", ("rep", "mdl")), P("mdl", None), P("mdl", None)),
        check_vma=False,
    )
```

```python
import functools
import math

import jax
import jax.numpy as jnp
from jax import lax
from jax.experimental import pallas as pl
from jax.experimental.pallas import tpu as pltpu
from jax.sharding import PartitionSpec as P

HEAD = 128
epsilon = 1e-05
clip_range = 0.2
masked_score = -1e30
LOG2E = 1.4426950408889634
F32 = jnp.float32
BF16 = jnp.bfloat16
CHUNKS = 2
TABLE = 6
ROWS = (0, 2, 1, 3)
LIMIT = 40 * 2**20
HIGH = 56 * 2**20
VMEM = pl.BlockSpec(memory_space=pltpu.VMEM)
SMEM = pl.BlockSpec(memory_space=pltpu.SMEM)
ANY = pl.BlockSpec(memory_space=pl.ANY)
HBM = pl.BlockSpec(memory_space=pltpu.HBM)


def dot(a, b):
    return jnp.dot(a, b, preferred_element_type=F32)


def tied(*items):
    return lax.optimization_barrier(items)


def row_factor(source):
    return lax.rsqrt(jnp.mean(source * source, axis=-1, keepdims=True) + epsilon)


def start_copies(pairs, sems):
    copies = [
        pltpu.make_async_copy(source, target, sems.at[i])
        for i, (source, target) in enumerate(pairs)
    ]
    for copy in copies:
        copy.start()
    return copies


def first_kernel(obs_hbm, w_hbm, kv_ref, factor_ref, obs_ref, w_ref, sems):
    rows, depth = obs_ref.shape
    width = w_hbm.shape[2]
    block = rows // 2
    spans = [slice(i * block, (i + 1) * block) for i in range(2)]
    copies = start_copies(
        [(w_hbm.at[c], w_ref.at[:, c * width : (c + 1) * width]) for c in range(2)]
        + [(obs_hbm.at[span], obs_ref.at[span]) for span in spans],
        sems,
    )
    for i, span in enumerate(spans):
        copies[2 + i].wait()
        part = obs_ref[span, :]
        factor = row_factor(part.astype(F32))
        if i == 0:
            copies[0].wait()
            copies[1].wait()
        both = dot(part, w_ref[...]) * factor
        kv_ref[0, span, :] = both[:, :width].astype(BF16)
        kv_ref[1, span, :] = both[:, width:].astype(BF16)
        factor_ref[span, :] = jnp.broadcast_to(factor, (block, HEAD))


def first_projection(obs, w_keyval):
    rows, depth = obs.shape
    width = w_keyval.shape[2]
    return pl.pallas_call(
        first_kernel,
        in_specs=[HBM] * 2,
        out_specs=[VMEM] * 2,
        out_shape=[
            jax.ShapeDtypeStruct((2, rows, width), BF16),
            jax.ShapeDtypeStruct((rows, HEAD), F32),
        ],
        scratch_shapes=[
            pltpu.VMEM((rows, depth), BF16),
            pltpu.VMEM((depth, 2 * width), BF16),
            pltpu.SemaphoreType.DMA((4,)),
        ],
        compiler_params=pltpu.CompilerParams(vmem_limit_bytes=HIGH),
        cost_estimate=pl.CostEstimate(
            flops=4 * rows * depth * width, bytes_accessed=2 * rows * depth, transcendentals=0
        ),
        name="first_projection",
    )(obs, w_keyval)


def query_kernel(scale, obs_hbm, w_hbm, factor_ref, q_ref, obs_ref, w_ref, sems):
    for copy in start_copies([(w_hbm, w_ref), (obs_hbm, obs_ref)], sems):
        copy.wait()
    q_ref[...] = (dot(obs_ref[...], w_ref[...]) * (factor_ref[:, :1] * scale)).astype(BF16)


def query_projection(obs, w_query, factor, scale):
    rows, depth = obs.shape
    width = w_query.shape[1]
    return pl.pallas_call(
        functools.partial(query_kernel, scale),
        in_specs=[HBM, HBM, VMEM],
        out_specs=VMEM,
        out_shape=jax.ShapeDtypeStruct((rows, width), BF16),
        scratch_shapes=[
            pltpu.VMEM((rows, depth), BF16),
            pltpu.VMEM((depth, width), BF16),
            pltpu.SemaphoreType.DMA((2,)),
        ],
        compiler_params=pltpu.CompilerParams(vmem_limit_bytes=LIMIT),
        cost_estimate=pl.CostEstimate(
            flops=2 * rows * depth * width, bytes_accessed=2 * rows * depth, transcendentals=0
        ),
        name="query_projection",
    )(obs, w_query, factor)


def attend_blocks(groups, units, first, left_ref, q_ref, kv_refs):
    def fetch(head, span):
        kv_head = head // groups
        columns = slice(kv_head * HEAD, (kv_head + 1) * HEAD)
        query = q_ref[span, head * HEAD : (head + 1) * HEAD]
        lane = lax.broadcasted_iota(jnp.int32, query.shape, 1)
        query = jnp.concatenate([query, (lane == 0).astype(BF16)], axis=1)
        scores = []
        for p, ref in enumerate(kv_refs):
            keys = ref[0, :, columns]
            key = lax.broadcasted_iota(jnp.int32, keys.shape, 0)
            lane = lax.broadcasted_iota(jnp.int32, keys.shape, 1)
            dead = (key >= left_ref[first + p]) & (lane == 0)
            bias = jnp.where(dead, F32(masked_score), F32(0.0)).astype(BF16)
            keys = jnp.concatenate([keys, bias], axis=1)
            scores.append(
                lax.dot_general(
                    query, keys, (((1,), (1,)), ((), ())), preferred_element_type=F32
                )
            )
        return scores

    def values(head, p):
        kv_head = head // groups
        vals = kv_refs[p][1, :, kv_head * HEAD : (kv_head + 1) * HEAD]
        return jnp.concatenate([vals, jnp.ones_like(vals)], axis=1)

    ahead = fetch(*units[0])
    for i, (head, span) in enumerate(units):
        scores = ahead
        if i + 1 < len(units):
            ahead = fetch(*units[i + 1])
        yield head, span, scores, functools.partial(values, head)


def weigh(scores, top, values):
    total = None
    for p, part in enumerate(scores):
        both = dot(jnp.exp2(part - top).astype(BF16), values(p))
        total = both if total is None else total + both
    return total


def highest(scores):
    return functools.reduce(
        jnp.maximum, [jnp.max(part, axis=-1, keepdims=True) for part in scores]
    )


def open_kernel(groups, units, first, left_ref, q_ref, *refs):
    *kv_refs, wide_ref, top_ref = refs
    for head, span, scores, values in attend_blocks(
        groups, units, first, left_ref, q_ref, kv_refs
    ):
        top = highest(scores)
        wide_ref[span, head * 2 * HEAD : (head + 1) * 2 * HEAD] = weigh(scores, top, values)
        top_ref[span, head * HEAD : (head + 1) * HEAD] = jnp.broadcast_to(
            top, (top.shape[0], HEAD)
        )


def close_kernel(groups, units, first, left_ref, q_ref, wide_ref, top_ref, *refs):
    *kv_refs, o_ref = refs
    for head, span, scores, values in attend_blocks(
        groups, units, first, left_ref, q_ref, kv_refs
    ):
        before = top_ref[span, head * HEAD : head * HEAD + 1]
        top = jnp.maximum(before, highest(scores))
        wide = wide_ref[span, head * 2 * HEAD : (head + 1) * 2 * HEAD]
        wide = wide * jnp.exp2(before - top) + weigh(scores, top, values)
        o_ref[span, head * HEAD : (head + 1) * HEAD] = (
            wide[:, :HEAD] / wide[:, HEAD:]
        ).astype(BF16)


def attend_call(queries, pieces, first, place, state):
    rows, width = queries.shape
    heads = width // HEAD
    groups = heads // (pieces[0].shape[2] // HEAD)
    block = min(rows, 256)
    units = [
        (head, slice(i, i + block)) for head in range(heads) for i in range(0, rows, block)
    ]
    count = len(pieces) * pieces[0].shape[1]
    weight = 1 if state else 24
    if state:
        body, name = close_kernel, "attend_close"
        out = jax.ShapeDtypeStruct((rows, width), BF16)
    else:
        body, name = open_kernel, "attend_open"
        out = [
            jax.ShapeDtypeStruct((rows, 2 * width), F32),
            jax.ShapeDtypeStruct((rows, width), F32),
        ]
    return pl.pallas_call(
        functools.partial(body, groups, units, TABLE + first),
        in_specs=[SMEM] + [VMEM] * (1 + len(state) + len(pieces)),
        out_specs=VMEM if state else [VMEM] * 2,
        out_shape=out,
        compiler_params=pltpu.CompilerParams(vmem_limit_bytes=LIMIT),
        cost_estimate=pl.CostEstimate(
            flops=weight * rows * count * width,
            bytes_accessed=4 * rows * width,
            transcendentals=rows * count,
        ),
        name=name,
    )(place, queries, *state, *pieces)


def near_kernel(obs_hbm, t0, t1, w0, w1, sum_ref, obs_ref, w_ref, sems):
    inner, depth = w0.shape
    tile = depth // 3
    pairs = [(obs_hbm, obs_ref), (w0, w_ref.at[:inner]), (w1, w_ref.at[inner:])]
    for copy in start_copies(pairs, sems):
        copy.wait()
    for i in range(3):
        strip = slice(i * tile, (i + 1) * tile)
        parts = jnp.concatenate([t0[...], t1[...]], axis=1)
        sum_ref[:, strip] = obs_ref[:, strip].astype(F32) + dot(parts, w_ref[:, strip])


def near_rows(obs, parts, weights):
    rows, depth = obs.shape
    inner = weights[0].shape[0]
    return pl.pallas_call(
        near_kernel,
        in_specs=[HBM] + [VMEM] * 2 + [HBM, ANY],
        out_specs=VMEM,
        out_shape=jax.ShapeDtypeStruct((rows, depth), F32),
        scratch_shapes=[
            pltpu.VMEM((rows, depth), BF16),
            pltpu.VMEM((2 * inner, depth), BF16),
            pltpu.SemaphoreType.DMA((3,)),
        ],
        compiler_params=pltpu.CompilerParams(vmem_limit_bytes=LIMIT),
        cost_estimate=pl.CostEstimate(
            flops=4 * rows * depth * inner, bytes_accessed=4 * depth * inner, transcendentals=0
        ),
        name="near_rows",
    )(obs, *parts, *weights)


def hidden_kernel(sum_ref, t2, t3, w2, w3, c_hbm, o_ref, emb_ref, w_ref, c_ref, sems):
    inner, depth = w2.shape
    tile = depth // 3
    copies = start_copies(
        [(w2, w_ref.at[:inner]), (w3, w_ref.at[inner:]), (c_hbm, c_ref)], sems
    )
    copies[0].wait()
    copies[1].wait()
    for i in range(3):
        strip = slice(i * tile, (i + 1) * tile)
        parts = jnp.concatenate([t2[...], t3[...]], axis=1)
        o_ref[:, strip] = (sum_ref[:, strip] + dot(parts, w_ref[:, strip])).astype(BF16)
    copies[2].wait()
    emb_ref[...] = dot(o_ref[...], c_ref[...]).astype(BF16)


def hidden_rows(near_sum, parts, weights, c_in):
    rows, depth = near_sum.shape
    inner = weights[0].shape[0]
    width = c_in.shape[1]
    return pl.pallas_call(
        hidden_kernel,
        in_specs=[VMEM] * 3 + [ANY] * 2 + [HBM],
        out_specs=[VMEM] * 2,
        out_shape=[
            jax.ShapeDtypeStruct((rows, depth), BF16),
            jax.ShapeDtypeStruct((rows, width), BF16),
        ],
        scratch_shapes=[
            pltpu.VMEM((2 * inner, depth), BF16),
            pltpu.VMEM((depth, width), BF16),
            pltpu.SemaphoreType.DMA((3,)),
        ],
        compiler_params=pltpu.CompilerParams(vmem_limit_bytes=LIMIT),
        cost_estimate=pl.CostEstimate(
            flops=8 * rows * depth * inner, bytes_accessed=8 * depth * inner, transcendentals=0
        ),
        name="hidden_rows",
    )(near_sum, *parts, *weights, c_in)


def join_kernel(place_ref, e0, e1, e2, e3, wkv_any, kv_ref, factor_ref, emb_ref, wkv_ref, sems):
    rows, wide = emb_ref.shape
    width = wkv_any.shape[2]
    strip = e0.shape[1]
    copies = start_copies(
        [(wkv_any.at[c], wkv_ref.at[:, c * width : (c + 1) * width]) for c in range(2)], sems
    )
    starts = [pl.multiple_of((place_ref[1] ^ code) * strip, strip) for code in range(4)]
    parts = (e0, e1, e2, e3)
    for copy in copies:
        copy.wait()
    block = rows // 2
    for i in range(2):
        span = slice(i * block, (i + 1) * block)
        square, both = 0.0, 0.0
        for part, start in zip(parts, starts):
            emb = part[span, :]
            wide_emb = emb.astype(F32)
            square = square + jnp.sum(wide_emb * wide_emb, axis=-1, keepdims=True)
            both = both + dot(emb, wkv_ref[pl.ds(start, strip), :])
            emb_ref[span, pl.ds(start, strip)] = emb
        factor = lax.rsqrt(square / wide + epsilon)
        both = both * factor
        kv_ref[0, span, :] = both[:, :width].astype(BF16)
        kv_ref[1, span, :] = both[:, width:].astype(BF16)
        factor_ref[span, :] = jnp.broadcast_to(factor, (block, HEAD))


def join_rows(place, parts, w_keyval):
    rows, strip = parts[0].shape
    wide = 4 * strip
    width = w_keyval.shape[2]
    return pl.pallas_call(
        join_kernel,
        in_specs=[SMEM] + [VMEM] * 4 + [HBM],
        out_specs=[VMEM] * 3,
        out_shape=[
            jax.ShapeDtypeStruct((2, rows, width), BF16),
            jax.ShapeDtypeStruct((rows, HEAD), F32),
            jax.ShapeDtypeStruct((rows, wide), BF16),
        ],
        scratch_shapes=[pltpu.VMEM((wide, 2 * width), BF16), pltpu.SemaphoreType.DMA((2,))],
        compiler_params=pltpu.CompilerParams(vmem_limit_bytes=LIMIT),
        cost_estimate=pl.CostEstimate(
            flops=4 * rows * wide * width, bytes_accessed=4 * rows * wide, transcendentals=0
        ),
        name="join_rows",
    )(place, *parts, w_keyval)


def part_kernel(place_ref, att_ref, c_hbm, send_ref, keep_ref, order_ref, c_ref, sems):
    rows, inner = att_ref.shape
    wide = c_ref.shape[1]
    block = rows // 4
    half = inner // 2
    spans = [slice(i * half, (i + 1) * half) for i in range(2)]
    copies = start_copies([(c_hbm.at[span], c_ref.at[span]) for span in spans], sems)
    for at, code in enumerate(ROWS):
        start = pl.multiple_of((place_ref[1] ^ code) * block, block)
        order_ref[at * block : (at + 1) * block, :] = att_ref[pl.ds(start, block), :]
    for copy in copies:
        copy.wait()
    tile = 512
    for out, source in ((send_ref, order_ref[2 * block :, :]), (keep_ref, order_ref[: 2 * block, :])):
        for j in range(wide // tile):
            columns = slice(j * tile, (j + 1) * tile)
            out[:, columns] = dot(source, c_ref[:, columns]).astype(out.dtype)


def part_rows(place, attended, c_out):
    rows, inner = attended.shape
    wide = c_out.shape[1]
    return pl.pallas_call(
        part_kernel,
        in_specs=[SMEM, VMEM, HBM],
        out_specs=[VMEM] * 3,
        out_shape=[
            jax.ShapeDtypeStruct((rows // 2, wide), BF16),
            jax.ShapeDtypeStruct((rows // 2, wide), F32),
            jax.ShapeDtypeStruct((rows, inner), BF16),
        ],
        scratch_shapes=[pltpu.VMEM((inner, wide), BF16), pltpu.SemaphoreType.DMA((2,))],
        compiler_params=pltpu.CompilerParams(vmem_limit_bytes=LIMIT),
        cost_estimate=pl.CostEstimate(
            flops=2 * rows * wide * inner, bytes_accessed=8 * wide * inner, transcendentals=0
        ),
        name="part_rows",
    )(place, attended, c_out)


def mixed_kernel(
    place_ref, emb_ref, keep_ref, near_ref, got_ref, wv_ref, ret_ref,
    value_ref, other_ref, own_ref, mixed_ref,
):
    rows, wide = got_ref.shape
    half = wide // 2
    block = 32
    base = place_ref[1] * rows
    live_total = place_ref[4].astype(F32)

    @pl.loop(0, rows // block)
    def _(i):
        start = pl.multiple_of(i * block, block)
        span = pl.ds(start, block)
        mixed = emb_ref[span, :].astype(F32) + (
            keep_ref[span, :] + near_ref[span, :].astype(F32) + got_ref[span, :].astype(F32)
        )
        mixed_ref[...] = mixed
        factor = row_factor(mixed)
        value = factor * jnp.sum(mixed * wv_ref[...].astype(F32), axis=-1, keepdims=True)
        row = place_ref[2] + base + start + lax.broadcasted_iota(jnp.int32, (block, 1), 0)
        gap = jnp.where(row < place_ref[3], value - ret_ref[span, :], F32(0.0)) / live_total
        lead = factor * gap
        pull = lead * factor * value / wide
        value_ref[span, :] = jnp.broadcast_to(value, (block, HEAD))
        for out, side in ((own_ref, place_ref[0]), (other_ref, 1 - place_ref[0])):
            columns = pl.ds(pl.multiple_of(side * half, half), half)
            part = mixed_ref[:, columns]
            out[span, :] = (lead * wv_ref[:, columns].astype(F32) - part * pull).astype(BF16)


def mixed_rows(place, embedded, keep, near, got, w_value, returns):
    rows, wide = got.shape
    return pl.pallas_call(
        mixed_kernel,
        in_specs=[SMEM] + [VMEM] * 6,
        out_specs=[VMEM] * 3,
        out_shape=[
            jax.ShapeDtypeStruct((rows, HEAD), F32),
            jax.ShapeDtypeStruct((rows, wide // 2), BF16),
            jax.ShapeDtypeStruct((rows, wide // 2), BF16),
        ],
        scratch_shapes=[pltpu.VMEM((32, wide), F32)],
        compiler_params=pltpu.CompilerParams(vmem_limit_bytes=LIMIT),
        cost_estimate=pl.CostEstimate(
            flops=10 * rows * wide, bytes_accessed=12 * rows * wide, transcendentals=0
        ),
        name="mixed_rows",
    )(place, embedded, keep, near, got, w_value, returns)


def gather_codes(size):
    codes, bit = [0], size // 2
    while bit >= 1:
        codes = codes + [code ^ bit for code in codes]
        bit //= 2
    return codes


def split_kernel(codes, index_ref, own_ref, got_ref, keep_ref, send_ref):
    block = own_ref.shape[0] // len(codes)
    side = len(codes) // 2
    for k, code in enumerate(codes):
        span = pl.ds(pl.multiple_of((index_ref[0] ^ code) * block, block), block)
        out = (keep_ref, send_ref)[k // side]
        at = k % side * block
        total = own_ref[span, :] + got_ref[span, :].astype(F32)
        out[at : at + block, :] = total.astype(out.dtype)


def split_sum(index, own, got, count):
    rows, wide = own.shape
    if (rows // count) % 16:
        got = got.astype(F32)
    send_type = BF16 if (rows // count) % 16 == 0 else F32
    return pl.pallas_call(
        functools.partial(split_kernel, gather_codes(count)),
        in_specs=[SMEM, VMEM, VMEM],
        out_specs=[VMEM] * 2,
        out_shape=[
            jax.ShapeDtypeStruct((rows // 2, wide), F32),
            jax.ShapeDtypeStruct((rows // 2, wide), send_type),
        ],
        compiler_params=pltpu.CompilerParams(vmem_limit_bytes=LIMIT),
        cost_estimate=pl.CostEstimate(
            flops=rows * wide, bytes_accessed=8 * rows * wide, transcendentals=0
        ),
        name="split_sum",
    )(index, own, got)


def assemble_kernel(spots, chunks, place_ref, *refs):
    parts = refs[: len(spots)]
    out, got_ref, wide_ref, got_sems, sems = refs[-5:]
    block, strip = parts[0].shape
    got = start_copies([(part, got_ref.at[i]) for i, part in enumerate(parts)], got_sems)
    copies = []
    for i, (chunk, side, code) in enumerate(spots):
        row = pl.multiple_of((place_ref[5] ^ code) * block, block)
        column = pl.multiple_of(((place_ref[0] ^ side) * chunks + chunk) * strip, strip)
        got[i].wait()
        wide_ref[i] = got_ref[i].astype(F32)
        copy = pltpu.make_async_copy(
            wide_ref.at[i], out.at[pl.ds(row, block), pl.ds(column, strip)], sems.at[i]
        )
        copy.start()
        copies.append(copy)
    for copy in copies:
        copy.wait()


def assemble(place, parts, spots, count, chunks, before):
    block, strip = parts[0].shape
    rows, wide = block * count, strip * 2 * chunks
    return pl.pallas_call(
        functools.partial(assemble_kernel, spots, chunks),
        in_specs=[SMEM] + [ANY] * (len(parts) + len(before)),
        out_specs=ANY,
        out_shape=jax.ShapeDtypeStruct((rows, wide), F32),
        input_output_aliases={1 + len(parts): 0} if before else {},
        scratch_shapes=[
            pltpu.VMEM((len(parts), block, strip), BF16),
            pltpu.VMEM((len(parts), block, strip), F32),
            pltpu.SemaphoreType.DMA((len(parts),)),
            pltpu.SemaphoreType.DMA((len(parts),)),
        ],
        compiler_params=pltpu.CompilerParams(vmem_limit_bytes=LIMIT),
        cost_estimate=pl.CostEstimate(
            flops=rows * wide, bytes_accessed=6 * rows * wide, transcendentals=0
        ),
        name="assemble",
    )(place, *parts, *before)


def swap(block, axis, bit):
    size = lax.axis_size(axis)
    return lax.ppermute(block, axis, [(i, i ^ bit) for i in range(size)])


def gather_blocks(block, axis, late=None):
    blocks, bit = [block], lax.axis_size(axis) // 2
    while bit >= 1:
        sources = blocks if bit > 1 or late is None else [late] + blocks[1:]
        blocks = blocks + [swap(item, axis, bit) for item in sources]
        bit //= 2
    return blocks


def gather_parts(part):
    far = swap(part, "mdl", 2)
    return [part, swap(part, "mdl", 1), far, swap(far, "mdl", 1)], far


def product(left, right):
    return jnp.einsum("rh,rd->hd", left, right, preferred_element_type=F32)


def halve(keep, got):
    total = keep + got.astype(F32)
    side = total.shape[0] // 2
    return total[:side], total[side:].astype(BF16)


def on_device(
    obs,
    a_query,
    a_keyval,
    a_out,
    w_policy,
    c_in,
    c_query,
    c_keyval,
    c_out,
    w_value,
    actions,
    advantages,
    old_logp,
    returns,
    robot_count,
):
    row_count = obs.shape[1]
    batch_index = lax.axis_index("sec")
    rep_index = lax.axis_index("rep")
    rep_count = lax.axis_size("rep")
    robot_total = robot_count[batch_index]
    live_sum = jnp.sum(robot_count)
    live_total = live_sum.astype(F32)
    first_row = rep_index * row_count
    live_mask = first_row + lax.iota(jnp.int32, row_count) < robot_total
    mdl_count = lax.axis_size("mdl")
    assert mdl_count == 4 and lax.axis_size("sec") == 2
    mdl_index = lax.axis_index("mdl")
    value_rows = row_count // mdl_count
    score_scale = HEAD ** (-0.5) * LOG2E
    rep_place = rep_index.reshape(1).astype(jnp.int32)

    place = jnp.stack(
        [batch_index, mdl_index, first_row, robot_total, live_sum, rep_index]
        + [
            jnp.clip(robot_total - (rep_index ^ code) * row_count, 0, row_count)
            for code in gather_codes(rep_count)
        ]
    ).astype(jnp.int32)

    obs_in = obs[0]
    keyval, factor_a = first_projection(obs_in, a_keyval)
    a_far = swap(a_out, "mdl", 2)
    queries = query_projection(obs_in, a_query, factor_a, score_scale)
    late_keyval, queries = tied(keyval, queries)
    pieces_k = gather_blocks(keyval, "rep", late_keyval)
    state = attend_call(queries, pieces_k[:-1], 0, place, [])
    attended = attend_call(queries, pieces_k[-1:], rep_count - 1, place, state)
    attended, a_far = tied(attended, a_far)
    attended_far = swap(attended, "mdl", 2)
    attended_near = swap(attended, "mdl", 1)
    near_sum = near_rows(obs_in, [attended, attended_near], [a_out, swap(a_out, "mdl", 1)])
    attended_far, near_sum = tied(attended_far, near_sum)
    hidden, embed_part = hidden_rows(
        near_sum,
        [attended_far, swap(attended_far, "mdl", 1)],
        [a_far, swap(a_far, "mdl", 1)],
        c_in,
    )

    embed_parts, _ = gather_parts(embed_part)
    critic_keyval, factor_c, embedded = join_rows(place, embed_parts, c_keyval)
    critic_queries = (dot(embedded, c_query) * (factor_c[:, :1] * score_scale)).astype(BF16)

    late_hidden, critic_keyval = tied(hidden, critic_keyval)
    source = late_hidden.astype(F32)
    factor_h = row_factor(source)
    late_keyval, factor_h = tied(critic_keyval, factor_h)
    pieces_c = gather_blocks(critic_keyval, "rep", late_keyval)
    logits = dot(late_hidden, w_policy) * factor_h
    log_probs = jax.nn.log_softmax(logits, axis=-1)
    onehot = (
        actions[0][:, None] == lax.broadcasted_iota(jnp.int32, logits.shape, 1)
    ).astype(F32)
    chosen = jnp.sum(onehot * log_probs, axis=-1)
    prob_ratio = jnp.exp(chosen - old_logp[0])
    plain_term = prob_ratio * advantages[0]
    bounded = jnp.clip(prob_ratio, 1.0 - clip_range, 1.0 + clip_range) * advantages[0]
    slope = jnp.where(live_mask & (plain_term <= bounded), -plain_term / live_total, F32(0.0))
    dlogits = slope[:, None] * (onehot - jnp.exp(log_probs))
    along = jnp.sum(dlogits * logits, axis=-1, keepdims=True) / source.shape[1]
    dnormed = dot(dlogits.astype(BF16), w_policy.T)
    dhidden = (factor_h * (dnormed - source * (factor_h * along))).astype(BF16)
    half_a = dhidden.shape[1] // 2
    got_a = swap(
        product(attended, lax.dynamic_slice_in_dim(dhidden, (1 - batch_index) * half_a, half_a, 1))
        .astype(BF16),
        "sec",
        1,
    )
    own_a = product(attended, lax.dynamic_slice_in_dim(dhidden, batch_index * half_a, half_a, 1))

    wide = w_value.shape[0]
    target = lax.dynamic_slice_in_dim(returns[0], mdl_index * value_rows, value_rows, 0)
    emb_mine = lax.dynamic_slice_in_dim(embedded, mdl_index * value_rows, value_rows, 0)
    critic_queries, own_a, w_row, target, emb_mine = tied(
        critic_queries,
        own_a,
        w_value.reshape(1, wide),
        target.reshape(value_rows, 1),
        emb_mine,
    )
    state_c = attend_call(critic_queries, pieces_c[:-1], 0, place, [])
    *state_c, got_a, pieces_c[-1] = tied(*state_c, got_a, pieces_c[-1])
    keep_a, send_a = split_sum(rep_place, own_a, got_a, rep_count)
    *state_c, send_a = tied(*state_c, send_a)
    moved_a = swap(send_a.astype(BF16), "rep", 1)
    critic_attended = attend_call(critic_queries, pieces_c[-1:], rep_count - 1, place, state_c)

    send_m, keep_m, att_rows = part_rows(place, critic_attended, c_out)
    near_m = swap(send_m, "mdl", 1)
    send_y = (keep_m[value_rows:] + near_m[value_rows:].astype(F32)).astype(BF16)
    got_y = swap(send_y, "mdl", 2)
    att_there = swap(critic_attended, "sec", 1)
    got_y, moved_a = tied(got_y, moved_a)
    bit = 2
    while bit < rep_count:
        keep_a, send_a = halve(keep_a, moved_a)
        moved_a = swap(send_a, "rep", bit)
        bit *= 2
    value_wide, d_other, d_own = mixed_rows(
        place, emb_mine, keep_m, near_m, got_y, w_row, target
    )

    d_there = swap(d_other, "sec", 1)
    d_far = swap(d_own, "mdl", 2)
    there_far = swap(d_other, ("sec", "mdl"), mdl_count | 2)
    d_there, moved_a = tied(d_there, moved_a)
    total_a = (keep_a + moved_a.astype(F32)).astype(BF16)
    own_rows = jnp.concatenate(
        [d_own, d_far, swap(d_own, "mdl", 1), swap(d_far, "mdl", 1)], axis=0
    )
    there_rows = jnp.concatenate(
        [d_there, there_far, swap(d_there, "mdl", 1), swap(there_far, "mdl", 1)], axis=0
    )
    att_there = jnp.concatenate(
        [
            lax.dynamic_slice_in_dim(att_there, (mdl_index ^ code) * value_rows, value_rows, 0)
            for code in ROWS
        ],
        axis=0,
    )
    value_part, there_rows = tied(value_wide[:, 0], there_rows)
    codes = gather_codes(rep_count)

    strip = d_own.shape[1] // CHUNKS
    chunks = []
    for c in range(CHUNKS):
        span = slice(c * strip, (c + 1) * strip)
        keep, send = split_sum(
            rep_place,
            product(att_rows, own_rows[:, span]),
            product(att_there, there_rows[:, span]),
            rep_count,
        )
        chunks.append([keep, [swap(send.astype(BF16), "rep", 1)], [], [], []])
    levels = rep_count.bit_length() - 1
    last = 2 * levels + CHUNKS - 2
    first_swap = [swap(total_a, "rep", rep_count // 2)]
    chunks.append([None, first_swap, [total_a], [swap(total_a, "sec", 1)], []])
    starts = list(range(CHUNKS)) + [-levels]
    for tick in range(last + 1):
        turn = [c for c, start in enumerate(starts) if 0 <= tick - start < 2 * levels]
        waited = [item for c in turn for item in chunks[c][1] + chunks[c][3]]
        extra = []
        if tick == 0:
            extra = [chunks[c][0] for c in range(1, CHUNKS)]
        if tick == levels:
            extra = chunks[CHUNKS][3]
        if tick == 2 * levels - 1:
            _, _, mine, crossing, theirs = chunks[CHUNKS]
            spots = [(0, side, code) for side in range(2) for code in codes]
            extra = [assemble(place, mine + theirs + crossing, spots, rep_count, 1, [])]
        if tick == last:
            done = [
                (item, (c, side, code))
                for c in range(CHUNKS)
                for side in range(2)
                for item, code in zip(chunks[c][2 + 2 * side], codes)
            ]
            extra = [assemble(place, *zip(*done), rep_count, CHUNKS, [])]
        outs = list(tied(*waited, *extra))
        if tick == 0:
            for c in range(1, CHUNKS):
                chunks[c][0] = outs[len(waited) + c - 1]
        if tick == levels:
            chunks[CHUNKS][3] = outs[len(waited) :]
        if tick == 2 * levels - 1:
            actor_summed = outs[-1]
        if tick == last:
            result = outs[-1]
        for c in turn:
            keep, pending, mine, crossing, theirs = chunks[c]
            arrived, outs = outs[: len(pending)], outs[len(pending) :]
            crossed, outs = outs[: len(crossing)], outs[len(crossing) :]
            theirs = theirs + crossed
            level = tick - starts[c] + 1
            if level < levels:
                keep, send = halve(keep, arrived[0])
                pending = [swap(send, "rep", 1 << level)]
            else:
                fresh = arrived
                if level == levels:
                    fresh = [(keep + arrived[0].astype(F32)).astype(BF16)]
                mine = mine + fresh
                crossing = [swap(block, "sec", 1) for block in fresh]
                bit = rep_count >> (level - levels + 1)
                pending = [swap(block, "rep", bit) for block in mine] if bit else []
            chunks[c] = [keep, pending, mine, crossing, theirs]
    rest = [
        (item, (c, side, code))
        for c in range(CHUNKS)
        for side, group in enumerate((chunks[c][2], chunks[c][4] + chunks[c][3]))
        for item, code in zip(group, codes)
        if (c, side, code) not in [spot for _, spot in done]
    ]
    result = assemble(place, *zip(*rest), rep_count, CHUNKS, [result])

    return (value_part[None, :], actor_summed, result)


def solution(mesh):
    return jax.shard_map(
        on_device,
        mesh=mesh,
        in_specs=(
            P("sec", "rep", None),
            P(None, "mdl"),
            P(None, None, "mdl"),
            P("mdl", None),
            P(),
            P(None, "mdl"),
            P(None, "mdl"),
            P(None, None, "mdl"),
            P("mdl", None),
            P(),
            P("sec", "rep"),
            P("sec", "rep"),
            P("sec", "rep"),
            P("sec", "rep"),
            P(),
        ),
        out_specs=(P("sec", ("rep", "mdl")), P("mdl", None), P("mdl", None)),
        check_vma=False,
    )
```

```python
import functools
import math

import jax
import jax.numpy as jnp
from jax import lax
from jax.experimental import pallas as pl
from jax.experimental.pallas import tpu as pltpu
from jax.sharding import PartitionSpec as P

HEAD = 128
epsilon = 1e-05
clip_range = 0.2
masked_score = -1e30
LOG2E = 1.4426950408889634
F32 = jnp.float32
BF16 = jnp.bfloat16
CHUNKS = 1
TABLE = 6
ROWS = (0, 2, 1, 3)
LIMIT = 40 * 2**20
HIGH = 56 * 2**20
VMEM = pl.BlockSpec(memory_space=pltpu.VMEM)
SMEM = pl.BlockSpec(memory_space=pltpu.SMEM)
ANY = pl.BlockSpec(memory_space=pl.ANY)
HBM = pl.BlockSpec(memory_space=pltpu.HBM)


def dot(a, b):
    return jnp.dot(a, b, preferred_element_type=F32)


def tied(*items):
    return lax.optimization_barrier(items)


def row_factor(source):
    return lax.rsqrt(jnp.mean(source * source, axis=-1, keepdims=True) + epsilon)


def start_copies(pairs, sems):
    copies = [
        pltpu.make_async_copy(source, target, sems.at[i])
        for i, (source, target) in enumerate(pairs)
    ]
    for copy in copies:
        copy.start()
    return copies


def first_kernel(obs_hbm, w_hbm, kv_ref, factor_ref, obs_ref, w_ref, sems):
    rows, depth = obs_ref.shape
    width = w_hbm.shape[2]
    block = rows // 2
    spans = [slice(i * block, (i + 1) * block) for i in range(2)]
    copies = start_copies(
        [(w_hbm.at[c], w_ref.at[:, c * width : (c + 1) * width]) for c in range(2)]
        + [(obs_hbm.at[span], obs_ref.at[span]) for span in spans],
        sems,
    )
    for i, span in enumerate(spans):
        copies[2 + i].wait()
        part = obs_ref[span, :]
        factor = row_factor(part.astype(F32))
        if i == 0:
            copies[0].wait()
            copies[1].wait()
        both = dot(part, w_ref[...]) * factor
        kv_ref[0, span, :] = both[:, :width].astype(BF16)
        kv_ref[1, span, :] = both[:, width:].astype(BF16)
        factor_ref[span, :] = jnp.broadcast_to(factor, (block, HEAD))


def first_projection(obs, w_keyval):
    rows, depth = obs.shape
    width = w_keyval.shape[2]
    return pl.pallas_call(
        first_kernel,
        in_specs=[HBM] * 2,
        out_specs=[VMEM] * 2,
        out_shape=[
            jax.ShapeDtypeStruct((2, rows, width), BF16),
            jax.ShapeDtypeStruct((rows, HEAD), F32),
        ],
        scratch_shapes=[
            pltpu.VMEM((rows, depth), BF16),
            pltpu.VMEM((depth, 2 * width), BF16),
            pltpu.SemaphoreType.DMA((4,)),
        ],
        compiler_params=pltpu.CompilerParams(vmem_limit_bytes=HIGH),
        cost_estimate=pl.CostEstimate(
            flops=4 * rows * depth * width, bytes_accessed=2 * rows * depth, transcendentals=0
        ),
        name="first_projection",
    )(obs, w_keyval)


def query_kernel(scale, obs_hbm, w_hbm, factor_ref, q_ref, obs_ref, w_ref, sems):
    for copy in start_copies([(w_hbm, w_ref), (obs_hbm, obs_ref)], sems):
        copy.wait()
    q_ref[...] = (dot(obs_ref[...], w_ref[...]) * (factor_ref[:, :1] * scale)).astype(BF16)


def query_projection(obs, w_query, factor, scale):
    rows, depth = obs.shape
    width = w_query.shape[1]
    return pl.pallas_call(
        functools.partial(query_kernel, scale),
        in_specs=[HBM, HBM, VMEM],
        out_specs=VMEM,
        out_shape=jax.ShapeDtypeStruct((rows, width), BF16),
        scratch_shapes=[
            pltpu.VMEM((rows, depth), BF16),
            pltpu.VMEM((depth, width), BF16),
            pltpu.SemaphoreType.DMA((2,)),
        ],
        compiler_params=pltpu.CompilerParams(vmem_limit_bytes=LIMIT),
        cost_estimate=pl.CostEstimate(
            flops=2 * rows * depth * width, bytes_accessed=2 * rows * depth, transcendentals=0
        ),
        name="query_projection",
    )(obs, w_query, factor)


def attend_blocks(groups, units, first, left_ref, q_ref, kv_refs):
    def fetch(head, span):
        kv_head = head // groups
        columns = slice(kv_head * HEAD, (kv_head + 1) * HEAD)
        query = q_ref[span, head * HEAD : (head + 1) * HEAD]
        lane = lax.broadcasted_iota(jnp.int32, query.shape, 1)
        query = jnp.concatenate([query, (lane == 0).astype(BF16)], axis=1)
        scores = []
        for p, ref in enumerate(kv_refs):
            keys = ref[0, :, columns]
            key = lax.broadcasted_iota(jnp.int32, keys.shape, 0)
            lane = lax.broadcasted_iota(jnp.int32, keys.shape, 1)
            dead = (key >= left_ref[first + p]) & (lane == 0)
            bias = jnp.where(dead, F32(masked_score), F32(0.0)).astype(BF16)
            keys = jnp.concatenate([keys, bias], axis=1)
            scores.append(
                lax.dot_general(
                    query, keys, (((1,), (1,)), ((), ())), preferred_element_type=F32
                )
            )
        return scores

    def values(head, p):
        kv_head = head // groups
        vals = kv_refs[p][1, :, kv_head * HEAD : (kv_head + 1) * HEAD]
        return jnp.concatenate([vals, jnp.ones_like(vals)], axis=1)

    ahead = fetch(*units[0])
    for i, (head, span) in enumerate(units):
        scores = ahead
        if i + 1 < len(units):
            ahead = fetch(*units[i + 1])
        yield head, span, scores, functools.partial(values, head)


def weigh(scores, top, values):
    total = None
    for p, part in enumerate(scores):
        both = dot(jnp.exp2(part - top).astype(BF16), values(p))
        total = both if total is None else total + both
    return total


def highest(scores):
    return functools.reduce(
        jnp.maximum, [jnp.max(part, axis=-1, keepdims=True) for part in scores]
    )


def open_kernel(groups, units, first, left_ref, q_ref, *refs):
    *kv_refs, wide_ref, top_ref = refs
    for head, span, scores, values in attend_blocks(
        groups, units, first, left_ref, q_ref, kv_refs
    ):
        top = highest(scores)
        wide_ref[span, head * 2 * HEAD : (head + 1) * 2 * HEAD] = weigh(scores, top, values)
        top_ref[span, head * HEAD : (head + 1) * HEAD] = jnp.broadcast_to(
            top, (top.shape[0], HEAD)
        )


def close_kernel(groups, units, first, left_ref, q_ref, wide_ref, top_ref, *refs):
    *kv_refs, o_ref = refs
    for head, span, scores, values in attend_blocks(
        groups, units, first, left_ref, q_ref, kv_refs
    ):
        before = top_ref[span, head * HEAD : head * HEAD + 1]
        top = jnp.maximum(before, highest(scores))
        wide = wide_ref[span, head * 2 * HEAD : (head + 1) * 2 * HEAD]
        wide = wide * jnp.exp2(before - top) + weigh(scores, top, values)
        o_ref[span, head * HEAD : (head + 1) * HEAD] = (
            wide[:, :HEAD] / wide[:, HEAD:]
        ).astype(BF16)


def attend_call(queries, pieces, first, place, state):
    rows, width = queries.shape
    heads = width // HEAD
    groups = heads // (pieces[0].shape[2] // HEAD)
    block = min(rows, 256)
    units = [
        (head, slice(i, i + block)) for head in range(heads) for i in range(0, rows, block)
    ]
    count = len(pieces) * pieces[0].shape[1]
    weight = 1 if state else 24
    if state:
        body, name = close_kernel, "attend_close"
        out = jax.ShapeDtypeStruct((rows, width), BF16)
    else:
        body, name = open_kernel, "attend_open"
        out = [
            jax.ShapeDtypeStruct((rows, 2 * width), F32),
            jax.ShapeDtypeStruct((rows, width), F32),
        ]
    return pl.pallas_call(
        functools.partial(body, groups, units, TABLE + first),
        in_specs=[SMEM] + [VMEM] * (1 + len(state) + len(pieces)),
        out_specs=VMEM if state else [VMEM] * 2,
        out_shape=out,
        compiler_params=pltpu.CompilerParams(vmem_limit_bytes=LIMIT),
        cost_estimate=pl.CostEstimate(
            flops=weight * rows * count * width,
            bytes_accessed=4 * rows * width,
            transcendentals=rows * count,
        ),
        name=name,
    )(place, queries, *state, *pieces)


def near_kernel(obs_hbm, t0, t1, w0, w1, sum_ref, obs_ref, w_ref, sems):
    inner, depth = w0.shape
    tile = depth // 3
    pairs = [(obs_hbm, obs_ref), (w0, w_ref.at[:inner]), (w1, w_ref.at[inner:])]
    for copy in start_copies(pairs, sems):
        copy.wait()
    for i in range(3):
        strip = slice(i * tile, (i + 1) * tile)
        parts = jnp.concatenate([t0[...], t1[...]], axis=1)
        sum_ref[:, strip] = obs_ref[:, strip].astype(F32) + dot(parts, w_ref[:, strip])


def near_rows(obs, parts, weights):
    rows, depth = obs.shape
    inner = weights[0].shape[0]
    return pl.pallas_call(
        near_kernel,
        in_specs=[HBM] + [VMEM] * 2 + [HBM, ANY],
        out_specs=VMEM,
        out_shape=jax.ShapeDtypeStruct((rows, depth), F32),
        scratch_shapes=[
            pltpu.VMEM((rows, depth), BF16),
            pltpu.VMEM((2 * inner, depth), BF16),
            pltpu.SemaphoreType.DMA((3,)),
        ],
        compiler_params=pltpu.CompilerParams(vmem_limit_bytes=LIMIT),
        cost_estimate=pl.CostEstimate(
            flops=4 * rows * depth * inner, bytes_accessed=4 * depth * inner, transcendentals=0
        ),
        name="near_rows",
    )(obs, *parts, *weights)


def hidden_kernel(sum_ref, t2, t3, w2, w3, c_hbm, o_ref, emb_ref, w_ref, c_ref, sems):
    inner, depth = w2.shape
    tile = depth // 3
    copies = start_copies(
        [(w2, w_ref.at[:inner]), (w3, w_ref.at[inner:]), (c_hbm, c_ref)], sems
    )
    copies[0].wait()
    copies[1].wait()
    for i in range(3):
        strip = slice(i * tile, (i + 1) * tile)
        parts = jnp.concatenate([t2[...], t3[...]], axis=1)
        o_ref[:, strip] = (sum_ref[:, strip] + dot(parts, w_ref[:, strip])).astype(BF16)
    copies[2].wait()
    emb_ref[...] = dot(o_ref[...], c_ref[...]).astype(BF16)


def hidden_rows(near_sum, parts, weights, c_in):
    rows, depth = near_sum.shape
    inner = weights[0].shape[0]
    width = c_in.shape[1]
    return pl.pallas_call(
        hidden_kernel,
        in_specs=[VMEM] * 3 + [ANY] * 2 + [HBM],
        out_specs=[VMEM] * 2,
        out_shape=[
            jax.ShapeDtypeStruct((rows, depth), BF16),
            jax.ShapeDtypeStruct((rows, width), BF16),
        ],
        scratch_shapes=[
            pltpu.VMEM((2 * inner, depth), BF16),
            pltpu.VMEM((depth, width), BF16),
            pltpu.SemaphoreType.DMA((3,)),
        ],
        compiler_params=pltpu.CompilerParams(vmem_limit_bytes=LIMIT),
        cost_estimate=pl.CostEstimate(
            flops=8 * rows * depth * inner, bytes_accessed=8 * depth * inner, transcendentals=0
        ),
        name="hidden_rows",
    )(near_sum, *parts, *weights, c_in)


def join_kernel(place_ref, e0, e1, e2, e3, wkv_any, kv_ref, factor_ref, emb_ref, wkv_ref, sems):
    rows, wide = emb_ref.shape
    width = wkv_any.shape[2]
    strip = e0.shape[1]
    copies = start_copies(
        [(wkv_any.at[c], wkv_ref.at[:, c * width : (c + 1) * width]) for c in range(2)], sems
    )
    starts = [pl.multiple_of((place_ref[1] ^ code) * strip, strip) for code in range(4)]
    parts = (e0, e1, e2, e3)
    for copy in copies:
        copy.wait()
    block = rows // 2
    for i in range(2):
        span = slice(i * block, (i + 1) * block)
        square, both = 0.0, 0.0
        for part, start in zip(parts, starts):
            emb = part[span, :]
            wide_emb = emb.astype(F32)
            square = square + jnp.sum(wide_emb * wide_emb, axis=-1, keepdims=True)
            both = both + dot(emb, wkv_ref[pl.ds(start, strip), :])
            emb_ref[span, pl.ds(start, strip)] = emb
        factor = lax.rsqrt(square / wide + epsilon)
        both = both * factor
        kv_ref[0, span, :] = both[:, :width].astype(BF16)
        kv_ref[1, span, :] = both[:, width:].astype(BF16)
        factor_ref[span, :] = jnp.broadcast_to(factor, (block, HEAD))


def join_rows(place, parts, w_keyval):
    rows, strip = parts[0].shape
    wide = 4 * strip
    width = w_keyval.shape[2]
    return pl.pallas_call(
        join_kernel,
        in_specs=[SMEM] + [VMEM] * 4 + [HBM],
        out_specs=[VMEM] * 3,
        out_shape=[
            jax.ShapeDtypeStruct((2, rows, width), BF16),
            jax.ShapeDtypeStruct((rows, HEAD), F32),
            jax.ShapeDtypeStruct((rows, wide), BF16),
        ],
        scratch_shapes=[pltpu.VMEM((wide, 2 * width), BF16), pltpu.SemaphoreType.DMA((2,))],
        compiler_params=pltpu.CompilerParams(vmem_limit_bytes=LIMIT),
        cost_estimate=pl.CostEstimate(
            flops=4 * rows * wide * width, bytes_accessed=4 * rows * wide, transcendentals=0
        ),
        name="join_rows",
    )(place, *parts, w_keyval)


def part_kernel(place_ref, att_ref, c_hbm, send_ref, keep_ref, order_ref, c_ref, sems):
    rows, inner = att_ref.shape
    wide = c_ref.shape[1]
    block = rows // 4
    half = inner // 2
    spans = [slice(i * half, (i + 1) * half) for i in range(2)]
    copies = start_copies([(c_hbm.at[span], c_ref.at[span]) for span in spans], sems)
    for at, code in enumerate(ROWS):
        start = pl.multiple_of((place_ref[1] ^ code) * block, block)
        order_ref[at * block : (at + 1) * block, :] = att_ref[pl.ds(start, block), :]
    for copy in copies:
        copy.wait()
    tile = 512
    for out, source in ((send_ref, order_ref[2 * block :, :]), (keep_ref, order_ref[: 2 * block, :])):
        for j in range(wide // tile):
            columns = slice(j * tile, (j + 1) * tile)
            out[:, columns] = dot(source, c_ref[:, columns]).astype(out.dtype)


def part_rows(place, attended, c_out):
    rows, inner = attended.shape
    wide = c_out.shape[1]
    return pl.pallas_call(
        part_kernel,
        in_specs=[SMEM, VMEM, HBM],
        out_specs=[VMEM] * 3,
        out_shape=[
            jax.ShapeDtypeStruct((rows // 2, wide), BF16),
            jax.ShapeDtypeStruct((rows // 2, wide), F32),
            jax.ShapeDtypeStruct((rows, inner), BF16),
        ],
        scratch_shapes=[pltpu.VMEM((inner, wide), BF16), pltpu.SemaphoreType.DMA((2,))],
        compiler_params=pltpu.CompilerParams(vmem_limit_bytes=LIMIT),
        cost_estimate=pl.CostEstimate(
            flops=2 * rows * wide * inner, bytes_accessed=8 * wide * inner, transcendentals=0
        ),
        name="part_rows",
    )(place, attended, c_out)


def mixed_kernel(
    place_ref, emb_ref, keep_ref, near_ref, got_ref, wv_ref, ret_ref,
    value_ref, other_ref, own_ref, mixed_ref,
):
    rows, wide = got_ref.shape
    half = wide // 2
    block = 32
    base = place_ref[1] * rows
    live_total = place_ref[4].astype(F32)

    @pl.loop(0, rows // block)
    def _(i):
        start = pl.multiple_of(i * block, block)
        span = pl.ds(start, block)
        mixed = emb_ref[span, :].astype(F32) + (
            keep_ref[span, :] + near_ref[span, :].astype(F32) + got_ref[span, :].astype(F32)
        )
        mixed_ref[...] = mixed
        factor = row_factor(mixed)
        value = factor * jnp.sum(mixed * wv_ref[...].astype(F32), axis=-1, keepdims=True)
        row = place_ref[2] + base + start + lax.broadcasted_iota(jnp.int32, (block, 1), 0)
        gap = jnp.where(row < place_ref[3], value - ret_ref[span, :], F32(0.0)) / live_total
        lead = factor * gap
        pull = lead * factor * value / wide
        value_ref[span, :] = jnp.broadcast_to(value, (block, HEAD))
        for out, side in ((own_ref, place_ref[0]), (other_ref, 1 - place_ref[0])):
            columns = pl.ds(pl.multiple_of(side * half, half), half)
            part = mixed_ref[:, columns]
            out[span, :] = (lead * wv_ref[:, columns].astype(F32) - part * pull).astype(BF16)


def mixed_rows(place, embedded, keep, near, got, w_value, returns):
    rows, wide = got.shape
    return pl.pallas_call(
        mixed_kernel,
        in_specs=[SMEM] + [VMEM] * 6,
        out_specs=[VMEM] * 3,
        out_shape=[
            jax.ShapeDtypeStruct((rows, HEAD), F32),
            jax.ShapeDtypeStruct((rows, wide // 2), BF16),
            jax.ShapeDtypeStruct((rows, wide // 2), BF16),
        ],
        scratch_shapes=[pltpu.VMEM((32, wide), F32)],
        compiler_params=pltpu.CompilerParams(vmem_limit_bytes=LIMIT),
        cost_estimate=pl.CostEstimate(
            flops=10 * rows * wide, bytes_accessed=12 * rows * wide, transcendentals=0
        ),
        name="mixed_rows",
    )(place, embedded, keep, near, got, w_value, returns)


def gather_codes(size):
    codes, bit = [0], size // 2
    while bit >= 1:
        codes = codes + [code ^ bit for code in codes]
        bit //= 2
    return codes


def split_kernel(codes, index_ref, own_ref, got_ref, keep_ref, send_ref):
    block = own_ref.shape[0] // len(codes)
    side = len(codes) // 2
    for k, code in enumerate(codes):
        span = pl.ds(pl.multiple_of((index_ref[0] ^ code) * block, block), block)
        out = (keep_ref, send_ref)[k // side]
        at = k % side * block
        total = own_ref[span, :] + got_ref[span, :].astype(F32)
        out[at : at + block, :] = total.astype(out.dtype)


def split_sum(index, own, got, count):
    rows, wide = own.shape
    if (rows // count) % 16:
        got = got.astype(F32)
    send_type = BF16 if (rows // count) % 16 == 0 else F32
    return pl.pallas_call(
        functools.partial(split_kernel, gather_codes(count)),
        in_specs=[SMEM, VMEM, VMEM],
        out_specs=[VMEM] * 2,
        out_shape=[
            jax.ShapeDtypeStruct((rows // 2, wide), F32),
            jax.ShapeDtypeStruct((rows // 2, wide), send_type),
        ],
        compiler_params=pltpu.CompilerParams(vmem_limit_bytes=LIMIT),
        cost_estimate=pl.CostEstimate(
            flops=rows * wide, bytes_accessed=8 * rows * wide, transcendentals=0
        ),
        name="split_sum",
    )(index, own, got)


def assemble_kernel(spots, chunks, place_ref, *refs):
    parts = refs[: len(spots)]
    out, got_ref, wide_ref, got_sems, sems = refs[-5:]
    block, strip = parts[0].shape
    got = start_copies([(part, got_ref.at[i]) for i, part in enumerate(parts)], got_sems)
    copies = []
    for i, (chunk, side, code) in enumerate(spots):
        row = pl.multiple_of((place_ref[5] ^ code) * block, block)
        column = pl.multiple_of(((place_ref[0] ^ side) * chunks + chunk) * strip, strip)
        got[i].wait()
        wide_ref[i] = got_ref[i].astype(F32)
        copy = pltpu.make_async_copy(
            wide_ref.at[i], out.at[pl.ds(row, block), pl.ds(column, strip)], sems.at[i]
        )
        copy.start()
        copies.append(copy)
    for copy in copies:
        copy.wait()


def assemble(place, parts, spots, count, chunks, before):
    block, strip = parts[0].shape
    rows, wide = block * count, strip * 2 * chunks
    return pl.pallas_call(
        functools.partial(assemble_kernel, spots, chunks),
        in_specs=[SMEM] + [ANY] * (len(parts) + len(before)),
        out_specs=ANY,
        out_shape=jax.ShapeDtypeStruct((rows, wide), F32),
        input_output_aliases={1 + len(parts): 0} if before else {},
        scratch_shapes=[
            pltpu.VMEM((len(parts), block, strip), BF16),
            pltpu.VMEM((len(parts), block, strip), F32),
            pltpu.SemaphoreType.DMA((len(parts),)),
            pltpu.SemaphoreType.DMA((len(parts),)),
        ],
        compiler_params=pltpu.CompilerParams(vmem_limit_bytes=LIMIT),
        cost_estimate=pl.CostEstimate(
            flops=rows * wide, bytes_accessed=6 * rows * wide, transcendentals=0
        ),
        name="assemble",
    )(place, *parts, *before)


def swap(block, axis, bit):
    size = lax.axis_size(axis)
    return lax.ppermute(block, axis, [(i, i ^ bit) for i in range(size)])


def gather_blocks(block, axis, late=None):
    blocks, bit = [block], lax.axis_size(axis) // 2
    while bit >= 1:
        sources = blocks if bit > 1 or late is None else [late] + blocks[1:]
        blocks = blocks + [swap(item, axis, bit) for item in sources]
        bit //= 2
    return blocks


def gather_parts(part):
    far = swap(part, "mdl", 2)
    return [part, swap(part, "mdl", 1), far, swap(far, "mdl", 1)], far


def product(left, right):
    return jnp.einsum("rh,rd->hd", left, right, preferred_element_type=F32)


def halve(keep, got):
    total = keep + got.astype(F32)
    side = total.shape[0] // 2
    return total[:side], total[side:].astype(BF16)


def on_device(
    obs,
    a_query,
    a_keyval,
    a_out,
    w_policy,
    c_in,
    c_query,
    c_keyval,
    c_out,
    w_value,
    actions,
    advantages,
    old_logp,
    returns,
    robot_count,
):
    row_count = obs.shape[1]
    batch_index = lax.axis_index("sec")
    rep_index = lax.axis_index("rep")
    rep_count = lax.axis_size("rep")
    robot_total = robot_count[batch_index]
    live_sum = jnp.sum(robot_count)
    live_total = live_sum.astype(F32)
    first_row = rep_index * row_count
    live_mask = first_row + lax.iota(jnp.int32, row_count) < robot_total
    mdl_count = lax.axis_size("mdl")
    assert mdl_count == 4 and lax.axis_size("sec") == 2
    mdl_index = lax.axis_index("mdl")
    value_rows = row_count // mdl_count
    score_scale = HEAD ** (-0.5) * LOG2E
    rep_place = rep_index.reshape(1).astype(jnp.int32)

    place = jnp.stack(
        [batch_index, mdl_index, first_row, robot_total, live_sum, rep_index]
        + [
            jnp.clip(robot_total - (rep_index ^ code) * row_count, 0, row_count)
            for code in gather_codes(rep_count)
        ]
    ).astype(jnp.int32)

    obs_in = obs[0]
    keyval, factor_a = first_projection(obs_in, a_keyval)
    a_far = swap(a_out, "mdl", 2)
    queries = query_projection(obs_in, a_query, factor_a, score_scale)
    late_keyval, queries = tied(keyval, queries)
    pieces_k = gather_blocks(keyval, "rep", late_keyval)
    state = attend_call(queries, pieces_k[:-1], 0, place, [])
    attended = attend_call(queries, pieces_k[-1:], rep_count - 1, place, state)
    attended, a_far = tied(attended, a_far)
    attended_far = swap(attended, "mdl", 2)
    attended_near = swap(attended, "mdl", 1)
    near_sum = near_rows(obs_in, [attended, attended_near], [a_out, swap(a_out, "mdl", 1)])
    attended_far, near_sum = tied(attended_far, near_sum)
    hidden, embed_part = hidden_rows(
        near_sum,
        [attended_far, swap(attended_far, "mdl", 1)],
        [a_far, swap(a_far, "mdl", 1)],
        c_in,
    )

    embed_parts, _ = gather_parts(embed_part)
    critic_keyval, factor_c, embedded = join_rows(place, embed_parts, c_keyval)
    critic_queries = (dot(embedded, c_query) * (factor_c[:, :1] * score_scale)).astype(BF16)

    late_hidden, critic_keyval = tied(hidden, critic_keyval)
    source = late_hidden.astype(F32)
    factor_h = row_factor(source)
    late_keyval, factor_h = tied(critic_keyval, factor_h)
    pieces_c = gather_blocks(critic_keyval, "rep", late_keyval)
    logits = dot(late_hidden, w_policy) * factor_h
    log_probs = jax.nn.log_softmax(logits, axis=-1)
    onehot = (
        actions[0][:, None] == lax.broadcasted_iota(jnp.int32, logits.shape, 1)
    ).astype(F32)
    chosen = jnp.sum(onehot * log_probs, axis=-1)
    prob_ratio = jnp.exp(chosen - old_logp[0])
    plain_term = prob_ratio * advantages[0]
    bounded = jnp.clip(prob_ratio, 1.0 - clip_range, 1.0 + clip_range) * advantages[0]
    slope = jnp.where(live_mask & (plain_term <= bounded), -plain_term / live_total, F32(0.0))
    dlogits = slope[:, None] * (onehot - jnp.exp(log_probs))
    along = jnp.sum(dlogits * logits, axis=-1, keepdims=True) / source.shape[1]
    dnormed = dot(dlogits.astype(BF16), w_policy.T)
    dhidden = (factor_h * (dnormed - source * (factor_h * along))).astype(BF16)
    half_a = dhidden.shape[1] // 2
    got_a = swap(
        product(attended, lax.dynamic_slice_in_dim(dhidden, (1 - batch_index) * half_a, half_a, 1))
        .astype(BF16),
        "sec",
        1,
    )
    own_a = product(attended, lax.dynamic_slice_in_dim(dhidden, batch_index * half_a, half_a, 1))

    wide = w_value.shape[0]
    target = lax.dynamic_slice_in_dim(returns[0], mdl_index * value_rows, value_rows, 0)
    emb_mine = lax.dynamic_slice_in_dim(embedded, mdl_index * value_rows, value_rows, 0)
    critic_queries, own_a, w_row, target, emb_mine = tied(
        critic_queries,
        own_a,
        w_value.reshape(1, wide),
        target.reshape(value_rows, 1),
        emb_mine,
    )
    state_c = attend_call(critic_queries, pieces_c[:-1], 0, place, [])
    *state_c, got_a, pieces_c[-1] = tied(*state_c, got_a, pieces_c[-1])
    keep_a, send_a = split_sum(rep_place, own_a, got_a, rep_count)
    *state_c, send_a = tied(*state_c, send_a)
    moved_a = swap(send_a.astype(BF16), "rep", 1)
    critic_attended = attend_call(critic_queries, pieces_c[-1:], rep_count - 1, place, state_c)

    send_m, keep_m, att_rows = part_rows(place, critic_attended, c_out)
    near_m = swap(send_m, "mdl", 1)
    send_y = (keep_m[value_rows:] + near_m[value_rows:].astype(F32)).astype(BF16)
    got_y = swap(send_y, "mdl", 2)
    att_there = swap(critic_attended, "sec", 1)
    got_y, moved_a = tied(got_y, moved_a)
    bit = 2
    while bit < rep_count:
        keep_a, send_a = halve(keep_a, moved_a)
        moved_a = swap(send_a, "rep", bit)
        bit *= 2
    value_wide, d_other, d_own = mixed_rows(
        place, emb_mine, keep_m, near_m, got_y, w_row, target
    )

    d_there = swap(d_other, "sec", 1)
    d_far = swap(d_own, "mdl", 2)
    there_far = swap(d_other, ("sec", "mdl"), mdl_count | 2)
    d_there, moved_a = tied(d_there, moved_a)
    total_a = (keep_a + moved_a.astype(F32)).astype(BF16)
    own_rows = jnp.concatenate(
        [d_own, d_far, swap(d_own, "mdl", 1), swap(d_far, "mdl", 1)], axis=0
    )
    there_rows = jnp.concatenate(
        [d_there, there_far, swap(d_there, "mdl", 1), swap(there_far, "mdl", 1)], axis=0
    )
    att_there = jnp.concatenate(
        [
            lax.dynamic_slice_in_dim(att_there, (mdl_index ^ code) * value_rows, value_rows, 0)
            for code in ROWS
        ],
        axis=0,
    )
    value_part, there_rows = tied(value_wide[:, 0], there_rows)
    codes = gather_codes(rep_count)

    strip = d_own.shape[1] // CHUNKS
    chunks = []
    for c in range(CHUNKS):
        span = slice(c * strip, (c + 1) * strip)
        keep, send = split_sum(
            rep_place,
            product(att_rows, own_rows[:, span]),
            product(att_there, there_rows[:, span]),
            rep_count,
        )
        chunks.append([keep, [swap(send.astype(BF16), "rep", 1)], [], [], []])
    levels = rep_count.bit_length() - 1
    last = 2 * levels + CHUNKS - 2
    eager = rep_count == 4
    first_swap = [swap(total_a, "rep", bit) for bit in ([2, 1] if eager else [rep_count // 2])]
    chunks.append([None, first_swap, [total_a], [swap(total_a, "sec", 1)], []])
    starts = list(range(CHUNKS)) + [-levels]
    for tick in range(last + 1):
        turn = [c for c, start in enumerate(starts) if 0 <= tick - start < 2 * levels]
        waited = [item for c in turn for item in chunks[c][1] + chunks[c][3]]
        extra = []
        if tick == 0:
            extra = [chunks[c][0] for c in range(1, CHUNKS)]
        if tick == levels:
            extra = chunks[CHUNKS][3]
        if tick == 2 * levels - 1:
            _, _, mine, crossing, theirs = chunks[CHUNKS]
            spots = [(0, side, code) for side in range(2) for code in codes]
            extra = extra + [assemble(place, mine + theirs + crossing, spots, rep_count, 1, [])]
        if tick == last:
            done = [
                (item, (c, side, code))
                for c in range(CHUNKS)
                for side in range(2)
                for item, code in zip(chunks[c][2 + 2 * side], codes)
            ]
            extra = extra + [assemble(place, *zip(*done), rep_count, CHUNKS, [])]
        outs = list(tied(*waited, *extra))
        if tick == 0:
            for c in range(1, CHUNKS):
                chunks[c][0] = outs[len(waited) + c - 1]
        if tick == levels:
            chunks[CHUNKS][3] = outs[len(waited) :]
        if tick == 2 * levels - 1:
            actor_summed = outs[len(waited)]
        if tick == last:
            result = outs[-1]
        for c in turn:
            keep, pending, mine, crossing, theirs = chunks[c]
            arrived, outs = outs[: len(pending)], outs[len(pending) :]
            crossed, outs = outs[: len(crossing)], outs[len(crossing) :]
            theirs = theirs + crossed
            level = tick - starts[c] + 1
            if level < levels:
                keep, send = halve(keep, arrived[0])
                pending = [swap(send, "rep", 1 << level)]
            else:
                fresh = arrived
                if level == levels:
                    fresh = [(keep + arrived[0].astype(F32)).astype(BF16)]
                mine = mine + fresh
                crossing = [swap(block, "sec", 1) for block in fresh]
                bit = rep_count >> (level - levels + 1)
                if eager and level == levels:
                    pending = [swap(mine[0], "rep", 2), swap(mine[0], "rep", 1)]
                elif eager and bit:
                    pending = [swap(mine[1], "rep", bit)]
                else:
                    pending = [swap(block, "rep", bit) for block in mine] if bit else []
            chunks[c] = [keep, pending, mine, crossing, theirs]
    rest = [
        (item, (c, side, code))
        for c in range(CHUNKS)
        for side, group in enumerate((chunks[c][2], chunks[c][4] + chunks[c][3]))
        for item, code in zip(group, codes)
        if (c, side, code) not in [spot for _, spot in done]
    ]
    result = assemble(place, *zip(*rest), rep_count, CHUNKS, [result])

    return (value_part[None, :], actor_summed, result)


def solution(mesh):
    return jax.shard_map(
        on_device,
        mesh=mesh,
        in_specs=(
            P("sec", "rep", None),
            P(None, "mdl"),
            P(None, None, "mdl"),
            P("mdl", None),
            P(),
            P(None, "mdl"),
            P(None, "mdl"),
            P(None, None, "mdl"),
            P("mdl", None),
            P(),
            P("sec", "rep"),
            P("sec", "rep"),
            P("sec", "rep"),
            P("sec", "rep"),
            P(),
        ),
        out_specs=(P("sec", ("rep", "mdl")), P("mdl", None), P("mdl", None)),
        check_vma=False,
    )
```

```python
import functools
import math

import jax
import jax.numpy as jnp
from jax import lax
from jax.experimental import pallas as pl
from jax.experimental.pallas import tpu as pltpu
from jax.sharding import PartitionSpec as P

HEAD = 128
epsilon = 1e-05
clip_range = 0.2
masked_score = -1e30
LOG2E = 1.4426950408889634
F32 = jnp.float32
BF16 = jnp.bfloat16
CHUNKS = 2
TABLE = 6
ROWS = (0, 2, 1, 3)
LIMIT = 40 * 2**20
HIGH = 56 * 2**20
VMEM = pl.BlockSpec(memory_space=pltpu.VMEM)
SMEM = pl.BlockSpec(memory_space=pltpu.SMEM)
ANY = pl.BlockSpec(memory_space=pl.ANY)
HBM = pl.BlockSpec(memory_space=pltpu.HBM)


def dot(a, b):
    return jnp.dot(a, b, preferred_element_type=F32)


def tied(*items):
    return lax.optimization_barrier(items)


def row_factor(source):
    return lax.rsqrt(jnp.mean(source * source, axis=-1, keepdims=True) + epsilon)


def start_copies(pairs, sems):
    copies = [
        pltpu.make_async_copy(source, target, sems.at[i])
        for i, (source, target) in enumerate(pairs)
    ]
    for copy in copies:
        copy.start()
    return copies


def first_kernel(obs_hbm, w_hbm, kv_ref, factor_ref, obs_ref, w_ref, sems):
    rows, depth = obs_ref.shape
    width = w_hbm.shape[2]
    block = rows // 2
    spans = [slice(i * block, (i + 1) * block) for i in range(2)]
    copies = start_copies(
        [(w_hbm.at[c], w_ref.at[:, c * width : (c + 1) * width]) for c in range(2)]
        + [(obs_hbm.at[span], obs_ref.at[span]) for span in spans],
        sems,
    )
    for i, span in enumerate(spans):
        copies[2 + i].wait()
        part = obs_ref[span, :]
        factor = row_factor(part.astype(F32))
        if i == 0:
            copies[0].wait()
            copies[1].wait()
        both = dot(part, w_ref[...]) * factor
        kv_ref[0, span, :] = both[:, :width].astype(BF16)
        kv_ref[1, span, :] = both[:, width:].astype(BF16)
        factor_ref[span, :] = jnp.broadcast_to(factor, (block, HEAD))


def first_projection(obs, w_keyval):
    rows, depth = obs.shape
    width = w_keyval.shape[2]
    return pl.pallas_call(
        first_kernel,
        in_specs=[HBM] * 2,
        out_specs=[VMEM] * 2,
        out_shape=[
            jax.ShapeDtypeStruct((2, rows, width), BF16),
            jax.ShapeDtypeStruct((rows, HEAD), F32),
        ],
        scratch_shapes=[
            pltpu.VMEM((rows, depth), BF16),
            pltpu.VMEM((depth, 2 * width), BF16),
            pltpu.SemaphoreType.DMA((4,)),
        ],
        compiler_params=pltpu.CompilerParams(vmem_limit_bytes=HIGH),
        cost_estimate=pl.CostEstimate(
            flops=4 * rows * depth * width, bytes_accessed=2 * rows * depth, transcendentals=0
        ),
        name="first_projection",
    )(obs, w_keyval)


def query_kernel(scale, obs_hbm, w_hbm, factor_ref, q_ref, obs_ref, w_ref, sems):
    for copy in start_copies([(w_hbm, w_ref), (obs_hbm, obs_ref)], sems):
        copy.wait()
    q_ref[...] = (dot(obs_ref[...], w_ref[...]) * (factor_ref[:, :1] * scale)).astype(BF16)


def query_projection(obs, w_query, factor, scale):
    rows, depth = obs.shape
    width = w_query.shape[1]
    return pl.pallas_call(
        functools.partial(query_kernel, scale),
        in_specs=[HBM, HBM, VMEM],
        out_specs=VMEM,
        out_shape=jax.ShapeDtypeStruct((rows, width), BF16),
        scratch_shapes=[
            pltpu.VMEM((rows, depth), BF16),
            pltpu.VMEM((depth, width), BF16),
            pltpu.SemaphoreType.DMA((2,)),
        ],
        compiler_params=pltpu.CompilerParams(vmem_limit_bytes=LIMIT),
        cost_estimate=pl.CostEstimate(
            flops=2 * rows * depth * width, bytes_accessed=2 * rows * depth, transcendentals=0
        ),
        name="query_projection",
    )(obs, w_query, factor)


def attend_blocks(groups, units, first, left_ref, q_ref, kv_refs):
    def fetch(head, span):
        kv_head = head // groups
        columns = slice(kv_head * HEAD, (kv_head + 1) * HEAD)
        query = q_ref[span, head * HEAD : (head + 1) * HEAD]
        lane = lax.broadcasted_iota(jnp.int32, query.shape, 1)
        query = jnp.concatenate([query, (lane == 0).astype(BF16)], axis=1)
        scores = []
        for p, ref in enumerate(kv_refs):
            keys = ref[0, :, columns]
            key = lax.broadcasted_iota(jnp.int32, keys.shape, 0)
            lane = lax.broadcasted_iota(jnp.int32, keys.shape, 1)
            dead = (key >= left_ref[first + p]) & (lane == 0)
            bias = jnp.where(dead, F32(masked_score), F32(0.0)).astype(BF16)
            keys = jnp.concatenate([keys, bias], axis=1)
            scores.append(
                lax.dot_general(
                    query, keys, (((1,), (1,)), ((), ())), preferred_element_type=F32
                )
            )
        return scores

    def values(head, p):
        kv_head = head // groups
        vals = kv_refs[p][1, :, kv_head * HEAD : (kv_head + 1) * HEAD]
        return jnp.concatenate([vals, jnp.ones_like(vals)], axis=1)

    ahead = fetch(*units[0])
    for i, (head, span) in enumerate(units):
        scores = ahead
        if i + 1 < len(units):
            ahead = fetch(*units[i + 1])
        yield head, span, scores, functools.partial(values, head)


def weigh(scores, top, values):
    total = None
    for p, part in enumerate(scores):
        both = dot(jnp.exp2(part - top).astype(BF16), values(p))
        total = both if total is None else total + both
    return total


def highest(scores):
    return functools.reduce(
        jnp.maximum, [jnp.max(part, axis=-1, keepdims=True) for part in scores]
    )


def open_kernel(groups, units, first, left_ref, q_ref, *refs):
    *kv_refs, wide_ref, top_ref = refs
    for head, span, scores, values in attend_blocks(
        groups, units, first, left_ref, q_ref, kv_refs
    ):
        top = highest(scores)
        wide_ref[span, head * 2 * HEAD : (head + 1) * 2 * HEAD] = weigh(scores, top, values)
        top_ref[span, head * HEAD : (head + 1) * HEAD] = jnp.broadcast_to(
            top, (top.shape[0], HEAD)
        )


def close_kernel(groups, units, first, left_ref, q_ref, wide_ref, top_ref, *refs):
    *kv_refs, o_ref = refs
    for head, span, scores, values in attend_blocks(
        groups, units, first, left_ref, q_ref, kv_refs
    ):
        before = top_ref[span, head * HEAD : head * HEAD + 1]
        top = jnp.maximum(before, highest(scores))
        wide = wide_ref[span, head * 2 * HEAD : (head + 1) * 2 * HEAD]
        wide = wide * jnp.exp2(before - top) + weigh(scores, top, values)
        o_ref[span, head * HEAD : (head + 1) * HEAD] = (
            wide[:, :HEAD] / wide[:, HEAD:]
        ).astype(BF16)


def attend_call(queries, pieces, first, place, state):
    rows, width = queries.shape
    heads = width // HEAD
    groups = heads // (pieces[0].shape[2] // HEAD)
    block = min(rows, 256)
    units = [
        (head, slice(i, i + block)) for head in range(heads) for i in range(0, rows, block)
    ]
    count = len(pieces) * pieces[0].shape[1]
    weight = 1 if state else 24
    if state:
        body, name = close_kernel, "attend_close"
        out = jax.ShapeDtypeStruct((rows, width), BF16)
    else:
        body, name = open_kernel, "attend_open"
        out = [
            jax.ShapeDtypeStruct((rows, 2 * width), F32),
            jax.ShapeDtypeStruct((rows, width), F32),
        ]
    return pl.pallas_call(
        functools.partial(body, groups, units, TABLE + first),
        in_specs=[SMEM] + [VMEM] * (1 + len(state) + len(pieces)),
        out_specs=VMEM if state else [VMEM] * 2,
        out_shape=out,
        compiler_params=pltpu.CompilerParams(vmem_limit_bytes=LIMIT),
        cost_estimate=pl.CostEstimate(
            flops=weight * rows * count * width,
            bytes_accessed=4 * rows * width,
            transcendentals=rows * count,
        ),
        name=name,
    )(place, queries, *state, *pieces)


def near_kernel(obs_hbm, t0, t1, w0, w1, sum_ref, obs_ref, w_ref, sems):
    inner, depth = w0.shape
    tile = depth // 3
    pairs = [(obs_hbm, obs_ref), (w0, w_ref.at[:inner]), (w1, w_ref.at[inner:])]
    for copy in start_copies(pairs, sems):
        copy.wait()
    for i in range(3):
        strip = slice(i * tile, (i + 1) * tile)
        parts = jnp.concatenate([t0[...], t1[...]], axis=1)
        sum_ref[:, strip] = obs_ref[:, strip].astype(F32) + dot(parts, w_ref[:, strip])


def near_rows(obs, parts, weights):
    rows, depth = obs.shape
    inner = weights[0].shape[0]
    return pl.pallas_call(
        near_kernel,
        in_specs=[HBM] + [VMEM] * 2 + [HBM, ANY],
        out_specs=VMEM,
        out_shape=jax.ShapeDtypeStruct((rows, depth), F32),
        scratch_shapes=[
            pltpu.VMEM((rows, depth), BF16),
            pltpu.VMEM((2 * inner, depth), BF16),
            pltpu.SemaphoreType.DMA((3,)),
        ],
        compiler_params=pltpu.CompilerParams(vmem_limit_bytes=LIMIT),
        cost_estimate=pl.CostEstimate(
            flops=4 * rows * depth * inner, bytes_accessed=4 * depth * inner, transcendentals=0
        ),
        name="near_rows",
    )(obs, *parts, *weights)


def hidden_kernel(sum_ref, t2, t3, w2, w3, c_hbm, o_ref, emb_ref, w_ref, c_ref, sems):
    inner, depth = w2.shape
    tile = depth // 3
    copies = start_copies(
        [(w2, w_ref.at[:inner]), (w3, w_ref.at[inner:]), (c_hbm, c_ref)], sems
    )
    copies[0].wait()
    copies[1].wait()
    for i in range(3):
        strip = slice(i * tile, (i + 1) * tile)
        parts = jnp.concatenate([t2[...], t3[...]], axis=1)
        o_ref[:, strip] = (sum_ref[:, strip] + dot(parts, w_ref[:, strip])).astype(BF16)
    copies[2].wait()
    emb_ref[...] = dot(o_ref[...], c_ref[...]).astype(BF16)


def hidden_rows(near_sum, parts, weights, c_in):
    rows, depth = near_sum.shape
    inner = weights[0].shape[0]
    width = c_in.shape[1]
    return pl.pallas_call(
        hidden_kernel,
        in_specs=[VMEM] * 3 + [ANY] * 2 + [HBM],
        out_specs=[VMEM] * 2,
        out_shape=[
            jax.ShapeDtypeStruct((rows, depth), BF16),
            jax.ShapeDtypeStruct((rows, width), BF16),
        ],
        scratch_shapes=[
            pltpu.VMEM((2 * inner, depth), BF16),
            pltpu.VMEM((depth, width), BF16),
            pltpu.SemaphoreType.DMA((3,)),
        ],
        compiler_params=pltpu.CompilerParams(vmem_limit_bytes=LIMIT),
        cost_estimate=pl.CostEstimate(
            flops=8 * rows * depth * inner, bytes_accessed=8 * depth * inner, transcendentals=0
        ),
        name="hidden_rows",
    )(near_sum, *parts, *weights, c_in)


def join_kernel(place_ref, e0, e1, e2, e3, wkv_any, kv_ref, factor_ref, emb_ref, wkv_ref, sems):
    rows, wide = emb_ref.shape
    width = wkv_any.shape[2]
    strip = e0.shape[1]
    copies = start_copies(
        [(wkv_any.at[c], wkv_ref.at[:, c * width : (c + 1) * width]) for c in range(2)], sems
    )
    starts = [pl.multiple_of((place_ref[1] ^ code) * strip, strip) for code in range(4)]
    parts = (e0, e1, e2, e3)
    for copy in copies:
        copy.wait()
    block = rows // 2
    for i in range(2):
        span = slice(i * block, (i + 1) * block)
        square, both = 0.0, 0.0
        for part, start in zip(parts, starts):
            emb = part[span, :]
            wide_emb = emb.astype(F32)
            square = square + jnp.sum(wide_emb * wide_emb, axis=-1, keepdims=True)
            both = both + dot(emb, wkv_ref[pl.ds(start, strip), :])
            emb_ref[span, pl.ds(start, strip)] = emb
        factor = lax.rsqrt(square / wide + epsilon)
        both = both * factor
        kv_ref[0, span, :] = both[:, :width].astype(BF16)
        kv_ref[1, span, :] = both[:, width:].astype(BF16)
        factor_ref[span, :] = jnp.broadcast_to(factor, (block, HEAD))


def join_rows(place, parts, w_keyval):
    rows, strip = parts[0].shape
    wide = 4 * strip
    width = w_keyval.shape[2]
    return pl.pallas_call(
        join_kernel,
        in_specs=[SMEM] + [VMEM] * 4 + [HBM],
        out_specs=[VMEM] * 3,
        out_shape=[
            jax.ShapeDtypeStruct((2, rows, width), BF16),
            jax.ShapeDtypeStruct((rows, HEAD), F32),
            jax.ShapeDtypeStruct((rows, wide), BF16),
        ],
        scratch_shapes=[pltpu.VMEM((wide, 2 * width), BF16), pltpu.SemaphoreType.DMA((2,))],
        compiler_params=pltpu.CompilerParams(vmem_limit_bytes=LIMIT),
        cost_estimate=pl.CostEstimate(
            flops=4 * rows * wide * width, bytes_accessed=4 * rows * wide, transcendentals=0
        ),
        name="join_rows",
    )(place, *parts, w_keyval)


def part_kernel(place_ref, att_ref, c_hbm, send_ref, keep_ref, order_ref, c_ref, sems):
    rows, inner = att_ref.shape
    wide = c_ref.shape[1]
    block = rows // 4
    half = inner // 2
    spans = [slice(i * half, (i + 1) * half) for i in range(2)]
    copies = start_copies([(c_hbm.at[span], c_ref.at[span]) for span in spans], sems)
    for at, code in enumerate(ROWS):
        start = pl.multiple_of((place_ref[1] ^ code) * block, block)
        order_ref[at * block : (at + 1) * block, :] = att_ref[pl.ds(start, block), :]
    for copy in copies:
        copy.wait()
    tile = 512
    for out, source in ((send_ref, order_ref[2 * block :, :]), (keep_ref, order_ref[: 2 * block, :])):
        for j in range(wide // tile):
            columns = slice(j * tile, (j + 1) * tile)
            out[:, columns] = dot(source, c_ref[:, columns]).astype(out.dtype)


def part_rows(place, attended, c_out):
    rows, inner = attended.shape
    wide = c_out.shape[1]
    return pl.pallas_call(
        part_kernel,
        in_specs=[SMEM, VMEM, HBM],
        out_specs=[VMEM] * 3,
        out_shape=[
            jax.ShapeDtypeStruct((rows // 2, wide), BF16),
            jax.ShapeDtypeStruct((rows // 2, wide), F32),
            jax.ShapeDtypeStruct((rows, inner), BF16),
        ],
        scratch_shapes=[pltpu.VMEM((inner, wide), BF16), pltpu.SemaphoreType.DMA((2,))],
        compiler_params=pltpu.CompilerParams(vmem_limit_bytes=LIMIT),
        cost_estimate=pl.CostEstimate(
            flops=2 * rows * wide * inner, bytes_accessed=8 * wide * inner, transcendentals=0
        ),
        name="part_rows",
    )(place, attended, c_out)


def mixed_kernel(
    place_ref, emb_ref, keep_ref, near_ref, got_ref, wv_ref, ret_ref,
    value_ref, other_ref, own_ref, mixed_ref,
):
    rows, wide = got_ref.shape
    half = wide // 2
    block = 32
    base = place_ref[1] * rows
    live_total = place_ref[4].astype(F32)

    @pl.loop(0, rows // block)
    def _(i):
        start = pl.multiple_of(i * block, block)
        span = pl.ds(start, block)
        mixed = emb_ref[span, :].astype(F32) + (
            keep_ref[span, :] + near_ref[span, :].astype(F32) + got_ref[span, :].astype(F32)
        )
        mixed_ref[...] = mixed
        factor = row_factor(mixed)
        value = factor * jnp.sum(mixed * wv_ref[...].astype(F32), axis=-1, keepdims=True)
        row = place_ref[2] + base + start + lax.broadcasted_iota(jnp.int32, (block, 1), 0)
        gap = jnp.where(row < place_ref[3], value - ret_ref[span, :], F32(0.0)) / live_total
        lead = factor * gap
        pull = lead * factor * value / wide
        value_ref[span, :] = jnp.broadcast_to(value, (block, HEAD))
        for out, side in ((own_ref, place_ref[0]), (other_ref, 1 - place_ref[0])):
            columns = pl.ds(pl.multiple_of(side * half, half), half)
            part = mixed_ref[:, columns]
            out[span, :] = (lead * wv_ref[:, columns].astype(F32) - part * pull).astype(BF16)


def mixed_rows(place, embedded, keep, near, got, w_value, returns):
    rows, wide = got.shape
    return pl.pallas_call(
        mixed_kernel,
        in_specs=[SMEM] + [VMEM] * 6,
        out_specs=[VMEM] * 3,
        out_shape=[
            jax.ShapeDtypeStruct((rows, HEAD), F32),
            jax.ShapeDtypeStruct((rows, wide // 2), BF16),
            jax.ShapeDtypeStruct((rows, wide // 2), BF16),
        ],
        scratch_shapes=[pltpu.VMEM((32, wide), F32)],
        compiler_params=pltpu.CompilerParams(vmem_limit_bytes=LIMIT),
        cost_estimate=pl.CostEstimate(
            flops=10 * rows * wide, bytes_accessed=12 * rows * wide, transcendentals=0
        ),
        name="mixed_rows",
    )(place, embedded, keep, near, got, w_value, returns)


def gather_codes(size):
    codes, bit = [0], size // 2
    while bit >= 1:
        codes = codes + [code ^ bit for code in codes]
        bit //= 2
    return codes


def split_kernel(codes, index_ref, own_ref, got_ref, keep_ref, send_ref):
    block = own_ref.shape[0] // len(codes)
    side = len(codes) // 2
    for k, code in enumerate(codes):
        span = pl.ds(pl.multiple_of((index_ref[0] ^ code) * block, block), block)
        out = (keep_ref, send_ref)[k // side]
        at = k % side * block
        total = own_ref[span, :] + got_ref[span, :].astype(F32)
        out[at : at + block, :] = total.astype(out.dtype)


def split_sum(index, own, got, count):
    rows, wide = own.shape
    if (rows // count) % 16:
        got = got.astype(F32)
    send_type = BF16 if (rows // count) % 16 == 0 else F32
    return pl.pallas_call(
        functools.partial(split_kernel, gather_codes(count)),
        in_specs=[SMEM, VMEM, VMEM],
        out_specs=[VMEM] * 2,
        out_shape=[
            jax.ShapeDtypeStruct((rows // 2, wide), F32),
            jax.ShapeDtypeStruct((rows // 2, wide), send_type),
        ],
        compiler_params=pltpu.CompilerParams(vmem_limit_bytes=LIMIT),
        cost_estimate=pl.CostEstimate(
            flops=rows * wide, bytes_accessed=8 * rows * wide, transcendentals=0
        ),
        name="split_sum",
    )(index, own, got)


def assemble_kernel(spots, chunks, place_ref, *refs):
    parts = refs[: len(spots)]
    out, got_ref, wide_ref, got_sems, sems = refs[-5:]
    block, strip = parts[0].shape
    got = start_copies([(part, got_ref.at[i]) for i, part in enumerate(parts)], got_sems)
    copies = []
    for i, (chunk, side, code) in enumerate(spots):
        row = pl.multiple_of((place_ref[5] ^ code) * block, block)
        column = pl.multiple_of(((place_ref[0] ^ side) * chunks + chunk) * strip, strip)
        got[i].wait()
        wide_ref[i] = got_ref[i].astype(F32)
        copy = pltpu.make_async_copy(
            wide_ref.at[i], out.at[pl.ds(row, block), pl.ds(column, strip)], sems.at[i]
        )
        copy.start()
        copies.append(copy)
    for copy in copies:
        copy.wait()


def assemble(place, parts, spots, count, chunks, before):
    block, strip = parts[0].shape
    rows, wide = block * count, strip * 2 * chunks
    return pl.pallas_call(
        functools.partial(assemble_kernel, spots, chunks),
        in_specs=[SMEM] + [ANY] * (len(parts) + len(before)),
        out_specs=ANY,
        out_shape=jax.ShapeDtypeStruct((rows, wide), F32),
        input_output_aliases={1 + len(parts): 0} if before else {},
        scratch_shapes=[
            pltpu.VMEM((len(parts), block, strip), BF16),
            pltpu.VMEM((len(parts), block, strip), F32),
            pltpu.SemaphoreType.DMA((len(parts),)),
            pltpu.SemaphoreType.DMA((len(parts),)),
        ],
        compiler_params=pltpu.CompilerParams(vmem_limit_bytes=LIMIT),
        cost_estimate=pl.CostEstimate(
            flops=rows * wide, bytes_accessed=6 * rows * wide, transcendentals=0
        ),
        name="assemble",
    )(place, *parts, *before)


def swap(block, axis, bit):
    size = lax.axis_size(axis)
    return lax.ppermute(block, axis, [(i, i ^ bit) for i in range(size)])


def gather_blocks(block, axis, late=None):
    blocks, bit = [block], lax.axis_size(axis) // 2
    while bit >= 1:
        sources = blocks if bit > 1 or late is None else [late] + blocks[1:]
        blocks = blocks + [swap(item, axis, bit) for item in sources]
        bit //= 2
    return blocks


def gather_parts(part):
    far = swap(part, "mdl", 2)
    return [part, swap(part, "mdl", 1), far, swap(far, "mdl", 1)], far


def product(left, right):
    return jnp.einsum("rh,rd->hd", left, right, preferred_element_type=F32)


def halve(keep, got):
    total = keep + got.astype(F32)
    side = total.shape[0] // 2
    return total[:side], total[side:].astype(BF16)


def on_device(
    obs,
    a_query,
    a_keyval,
    a_out,
    w_policy,
    c_in,
    c_query,
    c_keyval,
    c_out,
    w_value,
    actions,
    advantages,
    old_logp,
    returns,
    robot_count,
):
    row_count = obs.shape[1]
    batch_index = lax.axis_index("sec")
    rep_index = lax.axis_index("rep")
    rep_count = lax.axis_size("rep")
    robot_total = robot_count[batch_index]
    live_sum = jnp.sum(robot_count)
    live_total = live_sum.astype(F32)
    first_row = rep_index * row_count
    live_mask = first_row + lax.iota(jnp.int32, row_count) < robot_total
    mdl_count = lax.axis_size("mdl")
    assert mdl_count == 4 and lax.axis_size("sec") == 2
    mdl_index = lax.axis_index("mdl")
    value_rows = row_count // mdl_count
    score_scale = HEAD ** (-0.5) * LOG2E
    rep_place = rep_index.reshape(1).astype(jnp.int32)

    place = jnp.stack(
        [batch_index, mdl_index, first_row, robot_total, live_sum, rep_index]
        + [
            jnp.clip(robot_total - (rep_index ^ code) * row_count, 0, row_count)
            for code in gather_codes(rep_count)
        ]
    ).astype(jnp.int32)

    obs_in = obs[0]
    keyval, factor_a = first_projection(obs_in, a_keyval)
    a_far = swap(a_out, "mdl", 2)
    queries = query_projection(obs_in, a_query, factor_a, score_scale)
    late_keyval, queries = tied(keyval, queries)
    pieces_k = gather_blocks(keyval, "rep", late_keyval)
    state = attend_call(queries, pieces_k[:-1], 0, place, [])
    attended = attend_call(queries, pieces_k[-1:], rep_count - 1, place, state)
    attended, a_far = tied(attended, a_far)
    attended_far = swap(attended, "mdl", 2)
    attended_near = swap(attended, "mdl", 1)
    near_sum = near_rows(obs_in, [attended, attended_near], [a_out, swap(a_out, "mdl", 1)])
    attended_far, near_sum = tied(attended_far, near_sum)
    hidden, embed_part = hidden_rows(
        near_sum,
        [attended_far, swap(attended_far, "mdl", 1)],
        [a_far, swap(a_far, "mdl", 1)],
        c_in,
    )

    embed_parts, _ = gather_parts(embed_part)
    critic_keyval, factor_c, embedded = join_rows(place, embed_parts, c_keyval)
    critic_queries = (dot(embedded, c_query) * (factor_c[:, :1] * score_scale)).astype(BF16)

    late_hidden, critic_keyval = tied(hidden, critic_keyval)
    source = late_hidden.astype(F32)
    factor_h = row_factor(source)
    late_keyval, factor_h = tied(critic_keyval, factor_h)
    pieces_c = gather_blocks(critic_keyval, "rep", late_keyval)
    logits = dot(late_hidden, w_policy) * factor_h
    log_probs = jax.nn.log_softmax(logits, axis=-1)
    onehot = (
        actions[0][:, None] == lax.broadcasted_iota(jnp.int32, logits.shape, 1)
    ).astype(F32)
    chosen = jnp.sum(onehot * log_probs, axis=-1)
    prob_ratio = jnp.exp(chosen - old_logp[0])
    plain_term = prob_ratio * advantages[0]
    bounded = jnp.clip(prob_ratio, 1.0 - clip_range, 1.0 + clip_range) * advantages[0]
    slope = jnp.where(live_mask & (plain_term <= bounded), -plain_term / live_total, F32(0.0))
    dlogits = slope[:, None] * (onehot - jnp.exp(log_probs))
    along = jnp.sum(dlogits * logits, axis=-1, keepdims=True) / source.shape[1]
    dnormed = dot(dlogits.astype(BF16), w_policy.T)
    dhidden = (factor_h * (dnormed - source * (factor_h * along))).astype(BF16)
    half_a = dhidden.shape[1] // 2
    got_a = swap(
        product(attended, lax.dynamic_slice_in_dim(dhidden, (1 - batch_index) * half_a, half_a, 1))
        .astype(BF16),
        "sec",
        1,
    )
    own_a = product(attended, lax.dynamic_slice_in_dim(dhidden, batch_index * half_a, half_a, 1))

    wide = w_value.shape[0]
    target = lax.dynamic_slice_in_dim(returns[0], mdl_index * value_rows, value_rows, 0)
    emb_mine = lax.dynamic_slice_in_dim(embedded, mdl_index * value_rows, value_rows, 0)
    critic_queries, own_a, w_row, target, emb_mine = tied(
        critic_queries,
        own_a,
        w_value.reshape(1, wide),
        target.reshape(value_rows, 1),
        emb_mine,
    )
    state_c = attend_call(critic_queries, pieces_c[:-1], 0, place, [])
    *state_c, got_a, pieces_c[-1] = tied(*state_c, got_a, pieces_c[-1])
    keep_a, send_a = split_sum(rep_place, own_a, got_a, rep_count)
    *state_c, send_a = tied(*state_c, send_a)
    moved_a = swap(send_a.astype(BF16), "rep", 1)
    critic_attended = attend_call(critic_queries, pieces_c[-1:], rep_count - 1, place, state_c)

    send_m, keep_m, att_rows = part_rows(place, critic_attended, c_out)
    near_m = swap(send_m, "mdl", 1)
    send_y = (keep_m[value_rows:] + near_m[value_rows:].astype(F32)).astype(BF16)
    got_y = swap(send_y, "mdl", 2)
    att_there = swap(critic_attended, "sec", 1)
    got_y, moved_a = tied(got_y, moved_a)
    bit = 2
    while bit < rep_count:
        keep_a, send_a = halve(keep_a, moved_a)
        moved_a = swap(send_a, "rep", bit)
        bit *= 2
    value_wide, d_other, d_own = mixed_rows(
        place, emb_mine, keep_m, near_m, got_y, w_row, target
    )

    d_there = swap(d_other, "sec", 1)
    d_far = swap(d_own, "mdl", 2)
    there_far = swap(d_other, ("sec", "mdl"), mdl_count | 2)
    d_there, moved_a = tied(d_there, moved_a)
    total_a = (keep_a + moved_a.astype(F32)).astype(BF16)
    own_rows = jnp.concatenate(
        [d_own, d_far, swap(d_own, "mdl", 1), swap(d_far, "mdl", 1)], axis=0
    )
    there_rows = jnp.concatenate(
        [d_there, there_far, swap(d_there, "mdl", 1), swap(there_far, "mdl", 1)], axis=0
    )
    att_there = jnp.concatenate(
        [
            lax.dynamic_slice_in_dim(att_there, (mdl_index ^ code) * value_rows, value_rows, 0)
            for code in ROWS
        ],
        axis=0,
    )
    value_part, there_rows = tied(value_wide[:, 0], there_rows)
    codes = gather_codes(rep_count)

    strip = d_own.shape[1] // CHUNKS
    chunks = []
    for c in range(CHUNKS):
        span = slice(c * strip, (c + 1) * strip)
        keep, send = split_sum(
            rep_place,
            product(att_rows, own_rows[:, span]),
            product(att_there, there_rows[:, span]),
            rep_count,
        )
        chunks.append([keep, [swap(send.astype(BF16), "rep", 1)], [], [], []])
    levels = rep_count.bit_length() - 1
    last = 2 * levels + CHUNKS - 2
    eager = rep_count == 4
    first_swap = [swap(total_a, "rep", bit) for bit in ([2, 1] if eager else [rep_count // 2])]
    chunks.append([None, first_swap, [total_a], [swap(total_a, "sec", 1)], []])
    starts = list(range(CHUNKS)) + [-levels]
    for tick in range(last + 1):
        turn = [c for c, start in enumerate(starts) if 0 <= tick - start < 2 * levels]
        waited = [item for c in turn for item in chunks[c][1] + chunks[c][3]]
        extra = []
        if tick == 0:
            extra = [chunks[c][0] for c in range(1, CHUNKS)]
        if tick == levels:
            extra = chunks[CHUNKS][3]
        if tick == last:
            _, _, mine, crossing, theirs = chunks[CHUNKS]
            spots = [(0, side, code) for side in range(2) for code in codes]
            extra = extra + [assemble(place, mine + theirs + crossing, spots, rep_count, 1, [])]
        if tick == last:
            done = [
                (item, (c, side, code))
                for c in range(CHUNKS)
                for side in range(2)
                for item, code in zip(chunks[c][2 + 2 * side], codes)
            ]
            extra = extra + [assemble(place, *zip(*done), rep_count, CHUNKS, [])]
        outs = list(tied(*waited, *extra))
        if tick == 0:
            for c in range(1, CHUNKS):
                chunks[c][0] = outs[len(waited) + c - 1]
        if tick == levels:
            chunks[CHUNKS][3] = outs[len(waited) :]
        if tick == last:
            actor_summed = outs[len(waited)]
        if tick == last:
            result = outs[-1]
        for c in turn:
            keep, pending, mine, crossing, theirs = chunks[c]
            arrived, outs = outs[: len(pending)], outs[len(pending) :]
            crossed, outs = outs[: len(crossing)], outs[len(crossing) :]
            theirs = theirs + crossed
            level = tick - starts[c] + 1
            if level < levels:
                keep, send = halve(keep, arrived[0])
                pending = [swap(send, "rep", 1 << level)]
            else:
                fresh = arrived
                if level == levels:
                    fresh = [(keep + arrived[0].astype(F32)).astype(BF16)]
                mine = mine + fresh
                crossing = [swap(block, "sec", 1) for block in fresh]
                bit = rep_count >> (level - levels + 1)
                if eager and level == levels:
                    pending = [swap(mine[0], "rep", 2), swap(mine[0], "rep", 1)]
                elif eager and bit:
                    pending = [swap(mine[1], "rep", bit)]
                else:
                    pending = [swap(block, "rep", bit) for block in mine] if bit else []
            chunks[c] = [keep, pending, mine, crossing, theirs]
    rest = [
        (item, (c, side, code))
        for c in range(CHUNKS)
        for side, group in enumerate((chunks[c][2], chunks[c][4] + chunks[c][3]))
        for item, code in zip(group, codes)
        if (c, side, code) not in [spot for _, spot in done]
    ]
    result = assemble(place, *zip(*rest), rep_count, CHUNKS, [result])

    return (value_part[None, :], actor_summed, result)


def solution(mesh):
    return jax.shard_map(
        on_device,
        mesh=mesh,
        in_specs=(
            P("sec", "rep", None),
            P(None, "mdl"),
            P(None, None, "mdl"),
            P("mdl", None),
            P(),
            P(None, "mdl"),
            P(None, "mdl"),
            P(None, None, "mdl"),
            P("mdl", None),
            P(),
            P("sec", "rep"),
            P("sec", "rep"),
            P("sec", "rep"),
            P("sec", "rep"),
            P(),
        ),
        out_specs=(P("sec", ("rep", "mdl")), P("mdl", None), P("mdl", None)),
        check_vma=False,
    )
```

```python
import functools
import math

import jax
import jax.numpy as jnp
from jax import lax
from jax.experimental import pallas as pl
from jax.experimental.pallas import tpu as pltpu
from jax.sharding import PartitionSpec as P

HEAD = 128
epsilon = 1e-05
clip_range = 0.2
masked_score = -1e30
LOG2E = 1.4426950408889634
F32 = jnp.float32
BF16 = jnp.bfloat16
CHUNKS = 2
TABLE = 6
ROWS = (0, 2, 1, 3)
LIMIT = 28 * 2**20
HIGH = 56 * 2**20
VMEM = pl.BlockSpec(memory_space=pltpu.VMEM)
SMEM = pl.BlockSpec(memory_space=pltpu.SMEM)
ANY = pl.BlockSpec(memory_space=pl.ANY)
HBM = pl.BlockSpec(memory_space=pltpu.HBM)


def dot(a, b):
    return jnp.dot(a, b, preferred_element_type=F32)


def tied(*items):
    return lax.optimization_barrier(items)


def row_factor(source):
    return lax.rsqrt(jnp.mean(source * source, axis=-1, keepdims=True) + epsilon)


def start_copies(pairs, sems):
    copies = [
        pltpu.make_async_copy(source, target, sems.at[i])
        for i, (source, target) in enumerate(pairs)
    ]
    for copy in copies:
        copy.start()
    return copies


def first_kernel(obs_hbm, w_hbm, kv_ref, factor_ref, obs_ref, w_ref, sems):
    rows, depth = obs_ref.shape
    width = w_hbm.shape[2]
    block = rows // 2
    spans = [slice(i * block, (i + 1) * block) for i in range(2)]
    copies = start_copies(
        [(w_hbm.at[c], w_ref.at[:, c * width : (c + 1) * width]) for c in range(2)]
        + [(obs_hbm.at[span], obs_ref.at[span]) for span in spans],
        sems,
    )
    for i, span in enumerate(spans):
        copies[2 + i].wait()
        part = obs_ref[span, :]
        factor = row_factor(part.astype(F32))
        if i == 0:
            copies[0].wait()
            copies[1].wait()
        both = dot(part, w_ref[...]) * factor
        kv_ref[0, span, :] = both[:, :width].astype(BF16)
        kv_ref[1, span, :] = both[:, width:].astype(BF16)
        factor_ref[span, :] = jnp.broadcast_to(factor, (block, HEAD))


def first_projection(obs, w_keyval):
    rows, depth = obs.shape
    width = w_keyval.shape[2]
    return pl.pallas_call(
        first_kernel,
        in_specs=[HBM] * 2,
        out_specs=[VMEM] * 2,
        out_shape=[
            jax.ShapeDtypeStruct((2, rows, width), BF16),
            jax.ShapeDtypeStruct((rows, HEAD), F32),
        ],
        scratch_shapes=[
            pltpu.VMEM((rows, depth), BF16),
            pltpu.VMEM((depth, 2 * width), BF16),
            pltpu.SemaphoreType.DMA((4,)),
        ],
        compiler_params=pltpu.CompilerParams(vmem_limit_bytes=HIGH),
        cost_estimate=pl.CostEstimate(
            flops=4 * rows * depth * width, bytes_accessed=2 * rows * depth, transcendentals=0
        ),
        name="first_projection",
    )(obs, w_keyval)


def query_kernel(scale, obs_hbm, w_hbm, factor_ref, q_ref, obs_ref, w_ref, sems):
    for copy in start_copies([(w_hbm, w_ref), (obs_hbm, obs_ref)], sems):
        copy.wait()
    q_ref[...] = (dot(obs_ref[...], w_ref[...]) * (factor_ref[:, :1] * scale)).astype(BF16)


def query_projection(obs, w_query, factor, scale):
    rows, depth = obs.shape
    width = w_query.shape[1]
    return pl.pallas_call(
        functools.partial(query_kernel, scale),
        in_specs=[HBM, HBM, VMEM],
        out_specs=VMEM,
        out_shape=jax.ShapeDtypeStruct((rows, width), BF16),
        scratch_shapes=[
            pltpu.VMEM((rows, depth), BF16),
            pltpu.VMEM((depth, width), BF16),
            pltpu.SemaphoreType.DMA((2,)),
        ],
        compiler_params=pltpu.CompilerParams(vmem_limit_bytes=LIMIT),
        cost_estimate=pl.CostEstimate(
            flops=2 * rows * depth * width, bytes_accessed=2 * rows * depth, transcendentals=0
        ),
        name="query_projection",
    )(obs, w_query, factor)


def attend_blocks(groups, units, first, left_ref, q_ref, kv_refs):
    def fetch(head, span):
        kv_head = head // groups
        columns = slice(kv_head * HEAD, (kv_head + 1) * HEAD)
        query = q_ref[span, head * HEAD : (head + 1) * HEAD]
        lane = lax.broadcasted_iota(jnp.int32, query.shape, 1)
        query = jnp.concatenate([query, (lane == 0).astype(BF16)], axis=1)
        scores = []
        for p, ref in enumerate(kv_refs):
            keys = ref[0, :, columns]
            key = lax.broadcasted_iota(jnp.int32, keys.shape, 0)
            lane = lax.broadcasted_iota(jnp.int32, keys.shape, 1)
            dead = (key >= left_ref[first + p]) & (lane == 0)
            bias = jnp.where(dead, F32(masked_score), F32(0.0)).astype(BF16)
            keys = jnp.concatenate([keys, bias], axis=1)
            scores.append(
                lax.dot_general(
                    query, keys, (((1,), (1,)), ((), ())), preferred_element_type=F32
                )
            )
        return scores

    def values(head, p):
        kv_head = head // groups
        vals = kv_refs[p][1, :, kv_head * HEAD : (kv_head + 1) * HEAD]
        return jnp.concatenate([vals, jnp.ones_like(vals)], axis=1)

    ahead = fetch(*units[0])
    for i, (head, span) in enumerate(units):
        scores = ahead
        if i + 1 < len(units):
            ahead = fetch(*units[i + 1])
        yield head, span, scores, functools.partial(values, head)


def weigh(scores, top, values):
    total = None
    for p, part in enumerate(scores):
        both = dot(jnp.exp2(part - top).astype(BF16), values(p))
        total = both if total is None else total + both
    return total


def highest(scores):
    return functools.reduce(
        jnp.maximum, [jnp.max(part, axis=-1, keepdims=True) for part in scores]
    )


def open_kernel(groups, units, first, left_ref, q_ref, *refs):
    *kv_refs, wide_ref, top_ref = refs
    for head, span, scores, values in attend_blocks(
        groups, units, first, left_ref, q_ref, kv_refs
    ):
        top = highest(scores)
        wide_ref[span, head * 2 * HEAD : (head + 1) * 2 * HEAD] = weigh(scores, top, values)
        top_ref[span, head * HEAD : (head + 1) * HEAD] = jnp.broadcast_to(
            top, (top.shape[0], HEAD)
        )


def close_kernel(groups, units, first, left_ref, q_ref, wide_ref, top_ref, *refs):
    *kv_refs, o_ref = refs
    for head, span, scores, values in attend_blocks(
        groups, units, first, left_ref, q_ref, kv_refs
    ):
        before = top_ref[span, head * HEAD : head * HEAD + 1]
        top = jnp.maximum(before, highest(scores))
        wide = wide_ref[span, head * 2 * HEAD : (head + 1) * 2 * HEAD]
        wide = wide * jnp.exp2(before - top) + weigh(scores, top, values)
        o_ref[span, head * HEAD : (head + 1) * HEAD] = (
            wide[:, :HEAD] / wide[:, HEAD:]
        ).astype(BF16)


def attend_call(queries, pieces, first, place, state):
    rows, width = queries.shape
    heads = width // HEAD
    groups = heads // (pieces[0].shape[2] // HEAD)
    block = min(rows, 256)
    units = [
        (head, slice(i, i + block)) for head in range(heads) for i in range(0, rows, block)
    ]
    count = len(pieces) * pieces[0].shape[1]
    weight = 1 if state else 24
    if state:
        body, name = close_kernel, "attend_close"
        out = jax.ShapeDtypeStruct((rows, width), BF16)
    else:
        body, name = open_kernel, "attend_open"
        out = [
            jax.ShapeDtypeStruct((rows, 2 * width), F32),
            jax.ShapeDtypeStruct((rows, width), F32),
        ]
    return pl.pallas_call(
        functools.partial(body, groups, units, TABLE + first),
        in_specs=[SMEM] + [VMEM] * (1 + len(state) + len(pieces)),
        out_specs=VMEM if state else [VMEM] * 2,
        out_shape=out,
        compiler_params=pltpu.CompilerParams(vmem_limit_bytes=LIMIT),
        cost_estimate=pl.CostEstimate(
            flops=weight * rows * count * width,
            bytes_accessed=4 * rows * width,
            transcendentals=rows * count,
        ),
        name=name,
    )(place, queries, *state, *pieces)


def near_kernel(obs_hbm, t0, t1, w0, w1, sum_ref, obs_ref, w_ref, sems):
    inner, depth = w0.shape
    tile = depth // 3
    pairs = [(obs_hbm, obs_ref), (w0, w_ref.at[:inner]), (w1, w_ref.at[inner:])]
    for copy in start_copies(pairs, sems):
        copy.wait()
    for i in range(3):
        strip = slice(i * tile, (i + 1) * tile)
        parts = jnp.concatenate([t0[...], t1[...]], axis=1)
        sum_ref[:, strip] = obs_ref[:, strip].astype(F32) + dot(parts, w_ref[:, strip])


def near_rows(obs, parts, weights):
    rows, depth = obs.shape
    inner = weights[0].shape[0]
    return pl.pallas_call(
        near_kernel,
        in_specs=[HBM] + [VMEM] * 2 + [HBM, ANY],
        out_specs=VMEM,
        out_shape=jax.ShapeDtypeStruct((rows, depth), F32),
        scratch_shapes=[
            pltpu.VMEM((rows, depth), BF16),
            pltpu.VMEM((2 * inner, depth), BF16),
            pltpu.SemaphoreType.DMA((3,)),
        ],
        compiler_params=pltpu.CompilerParams(vmem_limit_bytes=LIMIT),
        cost_estimate=pl.CostEstimate(
            flops=4 * rows * depth * inner, bytes_accessed=4 * depth * inner, transcendentals=0
        ),
        name="near_rows",
    )(obs, *parts, *weights)


def hidden_kernel(sum_ref, t2, t3, w2, w3, c_hbm, o_ref, emb_ref, w_ref, c_ref, sems):
    inner, depth = w2.shape
    tile = depth // 3
    copies = start_copies(
        [(w2, w_ref.at[:inner]), (w3, w_ref.at[inner:]), (c_hbm, c_ref)], sems
    )
    copies[0].wait()
    copies[1].wait()
    for i in range(3):
        strip = slice(i * tile, (i + 1) * tile)
        parts = jnp.concatenate([t2[...], t3[...]], axis=1)
        o_ref[:, strip] = (sum_ref[:, strip] + dot(parts, w_ref[:, strip])).astype(BF16)
    copies[2].wait()
    emb_ref[...] = dot(o_ref[...], c_ref[...]).astype(BF16)


def hidden_rows(near_sum, parts, weights, c_in):
    rows, depth = near_sum.shape
    inner = weights[0].shape[0]
    width = c_in.shape[1]
    return pl.pallas_call(
        hidden_kernel,
        in_specs=[VMEM] * 3 + [ANY] * 2 + [HBM],
        out_specs=[VMEM] * 2,
        out_shape=[
            jax.ShapeDtypeStruct((rows, depth), BF16),
            jax.ShapeDtypeStruct((rows, width), BF16),
        ],
        scratch_shapes=[
            pltpu.VMEM((2 * inner, depth), BF16),
            pltpu.VMEM((depth, width), BF16),
            pltpu.SemaphoreType.DMA((3,)),
        ],
        compiler_params=pltpu.CompilerParams(vmem_limit_bytes=LIMIT),
        cost_estimate=pl.CostEstimate(
            flops=8 * rows * depth * inner, bytes_accessed=8 * depth * inner, transcendentals=0
        ),
        name="hidden_rows",
    )(near_sum, *parts, *weights, c_in)


def join_kernel(place_ref, e0, e1, e2, e3, wkv_any, kv_ref, factor_ref, emb_ref, wkv_ref, sems):
    rows, wide = emb_ref.shape
    width = wkv_any.shape[2]
    strip = e0.shape[1]
    copies = start_copies(
        [(wkv_any.at[c], wkv_ref.at[:, c * width : (c + 1) * width]) for c in range(2)], sems
    )
    starts = [pl.multiple_of((place_ref[1] ^ code) * strip, strip) for code in range(4)]
    parts = (e0, e1, e2, e3)
    for copy in copies:
        copy.wait()
    block = rows // 2
    for i in range(2):
        span = slice(i * block, (i + 1) * block)
        square, both = 0.0, 0.0
        for part, start in zip(parts, starts):
            emb = part[span, :]
            wide_emb = emb.astype(F32)
            square = square + jnp.sum(wide_emb * wide_emb, axis=-1, keepdims=True)
            both = both + dot(emb, wkv_ref[pl.ds(start, strip), :])
            emb_ref[span, pl.ds(start, strip)] = emb
        factor = lax.rsqrt(square / wide + epsilon)
        both = both * factor
        kv_ref[0, span, :] = both[:, :width].astype(BF16)
        kv_ref[1, span, :] = both[:, width:].astype(BF16)
        factor_ref[span, :] = jnp.broadcast_to(factor, (block, HEAD))


def join_rows(place, parts, w_keyval):
    rows, strip = parts[0].shape
    wide = 4 * strip
    width = w_keyval.shape[2]
    return pl.pallas_call(
        join_kernel,
        in_specs=[SMEM] + [VMEM] * 4 + [HBM],
        out_specs=[VMEM] * 3,
        out_shape=[
            jax.ShapeDtypeStruct((2, rows, width), BF16),
            jax.ShapeDtypeStruct((rows, HEAD), F32),
            jax.ShapeDtypeStruct((rows, wide), BF16),
        ],
        scratch_shapes=[pltpu.VMEM((wide, 2 * width), BF16), pltpu.SemaphoreType.DMA((2,))],
        compiler_params=pltpu.CompilerParams(vmem_limit_bytes=LIMIT),
        cost_estimate=pl.CostEstimate(
            flops=4 * rows * wide * width, bytes_accessed=4 * rows * wide, transcendentals=0
        ),
        name="join_rows",
    )(place, *parts, w_keyval)


def part_kernel(place_ref, att_ref, c_hbm, send_ref, keep_ref, order_ref, c_ref, sems):
    rows, inner = att_ref.shape
    wide = c_ref.shape[1]
    block = rows // 4
    half = inner // 2
    spans = [slice(i * half, (i + 1) * half) for i in range(2)]
    copies = start_copies([(c_hbm.at[span], c_ref.at[span]) for span in spans], sems)
    for at, code in enumerate(ROWS):
        start = pl.multiple_of((place_ref[1] ^ code) * block, block)
        order_ref[at * block : (at + 1) * block, :] = att_ref[pl.ds(start, block), :]
    for copy in copies:
        copy.wait()
    tile = 512
    for out, source in ((send_ref, order_ref[2 * block :, :]), (keep_ref, order_ref[: 2 * block, :])):
        for j in range(wide // tile):
            columns = slice(j * tile, (j + 1) * tile)
            out[:, columns] = dot(source, c_ref[:, columns]).astype(out.dtype)


def part_rows(place, attended, c_out):
    rows, inner = attended.shape
    wide = c_out.shape[1]
    return pl.pallas_call(
        part_kernel,
        in_specs=[SMEM, VMEM, HBM],
        out_specs=[VMEM] * 3,
        out_shape=[
            jax.ShapeDtypeStruct((rows // 2, wide), BF16),
            jax.ShapeDtypeStruct((rows // 2, wide), F32),
            jax.ShapeDtypeStruct((rows, inner), BF16),
        ],
        scratch_shapes=[pltpu.VMEM((inner, wide), BF16), pltpu.SemaphoreType.DMA((2,))],
        compiler_params=pltpu.CompilerParams(vmem_limit_bytes=LIMIT),
        cost_estimate=pl.CostEstimate(
            flops=2 * rows * wide * inner, bytes_accessed=8 * wide * inner, transcendentals=0
        ),
        name="part_rows",
    )(place, attended, c_out)


def mixed_kernel(
    place_ref, emb_ref, keep_ref, near_ref, got_ref, wv_ref, ret_ref,
    value_ref, other_ref, own_ref, mixed_ref,
):
    rows, wide = got_ref.shape
    half = wide // 2
    block = 32
    base = place_ref[1] * rows
    live_total = place_ref[4].astype(F32)

    @pl.loop(0, rows // block)
    def _(i):
        start = pl.multiple_of(i * block, block)
        span = pl.ds(start, block)
        mixed = emb_ref[span, :].astype(F32) + (
            keep_ref[span, :] + near_ref[span, :].astype(F32) + got_ref[span, :].astype(F32)
        )
        mixed_ref[...] = mixed
        factor = row_factor(mixed)
        value = factor * jnp.sum(mixed * wv_ref[...].astype(F32), axis=-1, keepdims=True)
        row = place_ref[2] + base + start + lax.broadcasted_iota(jnp.int32, (block, 1), 0)
        gap = jnp.where(row < place_ref[3], value - ret_ref[span, :], F32(0.0)) / live_total
        lead = factor * gap
        pull = lead * factor * value / wide
        value_ref[span, :] = jnp.broadcast_to(value, (block, HEAD))
        for out, side in ((own_ref, place_ref[0]), (other_ref, 1 - place_ref[0])):
            columns = pl.ds(pl.multiple_of(side * half, half), half)
            part = mixed_ref[:, columns]
            out[span, :] = (lead * wv_ref[:, columns].astype(F32) - part * pull).astype(BF16)


def mixed_rows(place, embedded, keep, near, got, w_value, returns):
    rows, wide = got.shape
    return pl.pallas_call(
        mixed_kernel,
        in_specs=[SMEM] + [VMEM] * 6,
        out_specs=[VMEM] * 3,
        out_shape=[
            jax.ShapeDtypeStruct((rows, HEAD), F32),
            jax.ShapeDtypeStruct((rows, wide // 2), BF16),
            jax.ShapeDtypeStruct((rows, wide // 2), BF16),
        ],
        scratch_shapes=[pltpu.VMEM((32, wide), F32)],
        compiler_params=pltpu.CompilerParams(vmem_limit_bytes=LIMIT),
        cost_estimate=pl.CostEstimate(
            flops=10 * rows * wide, bytes_accessed=12 * rows * wide, transcendentals=0
        ),
        name="mixed_rows",
    )(place, embedded, keep, near, got, w_value, returns)


def gather_codes(size):
    codes, bit = [0], size // 2
    while bit >= 1:
        codes = codes + [code ^ bit for code in codes]
        bit //= 2
    return codes


def split_kernel(codes, index_ref, own_ref, got_ref, keep_ref, send_ref):
    block = own_ref.shape[0] // len(codes)
    side = len(codes) // 2
    for k, code in enumerate(codes):
        span = pl.ds(pl.multiple_of((index_ref[0] ^ code) * block, block), block)
        out = (keep_ref, send_ref)[k // side]
        at = k % side * block
        total = own_ref[span, :] + got_ref[span, :].astype(F32)
        out[at : at + block, :] = total.astype(out.dtype)


def split_sum(index, own, got, count):
    rows, wide = own.shape
    if (rows // count) % 16:
        got = got.astype(F32)
    send_type = BF16 if (rows // count) % 16 == 0 else F32
    return pl.pallas_call(
        functools.partial(split_kernel, gather_codes(count)),
        in_specs=[SMEM, VMEM, VMEM],
        out_specs=[VMEM] * 2,
        out_shape=[
            jax.ShapeDtypeStruct((rows // 2, wide), F32),
            jax.ShapeDtypeStruct((rows // 2, wide), send_type),
        ],
        compiler_params=pltpu.CompilerParams(vmem_limit_bytes=LIMIT),
        cost_estimate=pl.CostEstimate(
            flops=rows * wide, bytes_accessed=8 * rows * wide, transcendentals=0
        ),
        name="split_sum",
    )(index, own, got)


def assemble_kernel(spots, chunks, place_ref, *refs):
    parts = refs[: len(spots)]
    out, got_ref, wide_ref, got_sems, sems = refs[-5:]
    block, strip = parts[0].shape
    got = start_copies([(part, got_ref.at[i]) for i, part in enumerate(parts)], got_sems)
    copies = []
    for i, (chunk, side, code) in enumerate(spots):
        row = pl.multiple_of((place_ref[5] ^ code) * block, block)
        column = pl.multiple_of(((place_ref[0] ^ side) * chunks + chunk) * strip, strip)
        got[i].wait()
        wide_ref[i] = got_ref[i].astype(F32)
        copy = pltpu.make_async_copy(
            wide_ref.at[i], out.at[pl.ds(row, block), pl.ds(column, strip)], sems.at[i]
        )
        copy.start()
        copies.append(copy)
    for copy in copies:
        copy.wait()


def assemble(place, parts, spots, count, chunks, before):
    block, strip = parts[0].shape
    rows, wide = block * count, strip * 2 * chunks
    return pl.pallas_call(
        functools.partial(assemble_kernel, spots, chunks),
        in_specs=[SMEM] + [ANY] * (len(parts) + len(before)),
        out_specs=ANY,
        out_shape=jax.ShapeDtypeStruct((rows, wide), F32),
        input_output_aliases={1 + len(parts): 0} if before else {},
        scratch_shapes=[
            pltpu.VMEM((len(parts), block, strip), BF16),
            pltpu.VMEM((len(parts), block, strip), F32),
            pltpu.SemaphoreType.DMA((len(parts),)),
            pltpu.SemaphoreType.DMA((len(parts),)),
        ],
        compiler_params=pltpu.CompilerParams(vmem_limit_bytes=LIMIT),
        cost_estimate=pl.CostEstimate(
            flops=rows * wide, bytes_accessed=6 * rows * wide, transcendentals=0
        ),
        name="assemble",
    )(place, *parts, *before)


def swap(block, axis, bit):
    size = lax.axis_size(axis)
    return lax.ppermute(block, axis, [(i, i ^ bit) for i in range(size)])


def gather_blocks(block, axis, late=None):
    blocks, bit = [block], lax.axis_size(axis) // 2
    while bit >= 1:
        sources = blocks if bit > 1 or late is None else [late] + blocks[1:]
        blocks = blocks + [swap(item, axis, bit) for item in sources]
        bit //= 2
    return blocks


def gather_parts(part):
    far = swap(part, "mdl", 2)
    return [part, swap(part, "mdl", 1), far, swap(far, "mdl", 1)], far


def product(left, right):
    return jnp.einsum("rh,rd->hd", left, right, preferred_element_type=F32)


def halve(keep, got):
    total = keep + got.astype(F32)
    side = total.shape[0] // 2
    return total[:side], total[side:].astype(BF16)


def on_device(
    obs,
    a_query,
    a_keyval,
    a_out,
    w_policy,
    c_in,
    c_query,
    c_keyval,
    c_out,
    w_value,
    actions,
    advantages,
    old_logp,
    returns,
    robot_count,
):
    row_count = obs.shape[1]
    batch_index = lax.axis_index("sec")
    rep_index = lax.axis_index("rep")
    rep_count = lax.axis_size("rep")
    robot_total = robot_count[batch_index]
    live_sum = jnp.sum(robot_count)
    live_total = live_sum.astype(F32)
    first_row = rep_index * row_count
    live_mask = first_row + lax.iota(jnp.int32, row_count) < robot_total
    mdl_count = lax.axis_size("mdl")
    assert mdl_count == 4 and lax.axis_size("sec") == 2
    mdl_index = lax.axis_index("mdl")
    value_rows = row_count // mdl_count
    score_scale = HEAD ** (-0.5) * LOG2E
    rep_place = rep_index.reshape(1).astype(jnp.int32)

    place = jnp.stack(
        [batch_index, mdl_index, first_row, robot_total, live_sum, rep_index]
        + [
            jnp.clip(robot_total - (rep_index ^ code) * row_count, 0, row_count)
            for code in gather_codes(rep_count)
        ]
    ).astype(jnp.int32)

    obs_in = obs[0]
    keyval, factor_a = first_projection(obs_in, a_keyval)
    a_far = swap(a_out, "mdl", 2)
    queries = query_projection(obs_in, a_query, factor_a, score_scale)
    late_keyval, queries = tied(keyval, queries)
    pieces_k = gather_blocks(keyval, "rep", late_keyval)
    state = attend_call(queries, pieces_k[:-1], 0, place, [])
    attended = attend_call(queries, pieces_k[-1:], rep_count - 1, place, state)
    attended, a_far = tied(attended, a_far)
    attended_far = swap(attended, "mdl", 2)
    attended_near = swap(attended, "mdl", 1)
    near_sum = near_rows(obs_in, [attended, attended_near], [a_out, swap(a_out, "mdl", 1)])
    attended_far, near_sum = tied(attended_far, near_sum)
    hidden, embed_part = hidden_rows(
        near_sum,
        [attended_far, swap(attended_far, "mdl", 1)],
        [a_far, swap(a_far, "mdl", 1)],
        c_in,
    )

    embed_parts, _ = gather_parts(embed_part)
    critic_keyval, factor_c, embedded = join_rows(place, embed_parts, c_keyval)
    critic_queries = (dot(embedded, c_query) * (factor_c[:, :1] * score_scale)).astype(BF16)

    late_hidden, critic_keyval = tied(hidden, critic_keyval)
    source = late_hidden.astype(F32)
    factor_h = row_factor(source)
    late_keyval, factor_h = tied(critic_keyval, factor_h)
    pieces_c = gather_blocks(critic_keyval, "rep", late_keyval)
    logits = dot(late_hidden, w_policy) * factor_h
    log_probs = jax.nn.log_softmax(logits, axis=-1)
    onehot = (
        actions[0][:, None] == lax.broadcasted_iota(jnp.int32, logits.shape, 1)
    ).astype(F32)
    chosen = jnp.sum(onehot * log_probs, axis=-1)
    prob_ratio = jnp.exp(chosen - old_logp[0])
    plain_term = prob_ratio * advantages[0]
    bounded = jnp.clip(prob_ratio, 1.0 - clip_range, 1.0 + clip_range) * advantages[0]
    slope = jnp.where(live_mask & (plain_term <= bounded), -plain_term / live_total, F32(0.0))
    dlogits = slope[:, None] * (onehot - jnp.exp(log_probs))
    along = jnp.sum(dlogits * logits, axis=-1, keepdims=True) / source.shape[1]
    dnormed = dot(dlogits.astype(BF16), w_policy.T)
    dhidden = (factor_h * (dnormed - source * (factor_h * along))).astype(BF16)
    half_a = dhidden.shape[1] // 2
    got_a = swap(
        product(attended, lax.dynamic_slice_in_dim(dhidden, (1 - batch_index) * half_a, half_a, 1))
        .astype(BF16),
        "sec",
        1,
    )
    own_a = product(attended, lax.dynamic_slice_in_dim(dhidden, batch_index * half_a, half_a, 1))

    wide = w_value.shape[0]
    target = lax.dynamic_slice_in_dim(returns[0], mdl_index * value_rows, value_rows, 0)
    emb_mine = lax.dynamic_slice_in_dim(embedded, mdl_index * value_rows, value_rows, 0)
    critic_queries, own_a, w_row, target, emb_mine = tied(
        critic_queries,
        own_a,
        w_value.reshape(1, wide),
        target.reshape(value_rows, 1),
        emb_mine,
    )
    state_c = attend_call(critic_queries, pieces_c[:-1], 0, place, [])
    *state_c, got_a, pieces_c[-1] = tied(*state_c, got_a, pieces_c[-1])
    keep_a, send_a = split_sum(rep_place, own_a, got_a, rep_count)
    *state_c, send_a = tied(*state_c, send_a)
    moved_a = swap(send_a.astype(BF16), "rep", 1)
    critic_attended = attend_call(critic_queries, pieces_c[-1:], rep_count - 1, place, state_c)

    send_m, keep_m, att_rows = part_rows(place, critic_attended, c_out)
    near_m = swap(send_m, "mdl", 1)
    send_y = (keep_m[value_rows:] + near_m[value_rows:].astype(F32)).astype(BF16)
    got_y = swap(send_y, "mdl", 2)
    att_there = swap(critic_attended, "sec", 1)
    got_y, moved_a = tied(got_y, moved_a)
    bit = 2
    while bit < rep_count:
        keep_a, send_a = halve(keep_a, moved_a)
        moved_a = swap(send_a, "rep", bit)
        bit *= 2
    value_wide, d_other, d_own = mixed_rows(
        place, emb_mine, keep_m, near_m, got_y, w_row, target
    )

    d_there = swap(d_other, "sec", 1)
    d_far = swap(d_own, "mdl", 2)
    there_far = swap(d_other, ("sec", "mdl"), mdl_count | 2)
    d_there, moved_a = tied(d_there, moved_a)
    total_a = (keep_a + moved_a.astype(F32)).astype(BF16)
    own_rows = jnp.concatenate(
        [d_own, d_far, swap(d_own, "mdl", 1), swap(d_far, "mdl", 1)], axis=0
    )
    there_rows = jnp.concatenate(
        [d_there, there_far, swap(d_there, "mdl", 1), swap(there_far, "mdl", 1)], axis=0
    )
    att_there = jnp.concatenate(
        [
            lax.dynamic_slice_in_dim(att_there, (mdl_index ^ code) * value_rows, value_rows, 0)
            for code in ROWS
        ],
        axis=0,
    )
    value_part, there_rows = tied(value_wide[:, 0], there_rows)
    codes = gather_codes(rep_count)

    strip = d_own.shape[1] // CHUNKS
    chunks = []
    for c in range(CHUNKS):
        span = slice(c * strip, (c + 1) * strip)
        keep, send = split_sum(
            rep_place,
            product(att_rows, own_rows[:, span]),
            product(att_there, there_rows[:, span]),
            rep_count,
        )
        chunks.append([keep, [swap(send.astype(BF16), "rep", 1)], [], [], []])
    levels = rep_count.bit_length() - 1
    last = 2 * levels + CHUNKS - 2
    first_swap = [swap(total_a, "rep", rep_count // 2)]
    chunks.append([None, first_swap, [total_a], [swap(total_a, "sec", 1)], []])
    starts = list(range(CHUNKS)) + [-levels]
    for tick in range(last + 1):
        turn = [c for c, start in enumerate(starts) if 0 <= tick - start < 2 * levels]
        waited = [item for c in turn for item in chunks[c][1] + chunks[c][3]]
        extra = []
        if tick == 0:
            extra = [chunks[c][0] for c in range(1, CHUNKS)]
        if tick == levels:
            extra = chunks[CHUNKS][3]
        if tick == 2 * levels - 1:
            _, _, mine, crossing, theirs = chunks[CHUNKS]
            spots = [(0, side, code) for side in range(2) for code in codes]
            extra = [assemble(place, mine + theirs + crossing, spots, rep_count, 1, [])]
        if tick == last:
            done = [
                (item, (c, side, code))
                for c in range(CHUNKS)
                for side in range(2)
                for item, code in zip(chunks[c][2 + 2 * side], codes)
            ]
            extra = [assemble(place, *zip(*done), rep_count, CHUNKS, [])]
        outs = list(tied(*waited, *extra))
        if tick == 0:
            for c in range(1, CHUNKS):
                chunks[c][0] = outs[len(waited) + c - 1]
        if tick == levels:
            chunks[CHUNKS][3] = outs[len(waited) :]
        if tick == 2 * levels - 1:
            actor_summed = outs[-1]
        if tick == last:
            result = outs[-1]
        for c in turn:
            keep, pending, mine, crossing, theirs = chunks[c]
            arrived, outs = outs[: len(pending)], outs[len(pending) :]
            crossed, outs = outs[: len(crossing)], outs[len(crossing) :]
            theirs = theirs + crossed
            level = tick - starts[c] + 1
            if level < levels:
                keep, send = halve(keep, arrived[0])
                pending = [swap(send, "rep", 1 << level)]
            else:
                fresh = arrived
                if level == levels:
                    fresh = [(keep + arrived[0].astype(F32)).astype(BF16)]
                mine = mine + fresh
                crossing = [swap(block, "sec", 1) for block in fresh]
                bit = rep_count >> (level - levels + 1)
                pending = [swap(block, "rep", bit) for block in mine] if bit else []
            chunks[c] = [keep, pending, mine, crossing, theirs]
    rest = [
        (item, (c, side, code))
        for c in range(CHUNKS)
        for side, group in enumerate((chunks[c][2], chunks[c][4] + chunks[c][3]))
        for item, code in zip(group, codes)
        if (c, side, code) not in [spot for _, spot in done]
    ]
    result = assemble(place, *zip(*rest), rep_count, CHUNKS, [result])

    return (value_part[None, :], actor_summed, result)


def solution(mesh):
    return jax.shard_map(
        on_device,
        mesh=mesh,
        in_specs=(
            P("sec", "rep", None),
            P(None, "mdl"),
            P(None, None, "mdl"),
            P("mdl", None),
            P(),
            P(None, "mdl"),
            P(None, "mdl"),
            P(None, None, "mdl"),
            P("mdl", None),
            P(),
            P("sec", "rep"),
            P("sec", "rep"),
            P("sec", "rep"),
            P("sec", "rep"),
            P(),
        ),
        out_specs=(P("sec", ("rep", "mdl")), P("mdl", None), P("mdl", None)),
        check_vma=False,
    )
```
